512 devices in a mesh: ctx: 32 (over y_hi, z), tp: 16 (over y_lo, x, core).
Axes of the slice: x: 4, y: 4 (y_hi: 2, y_lo: 2; y = y_hi * 2 + y_lo), z: 16, core: 2. Of those that a mesh axis runs over, the one named last changes fastest.
Arguments:
- query_rows: bfloat16 [4096, 1024], P('ctx', 'tp'), may hold values from -12 to 12
- key_rows: bfloat16 [4096, 1024], P('ctx', 'tp'), may hold values from -6 to 6
- value_rows: bfloat16 [4096, 1024], P('ctx', 'tp'), may hold values from -6 to 6
- valid_frames: int32 [1], replicated, may hold values from 3072 to 4096
- depth_kernel: float32 [32, 1024], P(None, 'tp'), may hold values from -1 to 1
- mix_weight: bfloat16 [1024, 1536], P('tp'), may hold values from -0.1875 to 0.1875
- out_grad: bfloat16 [4096, 1536], P(('ctx', 'tp')), may hold values from -6 to 6
Outputs:
- block_out: bfloat16 [4096, 1536], P(('ctx', 'tp'))
- query_grad: bfloat16 [4096, 1024], P('ctx', 'tp')
- key_grad: bfloat16 [4096, 1024], P('ctx', 'tp')
- value_grad: bfloat16 [4096, 1024], P('ctx', 'tp')
- mix_grad: float32 [1024, 1536], P('tp')
- kernel_grad: float32 [32, 1024], P(None, 'tp')
The draws below stay inside these ranges and needn't reach their ends.
Inputs may be any that keep to these rules, and one draw needn't show every extreme that they name: Frames from valid_frames on are padding.
All inputs are finite; a program needn't handle non-finite values.
Results may differ from the reference program's by a relative error of at most 0.039.
Values may be sent and summed in bfloat16 or wider, within the bound.
No kernel may reach another device: no remote copies, remote signals or barrier semaphores. Data moves between devices by JAX's collectives and lax.ppermute only.
A program may use at most 64 MiB of HBM per device.

```python
import jax
import jax.numpy as jnp
from jax import lax

D = 1536
HD = 64
KSIZE = 32
FR_DEV = 128
HEADS = 16
CH = 1024
FRAMES = 4096


def draw_key_rows(key, part):
    base = jnp.clip(jax.random.normal(jax.random.fold_in(key, 1), (FRAMES, CH), jnp.float32), -5.0, 5.0)
    return base.astype(jnp.bfloat16)


def draw_query_rows(key, part):
    base = jnp.clip(2.0 * jax.random.normal(jax.random.fold_in(key, 2), (FRAMES, CH), jnp.float32), -10.0, 10.0)
    return base.astype(jnp.bfloat16)


def block_scale(key, shape, split, low, high):
    level = 1.0
    for position, shards_of in split:
        heights = jax.random.uniform(jax.random.fold_in(jax.random.fold_in(key, 6), position), (shards_of,), jnp.float32, low / len(split), high / len(split))
        level = level * jnp.repeat(jnp.exp(heights), shape[position] // shards_of).reshape((-1,) + (1,) * (len(shape) - 1 - position))
    return level


def scatter_about(key, shape, scale, limit, cuts=(), dtype=jnp.bfloat16):
    entries = jax.random.normal(key, shape, jnp.float32) * scale
    if len(cuts) > 0:
        entries = block_scale(key, shape, cuts, -0.22, 0.18) * entries
    return jnp.clip(entries, min=-limit, max=limit).astype(dtype)


def setup_inputs(seed: int = 0) -> dict:
    key_of = jax.random.split(jax.random.key(seed), 8)
    return {
        "query_rows": draw_query_rows(jax.random.fold_in(key_of[7], 71), 0),
        "key_rows": draw_key_rows(jax.random.fold_in(key_of[7], 71), 0),
        "value_rows": scatter_about(key_of[2], (FRAMES, CH), 1.0, 6.0, ((0, 32), (1, 16))),
        "valid_frames": jax.random.randint(key_of[3], (1,), FRAMES * 3 // 4, FRAMES + 1).astype(jnp.int32),
        "depth_kernel": scatter_about(key_of[4], (KSIZE, CH), KSIZE ** -0.5, 1.0, ((1, 16),), jnp.float32),
        "mix_weight": scatter_about(key_of[5], (CH, D), CH ** -0.5, 0.1875, ((0, 16),)),
        "out_grad": scatter_about(key_of[6], (FRAMES, D), 1.0, 6.0, ((0, 512),)),
    }


def forward_head(head_parts, valid_count):
    query_head, key_head, value_head = head_parts
    key_live = jnp.arange(FRAMES) < valid_count
    score_scale = HD ** -0.5

    def one_block(query_block):
        scores = score_scale * jnp.dot(query_block, key_head.T, preferred_element_type=jnp.float32)
        capped = jnp.where(key_live[None, :], scores, -1e30)
        row_max = jnp.max(capped, axis=1)
        weights = jnp.where(key_live[None, :], jnp.exp(capped - row_max[:, None]), 0.0)
        log_total = row_max + jnp.log(jnp.sum(weights, axis=1))
        probs = jnp.where(key_live[None, :], jnp.exp(capped - log_total[:, None]), 0.0).astype(jnp.bfloat16)
        result = jnp.dot(probs, value_head, preferred_element_type=jnp.float32).astype(jnp.bfloat16)
        return result, log_total

    outputs, totals = lax.map(one_block, query_head.reshape(FRAMES // FR_DEV, FR_DEV, HD))
    return outputs.reshape(FRAMES, HD), totals.reshape(FRAMES)


def backward_head(head_parts, valid_count):
    query_head, key_head, value_head, attn_head, log_total, grad_head = head_parts
    key_live = jnp.arange(FRAMES) < valid_count
    score_scale = HD ** -0.5
    delta = jnp.sum(grad_head.astype(jnp.float32) * attn_head.astype(jnp.float32), axis=1)

    def one_block(carry, scan_item):
        query_block, total_block, delta_block, grad_block = scan_item
        scores = score_scale * jnp.dot(query_block, key_head.T, preferred_element_type=jnp.float32)
        capped = jnp.where(key_live[None, :], scores, -1e30)
        weights = jnp.where(key_live[None, :], jnp.exp(capped - total_block[:, None]), 0.0)
        dprobs = jnp.dot(grad_block, value_head.T, preferred_element_type=jnp.float32)
        dscores = (weights * (dprobs - delta_block[:, None])).astype(jnp.bfloat16)
        query_part = (score_scale * jnp.dot(dscores, key_head, preferred_element_type=jnp.float32)).astype(jnp.bfloat16)
        key_total = carry[0] + score_scale * jnp.dot(dscores.T, query_block, preferred_element_type=jnp.float32)
        value_total = carry[1] + jnp.dot(weights.astype(jnp.bfloat16).T, grad_block, preferred_element_type=jnp.float32)
        return (key_total, value_total), query_part

    blocks = FRAMES // FR_DEV
    start_carry = (jnp.zeros((FRAMES, HD), jnp.float32), jnp.zeros((FRAMES, HD), jnp.float32))
    carry, query_parts = lax.scan(one_block, start_carry, (query_head.reshape(blocks, FR_DEV, HD), log_total.reshape(blocks, FR_DEV), delta.reshape(blocks, FR_DEV), grad_head.reshape(blocks, FR_DEV, HD)))
    return query_parts.reshape(FRAMES, HD), carry[0].astype(jnp.bfloat16), carry[1].astype(jnp.bfloat16)


def split_heads(matrix):
    return matrix.reshape(FRAMES, HEADS, HD).transpose(1, 0, 2)


def join_heads(stacked):
    return stacked.transpose(1, 0, 2).reshape(FRAMES, CH)


def reference(query_rows, key_rows, value_rows, valid_frames, depth_kernel, mix_weight, out_grad):
    valid_count = valid_frames[0]
    query_heads = split_heads(query_rows)
    key_heads = split_heads(key_rows)
    value_heads = split_heads(value_rows)
    attn_heads, log_totals = lax.map(lambda head_parts: forward_head(head_parts, valid_count), (query_heads, key_heads, value_heads))
    attn = join_heads(attn_heads)
    frame_live = (jnp.arange(FRAMES) < valid_count)[:, None]
    masked = jnp.where(frame_live, attn, jnp.zeros_like(attn))
    rim_width = KSIZE // 2
    padded_attn = jnp.pad(masked, ((rim_width, rim_width), (0, 0)))
    depth_out = jnp.zeros((FRAMES, CH), jnp.float32)
    for offset in range(KSIZE):
        depth_out = depth_out + depth_kernel[offset][None, :] * padded_attn[offset:offset + FRAMES].astype(jnp.float32)
    swished = (depth_out * jax.nn.sigmoid(depth_out)).astype(jnp.bfloat16)
    block_out = jnp.dot(swished, mix_weight, preferred_element_type=jnp.float32).astype(jnp.bfloat16)
    mix_back = jnp.dot(out_grad, mix_weight.T, preferred_element_type=jnp.float32)
    gate_sig = jax.nn.sigmoid(depth_out)
    depth_grad = (mix_back * gate_sig * (1.0 + depth_out * (1.0 - gate_sig))).astype(jnp.bfloat16)
    grad_norm = FRAMES ** -0.5
    mix_grad = grad_norm * jnp.dot(swished.T, out_grad, preferred_element_type=jnp.float32)
    kernel_rows = []
    for offset in range(KSIZE):
        kernel_rows.append(jnp.sum(padded_attn[offset:offset + FRAMES].astype(jnp.float32) * depth_grad.astype(jnp.float32), axis=0))
    kernel_grad = grad_norm * jnp.stack(kernel_rows, axis=0)
    padded_grad = jnp.pad(depth_grad, ((rim_width, rim_width), (0, 0)))
    back_sum = jnp.zeros((FRAMES, CH), jnp.float32)
    for offset in range(KSIZE):
        first_row = 2 * rim_width - offset
        back_sum = back_sum + depth_kernel[offset][None, :] * padded_grad[first_row:first_row + FRAMES].astype(jnp.float32)
    attn_grad = jnp.where(frame_live, back_sum, jnp.zeros_like(back_sum)).astype(jnp.bfloat16)
    query_heads_grad, key_heads_grad, value_heads_grad = lax.map(lambda head_parts: backward_head(head_parts, valid_count), (query_heads, key_heads, value_heads, attn_heads, log_totals, split_heads(attn_grad)))
    return block_out, join_heads(query_heads_grad), join_heads(key_heads_grad), join_heads(value_heads_grad), mix_grad, kernel_grad
```

```python
import functools

import jax
import jax.numpy as jnp
from jax import lax
from jax.experimental import pallas as pl
from jax.experimental.pallas import tpu as pltpu
from jax.sharding import Mesh, PartitionSpec as P

F32 = jnp.float32
BF16 = jnp.bfloat16
KSIZE = 32
RIM = KSIZE // 2
LOW = -1e30
VMEM_BYTES = 48 * 1024 * 1024


def dot00(a, b):
    return lax.dot_general(a, b, (((0,), (0,)), ((), ())), preferred_element_type=F32)


def dot10(a, b):
    return lax.dot_general(a, b, (((1,), (0,)), ((), ())), preferred_element_type=F32)


def dot11(a, b):
    return lax.dot_general(a, b, (((1,), (1,)), ((), ())), preferred_element_type=F32)


def rows_of(count, lanes, entries):
    index = lax.broadcasted_iota(jnp.int32, (count, lanes), 0)
    out = jnp.zeros((count, lanes), F32)
    for where, value in entries:
        out = jnp.where(index == where, value, out)
    return out


def split3(x):
    high = x.astype(BF16).astype(F32)
    rest = x - high
    mid = rest.astype(BF16).astype(F32)
    return high, mid, rest - mid


def call(kernel, out_shapes, flops, scratch=()):
    return pl.pallas_call(
        kernel,
        out_shape=out_shapes,
        scratch_shapes=list(scratch),
        compiler_params=pltpu.CompilerParams(vmem_limit_bytes=VMEM_BYTES),
        cost_estimate=pl.CostEstimate(flops=flops, bytes_accessed=2 ** 20, transcendentals=0),
    )


def attend(all_ref, own_ref, pair_ref, bias_ref, mine_ref, other_ref, score_ref):
    blocks = all_ref.shape[0]
    head = 64
    width = 128
    scale = head ** -0.5
    query = jnp.concatenate([own_ref[0:head], pair_ref[0:head]], axis=1).astype(F32) * scale
    query = jnp.concatenate([query, rows_of(16, 2 * width, [(6, 1.0)])], axis=0).astype(BF16)
    peak = jnp.full((1, 2 * width), LOW, F32)
    for b in range(blocks):
        key = jnp.concatenate(
            [all_ref[b, head : 2 * head], rows_of(16, width, [(6, bias_ref[b : b + 1])]).astype(BF16)], axis=0
        )
        score = dot00(key, query)
        score_ref[b] = score
        peak = jnp.maximum(peak, jnp.max(score, axis=0, keepdims=True))
    total = jnp.zeros((1, 2 * width), F32)
    out = jnp.zeros((head, 2 * width), F32)
    for b in range(blocks):
        weight = jnp.exp(score_ref[b] - peak)
        total = total + jnp.sum(weight, axis=0, keepdims=True)
        out = out + dot10(all_ref[b, 2 * head : 3 * head], weight.astype(BF16))
    out = out / total
    lse = peak + jnp.log(total)
    both = jnp.concatenate([out, jnp.broadcast_to(lse, (8, 2 * width))], axis=0)
    mine_ref[...] = both[:, :width]
    other_ref[...] = both[:, width:]


def combine(mine_ref, got_ref, live_ref, attn_ref, masked_ref, lse_ref):
    mine = mine_ref[64:65]
    got = got_ref[64:65]
    top = jnp.maximum(mine, got)
    lse = top + jnp.log(jnp.exp(mine - top) + jnp.exp(got - top))
    attn = mine_ref[0:64] * jnp.exp(mine - lse) + got_ref[0:64] * jnp.exp(got - lse)
    attn_ref[...] = attn.astype(BF16)
    masked_ref[...] = jnp.where(live_ref[...] > 0.0, attn, 0.0).astype(BF16)
    lse_ref[...] = jnp.broadcast_to(lse, lse_ref.shape)


def ring_of(own, low, high):
    lane = lax.broadcasted_iota(jnp.int32, own.shape, 1)
    side = jnp.where(lane < own.shape[1] // 2, high.astype(F32), low.astype(F32))
    return jnp.concatenate([own.astype(F32), side], axis=1)


def shifted(ring, offset):
    size = ring.shape[1]
    if offset % size == 0:
        return ring[:, : size // 2]
    return pltpu.roll(ring, (-offset) % size, 1)[:, : size // 2]


def convolve(masked_ref, low_ref, high_ref, taps_ref, weight_ref, grad_ref, swish_ref, mix_ref, dgrad_ref, tap_grad_ref):
    ring = ring_of(masked_ref[...], low_ref[...], high_ref[...])
    taps = taps_ref[...]
    depth = jnp.zeros((64, 128), F32)
    for t in range(KSIZE):
        depth = depth + taps[:, t : t + 1] * shifted(ring, t - RIM)
    gate = jax.nn.sigmoid(depth)
    swish = (depth * gate).astype(BF16)
    swish_ref[...] = (depth * gate).T.astype(BF16)
    grad = grad_ref[...]
    mix = dot10(swish, grad)
    for piece in range(mix_ref.shape[0]):
        mix_ref[piece] = mix[:, piece * 128 : (piece + 1) * 128].astype(BF16)
    back = dot11(weight_ref[...], grad)
    dgrad = (back * gate * (1.0 + depth * (1.0 - gate))).astype(BF16)
    dgrad_ref[...] = dgrad
    wide = dgrad.astype(F32)
    lane = lax.broadcasted_iota(jnp.int32, (64, 128), 1)
    sums = jnp.zeros((64, 128), F32)
    for t in range(KSIZE):
        column = jnp.sum(shifted(ring, t - RIM) * wide, axis=1, keepdims=True)
        sums = jnp.where(lane == t, column, sums)
    turned = sums.T
    tap_grad_ref[...] = jnp.concatenate([turned[0:16, 0:64], turned[16:32, 0:64]], axis=1).astype(BF16)


def deconvolve(dgrad_ref, low_ref, high_ref, taps_ref, attn_ref, live_ref, lse_ref, tap_grad_ref, pack_ref):
    ring = ring_of(dgrad_ref[...], low_ref[...], high_ref[...])
    taps = taps_ref[...]
    total = jnp.zeros((64, 128), F32)
    for t in range(KSIZE):
        total = total + taps[:, t : t + 1] * shifted(ring, RIM - t)
    grad = jnp.where(live_ref[...] > 0.0, total, 0.0).astype(BF16)
    delta = jnp.sum(grad.astype(F32) * attn_ref[...].astype(F32), axis=0, keepdims=True)
    lse = lse_ref[0:1]
    a, b, c = split3(-lse)
    d, e, f = split3(-delta)
    stats = rows_of(16, 128, [(0, a), (1, b), (2, c), (3, d), (4, e), (5, f), (6, 1.0)])
    pack_ref[...] = jnp.concatenate([grad, stats.astype(BF16), tap_grad_ref[...]], axis=0)


def backward(all_ref, packs_ref, own_ref, pair_ref, pack_own_ref, pack_pair_ref, bias_ref, pair_bias_ref, mine_ref, other_ref):
    blocks = all_ref.shape[0]
    head = 64
    width = 128
    scale = head ** -0.5
    both = jnp.concatenate([own_ref[...], pair_ref[...]], axis=1)
    packs = jnp.concatenate([pack_own_ref[0:80], pack_pair_ref[0:80]], axis=1)
    query = (both[0:head].astype(F32) * scale).astype(BF16)
    query = jnp.concatenate([query, packs[head : head + 16]], axis=0)
    ones = [(0, 1.0), (1, 1.0), (2, 1.0)]
    key_rows = rows_of(16, 2 * width, ones + [(6, pair_bias_ref[0:1])]).astype(BF16)
    key = jnp.concatenate([both[head : 2 * head], key_rows], axis=0)
    value_rows = rows_of(16, 2 * width, [(3, 1.0), (4, 1.0), (5, 1.0)]).astype(BF16)
    value = jnp.concatenate([both[2 * head : 3 * head], value_rows], axis=0)
    d_query = jnp.zeros((head, 2 * width), F32)
    d_key = jnp.zeros((head, 2 * width), F32)
    d_value = jnp.zeros((head, 2 * width), F32)
    tap_sum = jnp.zeros((16, width), F32)
    for b in range(blocks):
        key_b = all_ref[b, head : 2 * head]
        key_aug = jnp.concatenate([key_b, rows_of(16, width, ones + [(6, bias_ref[b : b + 1])]).astype(BF16)], axis=0)
        value_aug = jnp.concatenate([all_ref[b, 2 * head : 3 * head], value_rows[:, :width]], axis=0)
        weight = jnp.exp(dot00(key_aug, query))
        d_score = (weight * dot00(value_aug, packs)).astype(BF16)
        d_query = d_query + dot10(key_b, d_score)

        query_b = (all_ref[b, 0:head].astype(F32) * scale).astype(BF16)
        query_aug = jnp.concatenate([query_b, packs_ref[b, head : head + 16]], axis=0)
        weight = jnp.exp(dot00(query_aug, key))
        d_score = (weight * dot00(packs_ref[b, 0:80], value)).astype(BF16)
        d_key = d_key + dot10(query_b, d_score)
        d_value = d_value + dot10(packs_ref[b, 0:head], weight.astype(BF16))
        tap_sum = tap_sum + packs_ref[b, 80:96].astype(F32)
    d_query = d_query * scale
    for ref, at in ((mine_ref, 0), (other_ref, width)):
        ref[0:head] = d_query[:, at : at + width]
        ref[head : 2 * head] = d_key[:, at : at + width]
        ref[2 * head : 3 * head] = d_value[:, at : at + width]
        ref[3 * head : 3 * head + 16] = tap_sum


def finish(norm, mine_ref, got_ref, query_ref, key_ref, value_ref, taps_ref):
    total = mine_ref[...] + got_ref[...]
    query_ref[...] = total[0:64].astype(BF16)
    key_ref[...] = total[64:128].astype(BF16)
    value_ref[...] = total[128:192].astype(BF16)
    tap = total[192:208] * norm
    taps_ref[0:16] = tap[:, 0:64]
    taps_ref[16:32] = tap[:, 64:128]


def mix_sum(parts_ref, out_ref):
    total = jnp.zeros(out_ref.shape, F32)
    for j in range(parts_ref.shape[0]):
        total = total + parts_ref[j].astype(F32)
    out_ref[...] = total.astype(BF16)


def mix_place(norm, parts_ref, out_ref):
    for piece in range(parts_ref.shape[0]):
        out_ref[:, piece * 128 : (piece + 1) * 128] = parts_ref[piece].astype(F32) * norm


def body(query_rows, key_rows, value_rows, valid_frames, depth_kernel, mix_weight, out_grad):
    width, head = query_rows.shape
    depth = lax.axis_size("z")
    ctx = ("yh", "z")
    devices = 2 * depth
    lanes = lax.axis_size("tp")
    model = mix_weight.shape[1]
    rows8 = out_grad.shape[0]
    norm = (width * devices) ** -0.5
    valid = valid_frames[0]
    half = lax.axis_index("yh")
    spot = lax.axis_index("z")
    frame = jnp.arange(width, dtype=jnp.int32)
    half_ids = (half * depth + jnp.arange(depth, dtype=jnp.int32)[:, None]) * width + frame[None, :]
    key_bias = jnp.where(half_ids < valid, 0.0, LOW).astype(F32)
    own_ids = (half * depth + spot) * width + frame
    pair_ids = ((1 - half) * depth + spot) * width + frame
    pair_bias = jnp.where(jnp.concatenate([own_ids, pair_ids]) < valid, 0.0, LOW).astype(F32)[None, :]
    live = (own_ids < valid).astype(F32)[None, :]
    swap = [(0, 1), (1, 0)]
    up = [(i, i + 1) for i in range(devices - 1)]
    down = [(i + 1, i) for i in range(devices - 1)]
    taps = depth_kernel.T

    shared = lax.all_gather(jnp.concatenate([out_grad, mix_weight], axis=0), "tp", axis=0)
    own = jnp.concatenate([query_rows.T, key_rows.T, value_rows.T], axis=0)
    pair = lax.ppermute(own, "yh", swap)
    everyone = lax.all_gather(own, "z", axis=0)

    part = jax.ShapeDtypeStruct((head + 8, width), F32)
    block = jax.ShapeDtypeStruct((head, width), BF16)
    mine, other = call(
        attend, (part, part), 2 ** 28, [pltpu.VMEM((depth, width, 2 * width), F32)]
    )(everyone, own, pair, key_bias)
    got = lax.ppermute(other, "yh", swap)
    attn, masked, lse = call(combine, (block, block, jax.ShapeDtypeStruct((8, width), F32)), 2 ** 20)(mine, got, live)
    low = lax.ppermute(masked, ctx, up)
    high = lax.ppermute(masked, ctx, down)
    grad_block = shared[:, :rows8].reshape(lanes * rows8, model)
    swish, mix_parts, dgrad, tap_grad = call(
        convolve,
        (
            jax.ShapeDtypeStruct((width, head), BF16),
            jax.ShapeDtypeStruct((model // 128, head, 128), BF16),
            block,
            jax.ShapeDtypeStruct((16, 128), BF16),
        ),
        2 ** 26,
    )(masked, low, high, taps, mix_weight, grad_block)
    grad_low = lax.ppermute(dgrad, ctx, up)
    grad_high = lax.ppermute(dgrad, ctx, down)
    pack = call(deconvolve, jax.ShapeDtypeStruct((96, width), BF16), 2 ** 22)(
        dgrad, grad_low, grad_high, taps, attn, live, lse, tap_grad
    )
    pack_pair = lax.ppermute(pack, "yh", swap)
    packs = lax.all_gather(pack, "z", axis=0)
    result = jax.ShapeDtypeStruct((3 * head + 16, width), F32)
    mine, other = call(backward, (result, result), 2 ** 29)(
        everyone, packs, own, pair, pack, pack_pair, key_bias, pair_bias
    )
    got = lax.ppermute(other, "yh", swap)
    d_query, d_key, d_value, tap_total = call(
        functools.partial(finish, norm), (block, block, block, jax.ShapeDtypeStruct((KSIZE, head), F32)), 2 ** 20
    )(mine, got)

    chunk = head * model // 128 // devices
    mine = lax.all_to_all(mix_parts.reshape(devices, chunk, 128), ctx, 0, 0, tiled=True)
    total = call(mix_sum, jax.ShapeDtypeStruct((chunk, 128), BF16), 2 ** 20)(mine)
    spread = jnp.broadcast_to(total[None], (devices, chunk, 128))
    pieces = lax.all_to_all(spread, ctx, 0, 0, tiled=True).reshape(model // 128, head, 128)
    mix_grad = call(functools.partial(mix_place, norm), jax.ShapeDtypeStruct((head, model), F32), 2 ** 20)(pieces)

    channel = lax.all_to_all(swish.reshape(lanes, rows8, head), "tp", 0, 0, tiled=True)
    channel = channel.transpose(1, 0, 2).reshape(rows8, lanes * head)
    full_weight = shared[:, rows8:].reshape(lanes * head, model)
    block_out = jnp.dot(channel, full_weight, preferred_element_type=F32).astype(BF16)
    return block_out, d_query.T, d_key.T, d_value.T, mix_grad, tap_total


def solution(mesh):
    count = mesh.shape["ctx"]
    fine = Mesh(mesh.devices.reshape(2, count // 2, mesh.shape["tp"]), ("yh", "z", "tp"))
    ctx = ("yh", "z")
    every = ("yh", "z", "tp")
    return jax.shard_map(
        body,
        mesh=fine,
        in_specs=(
            P(ctx, "tp"),
            P(ctx, "tp"),
            P(ctx, "tp"),
            P(),
            P(None, "tp"),
            P("tp", None),
            P(every, None),
        ),
        out_specs=(
            P(every, None),
            P(ctx, "tp"),
            P(ctx, "tp"),
            P(ctx, "tp"),
            P("tp", None),
            P(None, "tp"),
        ),
        check_vma=False,
    )
```

```python
import functools

import jax
import jax.numpy as jnp
from jax import lax
from jax.experimental import pallas as pl
from jax.experimental.pallas import tpu as pltpu
from jax.sharding import Mesh, PartitionSpec as P

F32 = jnp.float32
BF16 = jnp.bfloat16
KSIZE = 32
RIM = KSIZE // 2
LOW = -1e30
VMEM_BYTES = 48 * 1024 * 1024


def dot00(a, b):
    return lax.dot_general(a, b, (((0,), (0,)), ((), ())), preferred_element_type=F32)


def dot10(a, b):
    return lax.dot_general(a, b, (((1,), (0,)), ((), ())), preferred_element_type=F32)


def dot11(a, b):
    return lax.dot_general(a, b, (((1,), (1,)), ((), ())), preferred_element_type=F32)


def rows_of(count, lanes, entries):
    index = lax.broadcasted_iota(jnp.int32, (count, lanes), 0)
    out = jnp.zeros((count, lanes), F32)
    for where, value in entries:
        out = jnp.where(index == where, value, out)
    return out


def split3(x):
    high = x.astype(BF16).astype(F32)
    rest = x - high
    mid = rest.astype(BF16).astype(F32)
    return high, mid, rest - mid


def call(kernel, out_shapes, flops, scratch=(), scalars=0):
    specs = {}
    if scalars:
        count = kernel.__code__.co_argcount - len(scratch) - len(jax.tree.leaves(out_shapes))
        specs["in_specs"] = [pl.BlockSpec(memory_space=pltpu.SMEM)] + [pl.BlockSpec(memory_space=pltpu.VMEM)] * (count - 1)
    return pl.pallas_call(
        kernel,
        out_shape=out_shapes,
        **specs,
        scratch_shapes=list(scratch),
        compiler_params=pltpu.CompilerParams(vmem_limit_bytes=VMEM_BYTES),
        cost_estimate=pl.CostEstimate(flops=flops, bytes_accessed=2 ** 20, transcendentals=0),
    )


def side_of(low, high):
    lane = lax.broadcasted_iota(jnp.int32, low.shape, 1)
    return jnp.where(lane < low.shape[1] // 2, high, low)


def attend(place_ref, all_ref, own_ref, pair_ref, low_ref, high_ref, bias_ref, mine_ref, other_ref, score_ref):
    blocks = all_ref.shape[0]
    head = 64
    width = 128
    lanes = 3 * width
    scale = head ** -0.5
    spot = place_ref[0]
    first = spot == 0
    last = spot == blocks - 1
    low_here = all_ref[lax.rem(spot + blocks - 1, blocks), 0:head].astype(F32)
    high_here = all_ref[lax.rem(spot + 1, blocks), 0:head].astype(F32)
    low_there = low_ref[...].astype(F32)
    high_there = high_ref[...].astype(F32)
    side_own = side_of(jnp.where(first, low_there, low_here), jnp.where(last, high_there, high_here))
    side_pair = side_of(jnp.where(first, low_here, low_there), jnp.where(last, high_here, high_there))
    lane = lax.broadcasted_iota(jnp.int32, (head, width), 1)
    middle = (lane >= 32) & (lane < 96)
    edges = jnp.where(middle, pltpu.roll(side_pair, width // 2, 1), side_own)
    query = jnp.concatenate([own_ref[0:head].astype(F32), pair_ref[0:head].astype(F32), edges], axis=1) * scale
    query = jnp.concatenate([query, rows_of(16, lanes, [(6, 1.0)])], axis=0).astype(BF16)
    peak = jnp.full((1, lanes), LOW, F32)
    for b in range(blocks):
        key = jnp.concatenate(
            [all_ref[b, head : 2 * head], rows_of(16, width, [(6, bias_ref[b : b + 1])]).astype(BF16)], axis=0
        )
        score = dot00(key, query)
        score_ref[b] = score
        peak = jnp.maximum(peak, jnp.max(score, axis=0, keepdims=True))
    total = jnp.zeros((1, lanes), F32)
    out = jnp.zeros((head, lanes), F32)
    for b in range(blocks):
        weight = jnp.exp(score_ref[b] - peak)
        total = total + jnp.sum(weight, axis=0, keepdims=True)
        out = out + dot10(all_ref[b, 2 * head : 3 * head], weight.astype(BF16))
    out = out / total
    lse = peak + jnp.log(total)
    both = jnp.concatenate([out, jnp.broadcast_to(lse, (8, lanes))], axis=0)
    edges = both[:, 2 * width :]
    mine_ref[:, 0:width] = both[:, 0:width]
    mine_ref[:, width:] = edges
    other_ref[:, 0:width] = both[:, width : 2 * width]
    other_ref[:, width:] = pltpu.roll(edges, width // 2, 1)


def shifted(ring, offset):
    if offset == 0:
        return ring
    return pltpu.roll(ring, (-offset) % ring.shape[1], 1)


def middle_part(place_ref, mine_ref, got_ref, taps_ref, weight_ref, grad_ref, low_ref, high_ref, partial_ref, mix_ref, pack_ref):
    width = 128
    ring = 2 * width
    start = place_ref[1]
    valid = place_ref[2]
    frames = place_ref[3]
    mine = mine_ref[64:65]
    got = got_ref[64:65]
    top = jnp.maximum(mine, got)
    lse = top + jnp.log(jnp.exp(mine - top) + jnp.exp(got - top))
    attn = mine_ref[0:64] * jnp.exp(mine - lse) + got_ref[0:64] * jnp.exp(got - lse)
    attn = attn.astype(BF16).astype(F32)
    lane = lax.broadcasted_iota(jnp.int32, (1, ring), 1)
    frame = start + jnp.where(lane < ring - width // 2, lane, lane - ring)
    inside = (frame >= 0) & (frame < frames) & ((lane < width + 32) | (lane >= ring - 32))
    live = inside & (frame < valid)
    masked = jnp.where(live, attn, 0.0)
    taps = taps_ref[...]
    depth = jnp.zeros((64, ring), F32)
    for t in range(KSIZE):
        depth = depth + taps[:, t : t + 1] * shifted(masked, t - RIM)
    gate = jax.nn.sigmoid(depth)
    swish = (depth[:, :width] * gate[:, :width]).astype(BF16)
    grad = grad_ref[...]
    mix = dot10(swish, grad)
    for piece in range(mix_ref.shape[0]):
        mix_ref[piece] = mix[:, piece * 128 : (piece + 1) * 128].astype(BF16)
    weight = weight_ref[...]
    partial_ref[...] = dot00(swish, weight)
    gap = jnp.zeros((width - 2 * RIM, grad.shape[1]), BF16)
    side = jnp.concatenate([high_ref[...], gap, low_ref[...]], axis=0)
    back = jnp.concatenate([dot11(weight, grad), dot11(weight, side)], axis=1)
    dgrad = back * gate * (1.0 + depth * (1.0 - gate))
    dgrad = jnp.where(inside, dgrad, 0.0).astype(BF16).astype(F32)
    row = lax.broadcasted_iota(jnp.int32, (64, width), 1)
    sums = jnp.zeros((64, width), F32)
    total = jnp.zeros((64, width), F32)
    for t in range(KSIZE):
        column = jnp.sum(shifted(masked, t - RIM)[:, :width] * dgrad[:, :width], axis=1, keepdims=True)
        sums = jnp.where(row == t, column, sums)
        total = total + taps[:, t : t + 1] * shifted(dgrad, RIM - t)[:, :width]
    turned = sums.T
    tap_grad = jnp.concatenate([turned[0:16, 0:64], turned[16:32, 0:64]], axis=1).astype(BF16)
    grad_out = jnp.where(live[:, :width], total, 0.0).astype(BF16)
    delta = jnp.sum(grad_out.astype(F32) * attn[:, :width], axis=0, keepdims=True)
    a, b, c = split3(-lse[:, :width])
    d, e, f = split3(-delta)
    stats = rows_of(16, width, [(0, a), (1, b), (2, c), (3, d), (4, e), (5, f), (6, 1.0)])
    pack_ref[...] = jnp.concatenate([grad_out, stats.astype(BF16), tap_grad], axis=0)


def backward(all_ref, packs_ref, own_ref, pair_ref, pack_own_ref, pack_pair_ref, bias_ref, pair_bias_ref, mine_ref, other_ref):
    blocks = all_ref.shape[0]
    head = 64
    width = 128
    scale = head ** -0.5
    both = jnp.concatenate([own_ref[...], pair_ref[...]], axis=1)
    packs = jnp.concatenate([pack_own_ref[0:80], pack_pair_ref[0:80]], axis=1)
    query = (both[0:head].astype(F32) * scale).astype(BF16)
    query = jnp.concatenate([query, packs[head : head + 16]], axis=0)
    ones = [(0, 1.0), (1, 1.0), (2, 1.0)]
    key_rows = rows_of(16, 2 * width, ones + [(6, pair_bias_ref[0:1])]).astype(BF16)
    key = jnp.concatenate([both[head : 2 * head], key_rows], axis=0)
    value_rows = rows_of(16, 2 * width, [(3, 1.0), (4, 1.0), (5, 1.0)]).astype(BF16)
    value = jnp.concatenate([both[2 * head : 3 * head], value_rows], axis=0)
    d_query = jnp.zeros((head, 2 * width), F32)
    d_key = jnp.zeros((head, 2 * width), F32)
    d_value = jnp.zeros((head, 2 * width), F32)
    tap_sum = jnp.zeros((16, width), F32)
    for b in range(blocks):
        key_b = all_ref[b, head : 2 * head]
        key_aug = jnp.concatenate([key_b, rows_of(16, width, ones + [(6, bias_ref[b : b + 1])]).astype(BF16)], axis=0)
        value_aug = jnp.concatenate([all_ref[b, 2 * head : 3 * head], value_rows[:, :width]], axis=0)
        weight = jnp.exp(dot00(key_aug, query))
        d_score = (weight * dot00(value_aug, packs)).astype(BF16)
        d_query = d_query + dot10(key_b, d_score)

        query_b = (all_ref[b, 0:head].astype(F32) * scale).astype(BF16)
        query_aug = jnp.concatenate([query_b, packs_ref[b, head : head + 16]], axis=0)
        weight = jnp.exp(dot00(query_aug, key))
        d_score = (weight * dot00(packs_ref[b, 0:80], value)).astype(BF16)
        d_key = d_key + dot10(query_b, d_score)
        d_value = d_value + dot10(packs_ref[b, 0:head], weight.astype(BF16))
        tap_sum = tap_sum + packs_ref[b, 80:96].astype(F32)
    d_query = d_query * scale
    for ref, at in ((mine_ref, 0), (other_ref, width)):
        ref[0:head] = d_query[:, at : at + width]
        ref[head : 2 * head] = d_key[:, at : at + width]
        ref[2 * head : 3 * head] = d_value[:, at : at + width]
        ref[3 * head : 3 * head + 16] = tap_sum


def finish(norm, mine_ref, got_ref, query_ref, key_ref, value_ref, taps_ref):
    total = mine_ref[...] + got_ref[...]
    query_ref[...] = total[0:64].astype(BF16)
    key_ref[...] = total[64:128].astype(BF16)
    value_ref[...] = total[128:192].astype(BF16)
    tap = total[192:208] * norm
    taps_ref[0:16] = tap[:, 0:64]
    taps_ref[16:32] = tap[:, 64:128]


def mix_sum(parts_ref, out_ref):
    total = jnp.zeros(out_ref.shape, F32)
    for j in range(parts_ref.shape[0]):
        total = total + parts_ref[j].astype(F32)
    out_ref[...] = total.astype(BF16)


def mix_place(norm, parts_ref, out_ref):
    for piece in range(parts_ref.shape[0]):
        out_ref[:, piece * 128 : (piece + 1) * 128] = parts_ref[piece].astype(F32) * norm


def body(query_rows, key_rows, value_rows, valid_frames, depth_kernel, mix_weight, out_grad):
    width, head = query_rows.shape
    depth = lax.axis_size("z")
    ctx = ("yh", "z")
    devices = 2 * depth
    lanes = lax.axis_size("tp")
    model = mix_weight.shape[1]
    rows8 = out_grad.shape[0]
    norm = (width * devices) ** -0.5
    valid = valid_frames[0]
    half = lax.axis_index("yh")
    spot = lax.axis_index("z")
    frame = jnp.arange(width, dtype=jnp.int32)
    half_ids = (half * depth + jnp.arange(depth, dtype=jnp.int32)[:, None]) * width + frame[None, :]
    key_bias = jnp.where(half_ids < valid, 0.0, LOW).astype(F32)
    own_ids = (half * depth + spot) * width + frame
    pair_ids = ((1 - half) * depth + spot) * width + frame
    pair_bias = jnp.where(jnp.concatenate([own_ids, pair_ids]) < valid, 0.0, LOW).astype(F32)[None, :]
    place = jnp.stack([spot, (half * depth + spot) * width, valid, jnp.int32(width * devices)]).astype(jnp.int32)
    swap = [(0, 1), (1, 0)]
    taps = depth_kernel.T
    over_up = [(h * depth + z, (1 - h) * depth + (z + 1) % depth) for h in range(2) for z in range(depth)]
    over_down = [(h * depth + z, (1 - h) * depth + (z - 1) % depth) for h in range(2) for z in range(depth)]
    rim_pairs = []
    sides = RIM // rows8
    for i in range(devices - 1):
        for k in range(sides):
            rim_pairs.append((i * lanes + lanes - sides + k, (i + 1) * lanes + k))
            rim_pairs.append(((i + 1) * lanes + k, i * lanes + lanes - sides + k))

    rim_rows = lax.ppermute(out_grad, ("yh", "z", "tp"), rim_pairs)
    shared = lax.all_gather(jnp.concatenate([out_grad, rim_rows, mix_weight], axis=0), "tp", axis=0)
    query_turned = query_rows.T
    low = lax.ppermute(query_turned, ctx, over_up)
    high = lax.ppermute(query_turned, ctx, over_down)
    own = jnp.concatenate([query_turned, key_rows.T, value_rows.T], axis=0)
    pair = lax.ppermute(own, "yh", swap)
    everyone = lax.all_gather(own, "z", axis=0)

    part = jax.ShapeDtypeStruct((head + 8, 2 * width), F32)
    block = jax.ShapeDtypeStruct((head, width), BF16)
    mine, other = call(
        attend, (part, part), 2 ** 28, [pltpu.VMEM((depth, width, 3 * width), F32)], scalars=1
    )(place, everyone, own, pair, low, high, key_bias)
    got = lax.ppermute(other, "yh", swap)
    grad_block = shared[:, :rows8].reshape(lanes * rows8, model)
    grad_low = shared[:sides, rows8 : 2 * rows8].reshape(RIM, model)
    grad_high = shared[lanes - sides :, rows8 : 2 * rows8].reshape(RIM, model)
    partial, mix_parts, pack = call(
        middle_part,
        (
            jax.ShapeDtypeStruct((width, model), F32),
            jax.ShapeDtypeStruct((model // 128, head, 128), BF16),
            jax.ShapeDtypeStruct((96, width), BF16),
        ),
        2 ** 27,
        scalars=1,
    )(place, mine, got, taps, mix_weight, grad_block, grad_low, grad_high)
    block_out = lax.psum_scatter(partial, "tp", scatter_dimension=0, tiled=True).astype(BF16)
    chunk = head * model // 128 // devices
    mix_mine = lax.all_to_all(mix_parts.reshape(devices, chunk, 128), ctx, 0, 0, tiled=True)
    pack_pair = lax.ppermute(pack, "yh", swap)
    packs = lax.all_gather(pack, "z", axis=0)
    mix_mine, packs = lax.optimization_barrier((mix_mine, packs))
    result = jax.ShapeDtypeStruct((3 * head + 16, width), F32)
    mine, other = call(backward, (result, result), 2 ** 29)(
        everyone, packs, own, pair, pack, pack_pair, key_bias, pair_bias
    )
    got = lax.ppermute(other, "yh", swap)
    d_query, d_key, d_value, tap_total = call(
        functools.partial(finish, norm), (block, block, block, jax.ShapeDtypeStruct((KSIZE, head), F32)), 2 ** 20
    )(mine, got)

    mix_total = call(mix_sum, jax.ShapeDtypeStruct((chunk, 128), BF16), 2 ** 20)(mix_mine)
    spread = jnp.broadcast_to(mix_total[None], (devices, chunk, 128))
    pieces = lax.all_to_all(spread, ctx, 0, 0, tiled=True).reshape(model // 128, head, 128)
    mix_grad = call(functools.partial(mix_place, norm), jax.ShapeDtypeStruct((head, model), F32), 2 ** 20)(pieces)
    return block_out, d_query.T, d_key.T, d_value.T, mix_grad, tap_total


def solution(mesh):
    count = mesh.shape["ctx"]
    fine = Mesh(mesh.devices.reshape(2, count // 2, mesh.shape["tp"]), ("yh", "z", "tp"))
    ctx = ("yh", "z")
    every = ("yh", "z", "tp")
    return jax.shard_map(
        body,
        mesh=fine,
        in_specs=(
            P(ctx, "tp"),
            P(ctx, "tp"),
            P(ctx, "tp"),
            P(),
            P(None, "tp"),
            P("tp", None),
            P(every, None),
        ),
        out_specs=(
            P(every, None),
            P(ctx, "tp"),
            P(ctx, "tp"),
            P(ctx, "tp"),
            P("tp", None),
            P(None, "tp"),
        ),
        check_vma=False,
    )
```

```python
import functools

import jax
import jax.numpy as jnp
from jax import lax
from jax.experimental import pallas as pl
from jax.experimental.pallas import tpu as pltpu
from jax.sharding import Mesh, PartitionSpec as P

F32 = jnp.float32
BF16 = jnp.bfloat16
KSIZE = 32
RIM = KSIZE // 2
LOW = -1e30
VMEM_BYTES = 48 * 1024 * 1024


def dot00(a, b):
    return lax.dot_general(a, b, (((0,), (0,)), ((), ())), preferred_element_type=F32)


def dot10(a, b):
    return lax.dot_general(a, b, (((1,), (0,)), ((), ())), preferred_element_type=F32)


def dot11(a, b):
    return lax.dot_general(a, b, (((1,), (1,)), ((), ())), preferred_element_type=F32)


def rows_of(count, lanes, entries):
    index = lax.broadcasted_iota(jnp.int32, (count, lanes), 0)
    out = jnp.zeros((count, lanes), F32)
    for where, value in entries:
        out = jnp.where(index == where, value, out)
    return out


def split3(x):
    high = x.astype(BF16).astype(F32)
    rest = x - high
    mid = rest.astype(BF16).astype(F32)
    return high, mid, rest - mid


def call(kernel, out_shapes, flops, scratch=(), scalars=0):
    specs = {}
    if scalars:
        count = kernel.__code__.co_argcount - len(scratch) - len(jax.tree.leaves(out_shapes))
        specs["in_specs"] = [pl.BlockSpec(memory_space=pltpu.SMEM)] + [pl.BlockSpec(memory_space=pltpu.VMEM)] * (count - 1)
    return pl.pallas_call(
        kernel,
        out_shape=out_shapes,
        **specs,
        scratch_shapes=list(scratch),
        compiler_params=pltpu.CompilerParams(vmem_limit_bytes=VMEM_BYTES),
        cost_estimate=pl.CostEstimate(flops=flops, bytes_accessed=2 ** 20, transcendentals=0),
    )


def side_of(low, high):
    lane = lax.broadcasted_iota(jnp.int32, low.shape, 1)
    return jnp.where(lane < low.shape[1] // 2, high, low)


def bias_of(place_ref, block, base):
    lane = lax.broadcasted_iota(jnp.int32, (1, 128), 1)
    return jnp.where((base + block) * 128 + lane < place_ref[2], 0.0, LOW)


def edges_of(packed):
    packed = packed.astype(F32)
    return jnp.concatenate([packed, pltpu.roll(packed, 64, 1)], axis=0)


def first_pack(place_ref, both_ref, pack_ref, pair_ref):
    own = both_ref[place_ref[4]]
    pair = both_ref[1 - place_ref[4]]
    query = pair[0:64].astype(F32)
    lane = lax.broadcasted_iota(jnp.int32, query.shape, 1)
    edge = jnp.where(lane < 32, query, pltpu.roll(query, 64, 1))
    edge = jnp.where(lane[0:32] < 64, edge[0:32], pltpu.roll(edge[32:64], 64, 1))
    pair_ref[...] = pair
    pack_ref[0:192] = own
    pack_ref[192:224] = edge.astype(BF16)


def lay_grads(shared_ref, grad_ref, low_ref, high_ref, turned_ref):
    lanes = shared_ref.shape[0]
    for i in range(lanes // 2):
        even = shared_ref[2 * i].astype(F32)
        odd = shared_ref[2 * i + 1].astype(F32)
        grad_ref[16 * i : 16 * i + 16] = jnp.concatenate([even[0:8], odd[0:8]], axis=0).astype(BF16)
        if i == 0:
            low_ref[...] = jnp.concatenate([even[8:16], odd[8:16]], axis=0).astype(BF16)
        if i == lanes // 2 - 1:
            high_ref[...] = jnp.concatenate([even[8:16], odd[8:16]], axis=0).astype(BF16)
    for piece in range(grad_ref.shape[1] // 128):
        columns = slice(128 * piece, 128 * piece + 128)
        turned_ref[columns] = grad_ref[:, columns].astype(F32).T.astype(BF16)


def attend(place_ref, all_ref, own_ref, pair_ref, mine_ref, other_ref, score_ref):
    blocks = all_ref.shape[0]
    head = 64
    width = 128
    lanes = 3 * width
    scale = head ** -0.5
    spot = place_ref[0]
    first = spot == 0
    spot_rows = place_ref[4] * blocks
    last = spot == blocks - 1
    before = lax.rem(spot + blocks - 1, blocks)
    after = lax.rem(spot + 1, blocks)
    low_here = all_ref[before, 0:head].astype(F32)
    high_here = all_ref[after, 0:head].astype(F32)
    low_there = pltpu.roll(edges_of(all_ref[before, 3 * head : 3 * head + 32]), width // 2, 1)
    high_there = edges_of(all_ref[after, 3 * head : 3 * head + 32])
    side_own = side_of(jnp.where(first, low_there, low_here), jnp.where(last, high_there, high_here))
    side_pair = side_of(jnp.where(first, low_here, low_there), jnp.where(last, high_here, high_there))
    lane = lax.broadcasted_iota(jnp.int32, (head, width), 1)
    middle = (lane >= 32) & (lane < 96)
    edges = jnp.where(middle, pltpu.roll(side_pair, width // 2, 1), side_own)
    query = jnp.concatenate([own_ref[0:head].astype(F32), pair_ref[0:head].astype(F32), edges], axis=1) * scale
    query = jnp.concatenate([query, rows_of(16, lanes, [(6, 1.0)])], axis=0).astype(BF16)
    peak = jnp.full((1, lanes), LOW, F32)
    for b in range(blocks):
        key = jnp.concatenate(
            [all_ref[b, head : 2 * head], rows_of(16, width, [(6, bias_of(place_ref, b, spot_rows))]).astype(BF16)], axis=0
        )
        score = dot00(key, query)
        score_ref[b] = score
        peak = jnp.maximum(peak, jnp.max(score, axis=0, keepdims=True))
    total = jnp.zeros((1, lanes), F32)
    out = jnp.zeros((head, lanes), F32)
    for b in range(blocks):
        weight = jnp.exp(score_ref[b] - peak)
        total = total + jnp.sum(weight, axis=0, keepdims=True)
        out = out + dot10(all_ref[b, 2 * head : 3 * head], weight.astype(BF16))
    out = out / total
    lse = peak + jnp.log(total)
    both = jnp.concatenate([out, jnp.broadcast_to(lse, (8, lanes))], axis=0)
    edges = both[:, 2 * width :]
    mine_ref[:, 0:width] = both[:, 0:width]
    mine_ref[:, width:] = edges
    other_ref[:, 0:width] = both[:, width : 2 * width]
    other_ref[:, width:] = pltpu.roll(edges, width // 2, 1)


def shifted(ring, offset):
    if offset == 0:
        return ring
    return pltpu.roll(ring, (-offset) % ring.shape[1], 1)


def middle_part(place_ref, mine_ref, got_ref, taps_ref, weight_ref, grad_ref, low_ref, high_ref, partial_ref, pack_ref):
    width = 128
    ring = 2 * width
    start = place_ref[1]
    valid = place_ref[2]
    frames = place_ref[3]
    mine = mine_ref[64:65]
    got = got_ref[64:65]
    top = jnp.maximum(mine, got)
    lse = top + jnp.log(jnp.exp(mine - top) + jnp.exp(got - top))
    attn = mine_ref[0:64] * jnp.exp(mine - lse) + got_ref[0:64] * jnp.exp(got - lse)
    attn = attn.astype(BF16).astype(F32)
    lane = lax.broadcasted_iota(jnp.int32, (1, ring), 1)
    frame = start + jnp.where(lane < ring - width // 2, lane, lane - ring)
    inside = (frame >= 0) & (frame < frames) & ((lane < width + 32) | (lane >= ring - 32))
    live = inside & (frame < valid)
    masked = jnp.where(live, attn, 0.0)
    taps = taps_ref[...]
    depth = jnp.zeros((64, ring), F32)
    for t in range(KSIZE):
        depth = depth + taps[:, t : t + 1] * shifted(masked, t - RIM)
    gate = jax.nn.sigmoid(depth)
    swish = (depth[:, :width] * gate[:, :width]).astype(BF16)
    grad = grad_ref[...]
    weight = weight_ref[...]
    partial_ref[...] = dot00(swish, weight).astype(BF16)
    gap = jnp.zeros((width - 2 * RIM, grad.shape[1]), BF16)
    side = jnp.concatenate([high_ref[...], gap, low_ref[...]], axis=0)
    back = jnp.concatenate([dot11(weight, grad), dot11(weight, side)], axis=1)
    dgrad = back * gate * (1.0 + depth * (1.0 - gate))
    dgrad = jnp.where(inside, dgrad, 0.0).astype(BF16).astype(F32)
    row = lax.broadcasted_iota(jnp.int32, (64, width), 1)
    sums = jnp.zeros((64, width), F32)
    total = jnp.zeros((64, width), F32)
    for t in range(KSIZE):
        column = jnp.sum(shifted(masked, t - RIM)[:, :width] * dgrad[:, :width], axis=1, keepdims=True)
        sums = jnp.where(row == t, column, sums)
        total = total + taps[:, t : t + 1] * shifted(dgrad, RIM - t)[:, :width]
    turned = sums.T
    tap_grad = jnp.concatenate([turned[0:16, 0:64], turned[16:32, 0:64]], axis=1).astype(BF16)
    grad_out = jnp.where(live[:, :width], total, 0.0).astype(BF16)
    delta = jnp.sum(grad_out.astype(F32) * attn[:, :width], axis=0, keepdims=True)
    a, b, c = split3(-lse[:, :width])
    d, e, f = split3(-delta)
    stats = rows_of(16, width, [(0, a), (1, b), (2, c), (3, d), (4, e), (5, f), (6, 1.0)])
    pack_ref[...] = jnp.concatenate([grad_out, stats.astype(BF16), tap_grad, swish], axis=0)


def backward(place_ref, all_ref, packs_ref, own_ref, pair_ref, pack_own_ref, pack_pair_ref, mine_ref, other_ref):
    blocks = all_ref.shape[0]
    base = place_ref[4] * blocks
    pair_base = blocks - base
    pair_bias = jnp.concatenate([bias_of(place_ref, place_ref[0], base), bias_of(place_ref, place_ref[0], pair_base)], axis=1)
    head = 64
    width = 128
    scale = head ** -0.5
    both = jnp.concatenate([own_ref[...], pair_ref[...]], axis=1)
    packs = jnp.concatenate([pack_own_ref[0:80], pack_pair_ref[0:80]], axis=1)
    query = (both[0:head].astype(F32) * scale).astype(BF16)
    query = jnp.concatenate([query, packs[head : head + 16]], axis=0)
    ones = [(0, 1.0), (1, 1.0), (2, 1.0)]
    key_rows = rows_of(16, 2 * width, ones + [(6, pair_bias)]).astype(BF16)
    key = jnp.concatenate([both[head : 2 * head], key_rows], axis=0)
    value_rows = rows_of(16, 2 * width, [(3, 1.0), (4, 1.0), (5, 1.0)]).astype(BF16)
    value = jnp.concatenate([both[2 * head : 3 * head], value_rows], axis=0)
    d_query = jnp.zeros((head, 2 * width), F32)
    d_key = jnp.zeros((head, 2 * width), F32)
    d_value = jnp.zeros((head, 2 * width), F32)
    tap_sum = jnp.zeros((16, width), F32)
    for b in range(blocks):
        key_b = all_ref[b, head : 2 * head]
        key_aug = jnp.concatenate([key_b, rows_of(16, width, ones + [(6, bias_of(place_ref, b, base))]).astype(BF16)], axis=0)
        value_aug = jnp.concatenate([all_ref[b, 2 * head : 3 * head], value_rows[:, :width]], axis=0)
        weight = jnp.exp(dot00(key_aug, query))
        d_score = (weight * dot00(value_aug, packs)).astype(BF16)
        d_query = d_query + dot10(key_b, d_score)

        query_b = (all_ref[b, 0:head].astype(F32) * scale).astype(BF16)
        query_aug = jnp.concatenate([query_b, packs_ref[b, head : head + 16]], axis=0)
        weight = jnp.exp(dot00(query_aug, key))
        d_score = (weight * dot00(packs_ref[b, 0:80], value)).astype(BF16)
        d_key = d_key + dot10(query_b, d_score)
        d_value = d_value + dot10(packs_ref[b, 0:head], weight.astype(BF16))
        tap_sum = tap_sum + packs_ref[b, 80:96].astype(F32)
    d_query = d_query * scale
    for ref, at in ((mine_ref, 0), (other_ref, width)):
        ref[0:head] = d_query[:, at : at + width]
        ref[head : 2 * head] = d_key[:, at : at + width]
        ref[2 * head : 3 * head] = d_value[:, at : at + width]
        ref[3 * head : 3 * head + 16] = tap_sum


def finish(norm, mine_ref, got_ref, query_ref, key_ref, value_ref, taps_ref):
    total = mine_ref[...] + got_ref[...]
    query_ref[...] = total[0:64].astype(BF16)
    key_ref[...] = total[64:128].astype(BF16)
    value_ref[...] = total[128:192].astype(BF16)
    tap = total[192:208] * norm
    taps_ref[0:16] = tap[:, 0:64]
    taps_ref[16:32] = tap[:, 64:128]


def mix_slab(packs_ref, slab_ref, out_ref):
    total = jnp.zeros(out_ref.shape, F32)
    for b in range(packs_ref.shape[0]):
        total = total + dot11(packs_ref[b, 96:160], slab_ref[b])
    out_ref[...] = total


def mix_spread(mine_ref, got_ref, out_ref):
    total = (mine_ref[...] + got_ref[...]).astype(BF16)
    for j in range(out_ref.shape[0]):
        out_ref[j] = total


def mix_place(norm, parts_ref, out_ref):
    step = parts_ref.shape[2]
    for piece in range(parts_ref.shape[0]):
        out_ref[:, piece * step : (piece + 1) * step] = parts_ref[piece].astype(F32) * norm


def sum_blocks(parts_ref, out_ref):
    total = jnp.zeros(out_ref.shape, F32)
    for j in range(parts_ref.shape[0]):
        total = total + parts_ref[j].astype(F32)
    out_ref[...] = total.astype(BF16)


def body(query_rows, key_rows, value_rows, valid_frames, depth_kernel, mix_weight, out_grad):
    width, head = query_rows.shape
    depth = lax.axis_size("z")
    ctx = ("yh", "z")
    devices = 2 * depth
    lanes = lax.axis_size("tp")
    model = mix_weight.shape[1]
    rows8 = out_grad.shape[0]
    norm = (width * devices) ** -0.5
    valid = valid_frames[0]
    half = lax.axis_index("yh")
    spot = lax.axis_index("z")
    place = jnp.stack([spot, (half * depth + spot) * width, valid, jnp.int32(width * devices), half]).astype(jnp.int32)
    swap = [(0, 1), (1, 0)]
    taps = depth_kernel.T
    rim_pairs = []
    sides = RIM // rows8
    for i in range(devices - 1):
        for k in range(sides):
            rim_pairs.append((i * lanes + lanes - sides + k, (i + 1) * lanes + k))
            rim_pairs.append(((i + 1) * lanes + k, i * lanes + lanes - sides + k))

    rim_rows = lax.ppermute(out_grad, ("yh", "z", "tp"), rim_pairs)
    own = jnp.concatenate([query_rows.T, key_rows.T, value_rows.T], axis=0)
    both = lax.all_gather(own, "yh", axis=0)
    rim_rows, both = lax.optimization_barrier((rim_rows, both))
    front, pair = call(
        first_pack,
        (jax.ShapeDtypeStruct((3 * head + 32, width), BF16), jax.ShapeDtypeStruct((3 * head, width), BF16)),
        2 ** 20,
        scalars=1,
    )(place, both)
    with_rim = jnp.concatenate([out_grad, rim_rows], axis=0)
    shared = lax.all_to_all(jnp.broadcast_to(with_rim[None], (lanes,) + with_rim.shape), "tp", 0, 0, tiled=True)
    everyone = lax.all_gather(front, "z", axis=0)
    shared, everyone = lax.optimization_barrier((shared, everyone))

    part = jax.ShapeDtypeStruct((head + 8, 2 * width), F32)
    block = jax.ShapeDtypeStruct((head, width), BF16)
    mine, other = call(
        attend, (part, part), 2 ** 28, [pltpu.VMEM((depth, width, 3 * width), F32)], scalars=1
    )(place, everyone, own, pair)
    shared, other = lax.optimization_barrier((shared, other))
    got = lax.ppermute(other, "yh", swap)
    rim_shape = jax.ShapeDtypeStruct((RIM, model), BF16)
    grad_block, grad_low, grad_high, turned = call(
        lay_grads,
        (jax.ShapeDtypeStruct((width, model), BF16), rim_shape, rim_shape, jax.ShapeDtypeStruct((model, width), BF16)),
        2 ** 33,
    )(shared)
    slab = lax.all_to_all(turned.reshape(depth, model // depth, width), "z", 0, 0, tiled=True)
    partial, pack = call(
        middle_part,
        (jax.ShapeDtypeStruct((width, model), BF16), jax.ShapeDtypeStruct((96 + head, width), BF16)),
        2 ** 27,
        scalars=1,
    )(place, mine, got, taps, mix_weight, grad_block, grad_low, grad_high)
    pack_pair = lax.ppermute(pack, "yh", swap)
    packs = lax.all_gather(pack, "z", axis=0)
    packs, slab, partial = lax.optimization_barrier((packs, slab, partial))

    slab_shape = jax.ShapeDtypeStruct((head, model // depth), F32)
    mix_mine = call(mix_slab, slab_shape, 2 ** 27)(packs, slab)
    mix_got = lax.ppermute(mix_mine, "yh", swap)
    block_parts = lax.all_to_all(partial.reshape(lanes, rows8, model), "tp", 0, 0, tiled=True)
    packs, mix_mine = lax.optimization_barrier((packs, mix_mine))
    result = jax.ShapeDtypeStruct((3 * head + 16, width), F32)
    mine, other = call(backward, (result, result), 2 ** 29, scalars=1)(
        place, everyone, packs, own, pair, pack, pack_pair
    )
    got = lax.ppermute(other, "yh", swap)
    d_query, d_key, d_value, tap_total = call(
        functools.partial(finish, norm), (block, block, block, jax.ShapeDtypeStruct((KSIZE, head), F32)), 2 ** 20
    )(mine, got)

    mix_got, block_parts = lax.optimization_barrier((mix_got, block_parts))
    spread = call(mix_spread, jax.ShapeDtypeStruct((depth, head, model // depth), BF16), 2 ** 20)(mix_mine, mix_got)
    pieces = lax.all_to_all(spread, "z", 0, 0, tiled=True)
    block_out = call(sum_blocks, jax.ShapeDtypeStruct((rows8, model), BF16), 2 ** 20)(block_parts)
    mix_grad = call(functools.partial(mix_place, norm), jax.ShapeDtypeStruct((head, model), F32), 2 ** 20)(pieces)
    return block_out, d_query.T, d_key.T, d_value.T, mix_grad, tap_total


def solution(mesh):
    count = mesh.shape["ctx"]
    fine = Mesh(mesh.devices.reshape(2, count // 2, mesh.shape["tp"]), ("yh", "z", "tp"))
    ctx = ("yh", "z")
    every = ("yh", "z", "tp")
    return jax.shard_map(
        body,
        mesh=fine,
        in_specs=(
            P(ctx, "tp"),
            P(ctx, "tp"),
            P(ctx, "tp"),
            P(),
            P(None, "tp"),
            P("tp", None),
            P(every, None),
        ),
        out_specs=(
            P(every, None),
            P(ctx, "tp"),
            P(ctx, "tp"),
            P(ctx, "tp"),
            P("tp", None),
            P(None, "tp"),
        ),
        check_vma=False,
    )
```

```python
import functools

import jax
import jax.numpy as jnp
from jax import lax
from jax.experimental import pallas as pl
from jax.experimental.pallas import tpu as pltpu
from jax.sharding import Mesh, PartitionSpec as P

F32 = jnp.float32
BF16 = jnp.bfloat16
KSIZE = 32
RIM = KSIZE // 2
LOW = -1e30
VMEM_BYTES = 48 * 1024 * 1024


def dot00(a, b):
    return lax.dot_general(a, b, (((0,), (0,)), ((), ())), preferred_element_type=F32)


def dot10(a, b):
    return lax.dot_general(a, b, (((1,), (0,)), ((), ())), preferred_element_type=F32)


def dot11(a, b):
    return lax.dot_general(a, b, (((1,), (1,)), ((), ())), preferred_element_type=F32)


def rows_of(count, lanes, entries):
    index = lax.broadcasted_iota(jnp.int32, (count, lanes), 0)
    out = jnp.zeros((count, lanes), F32)
    for where, value in entries:
        out = jnp.where(index == where, value, out)
    return out


def split3(x):
    high = x.astype(BF16).astype(F32)
    rest = x - high
    mid = rest.astype(BF16).astype(F32)
    return high, mid, rest - mid


def call(kernel, out_shapes, flops, scratch=(), scalars=0):
    specs = {}
    if scalars:
        count = kernel.__code__.co_argcount - len(scratch) - len(jax.tree.leaves(out_shapes))
        specs["in_specs"] = [pl.BlockSpec(memory_space=pltpu.SMEM)] + [pl.BlockSpec(memory_space=pltpu.VMEM)] * (count - 1)
    return pl.pallas_call(
        kernel,
        out_shape=out_shapes,
        **specs,
        scratch_shapes=list(scratch),
        compiler_params=pltpu.CompilerParams(vmem_limit_bytes=VMEM_BYTES),
        cost_estimate=pl.CostEstimate(flops=flops, bytes_accessed=2 ** 20, transcendentals=0),
    )


def side_of(low, high):
    lane = lax.broadcasted_iota(jnp.int32, low.shape, 1)
    return jnp.where(lane < low.shape[1] // 2, high, low)


def bias_of(place_ref, block, base):
    lane = lax.broadcasted_iota(jnp.int32, (1, 128), 1)
    return jnp.where((base + block) * 128 + lane < place_ref[2], 0.0, LOW)


def edges_of(packed):
    packed = packed.astype(F32)
    return jnp.concatenate([packed, pltpu.roll(packed, 64, 1)], axis=0)


def first_pack(place_ref, both_ref, pack_ref, pair_ref):
    own = both_ref[place_ref[4]]
    pair = both_ref[1 - place_ref[4]]
    query = pair[0:64].astype(F32)
    lane = lax.broadcasted_iota(jnp.int32, query.shape, 1)
    edge = jnp.where(lane < 32, query, pltpu.roll(query, 64, 1))
    edge = jnp.where(lane[0:32] < 64, edge[0:32], pltpu.roll(edge[32:64], 64, 1))
    pair_ref[...] = pair
    pack_ref[0:192] = own
    pack_ref[192:224] = edge.astype(BF16)


def lay_grads(shared_ref, grad_ref, low_ref, high_ref, turned_ref):
    lanes = shared_ref.shape[0]
    for i in range(lanes // 2):
        even = shared_ref[2 * i].astype(F32)
        odd = shared_ref[2 * i + 1].astype(F32)
        grad_ref[16 * i : 16 * i + 16] = jnp.concatenate([even[0:8], odd[0:8]], axis=0).astype(BF16)
        if i == 0:
            low_ref[...] = jnp.concatenate([even[8:16], odd[8:16]], axis=0).astype(BF16)
        if i == lanes // 2 - 1:
            high_ref[...] = jnp.concatenate([even[8:16], odd[8:16]], axis=0).astype(BF16)
    for piece in range(grad_ref.shape[1] // 128):
        columns = slice(128 * piece, 128 * piece + 128)
        turned_ref[columns] = grad_ref[:, columns].astype(F32).T.astype(BF16)


def attend(place_ref, all_ref, own_ref, pair_ref, mine_ref, other_ref, score_ref):
    blocks = all_ref.shape[0]
    head = 64
    width = 128
    lanes = 3 * width
    scale = head ** -0.5
    spot = place_ref[0]
    first = spot == 0
    spot_rows = place_ref[4] * blocks
    last = spot == blocks - 1
    before = lax.rem(spot + blocks - 1, blocks)
    after = lax.rem(spot + 1, blocks)
    low_here = all_ref[before, 0:head].astype(F32)
    high_here = all_ref[after, 0:head].astype(F32)
    low_there = pltpu.roll(edges_of(all_ref[before, 3 * head : 3 * head + 32]), width // 2, 1)
    high_there = edges_of(all_ref[after, 3 * head : 3 * head + 32])
    side_own = side_of(jnp.where(first, low_there, low_here), jnp.where(last, high_there, high_here))
    side_pair = side_of(jnp.where(first, low_here, low_there), jnp.where(last, high_here, high_there))
    lane = lax.broadcasted_iota(jnp.int32, (head, width), 1)
    middle = (lane >= 32) & (lane < 96)
    edges = jnp.where(middle, pltpu.roll(side_pair, width // 2, 1), side_own)
    query = jnp.concatenate([own_ref[0:head].astype(F32), pair_ref[0:head].astype(F32), edges], axis=1) * scale
    query = jnp.concatenate([query, rows_of(16, lanes, [(6, 1.0)])], axis=0).astype(BF16)
    peak = jnp.full((1, lanes), LOW, F32)
    for b in range(blocks):
        key = jnp.concatenate(
            [all_ref[b, head : 2 * head], rows_of(16, width, [(6, bias_of(place_ref, b, spot_rows))]).astype(BF16)], axis=0
        )
        score = dot00(key, query)
        score_ref[b] = score
        peak = jnp.maximum(peak, jnp.max(score, axis=0, keepdims=True))
    total = jnp.zeros((1, lanes), F32)
    out = jnp.zeros((head, lanes), F32)
    for b in range(0, blocks, 2):
        pair_weight = []
        for k in (b, b + 1):
            weight = jnp.exp(score_ref[k] - peak)
            total = total + jnp.sum(weight, axis=0, keepdims=True)
            pair_weight.append(weight.astype(BF16))
        values = jnp.concatenate([all_ref[b, 2 * head : 3 * head], all_ref[b + 1, 2 * head : 3 * head]], axis=1)
        out = out + dot10(values, jnp.concatenate(pair_weight, axis=0))
    out = out / total
    lse = peak + jnp.log(total)
    both = jnp.concatenate([out, jnp.broadcast_to(lse, (8, lanes))], axis=0)
    edges = both[:, 2 * width :]
    mine_ref[:, 0:width] = both[:, 0:width]
    mine_ref[:, width:] = edges
    other_ref[:, 0:width] = both[:, width : 2 * width]
    other_ref[:, width:] = pltpu.roll(edges, width // 2, 1)


def shifted(ring, offset):
    if offset == 0:
        return ring
    return pltpu.roll(ring, (-offset) % ring.shape[1], 1)


def middle_part(place_ref, mine_ref, got_ref, taps_ref, weight_ref, grad_ref, low_ref, high_ref, partial_ref, pack_ref):
    width = 128
    ring = 2 * width
    start = place_ref[1]
    valid = place_ref[2]
    frames = place_ref[3]
    mine = mine_ref[64:65]
    side_at = 1 - place_ref[4]
    got = got_ref[side_at, 64:65]
    top = jnp.maximum(mine, got)
    lse = top + jnp.log(jnp.exp(mine - top) + jnp.exp(got - top))
    attn = mine_ref[0:64] * jnp.exp(mine - lse) + got_ref[side_at, 0:64] * jnp.exp(got - lse)
    attn = attn.astype(BF16).astype(F32)
    lane = lax.broadcasted_iota(jnp.int32, (1, ring), 1)
    frame = start + jnp.where(lane < ring - width // 2, lane, lane - ring)
    inside = (frame >= 0) & (frame < frames) & ((lane < width + 32) | (lane >= ring - 32))
    live = inside & (frame < valid)
    masked = jnp.where(live, attn, 0.0)
    taps = taps_ref[...]
    depth = jnp.zeros((64, ring), F32)
    for t in range(KSIZE):
        depth = depth + taps[:, t : t + 1] * shifted(masked, t - RIM)
    gate = jax.nn.sigmoid(depth)
    swish = (depth[:, :width] * gate[:, :width]).astype(BF16)
    grad = grad_ref[...]
    weight = weight_ref[...]
    partial_ref[...] = dot00(swish, weight).astype(BF16)
    gap = jnp.zeros((width - 2 * RIM, grad.shape[1]), BF16)
    side = jnp.concatenate([high_ref[...], gap, low_ref[...]], axis=0)
    back = jnp.concatenate([dot11(weight, grad), dot11(weight, side)], axis=1)
    dgrad = back * gate * (1.0 + depth * (1.0 - gate))
    dgrad = jnp.where(inside, dgrad, 0.0).astype(BF16).astype(F32)
    row = lax.broadcasted_iota(jnp.int32, (64, width), 1)
    sums = jnp.zeros((64, width), F32)
    total = jnp.zeros((64, width), F32)
    for t in range(KSIZE):
        column = jnp.sum(shifted(masked, t - RIM)[:, :width] * dgrad[:, :width], axis=1, keepdims=True)
        sums = jnp.where(row == t, column, sums)
        total = total + taps[:, t : t + 1] * shifted(dgrad, RIM - t)[:, :width]
    turned = sums.T
    tap_grad = jnp.concatenate([turned[0:16, 0:64], turned[16:32, 0:64]], axis=1).astype(BF16)
    grad_out = jnp.where(live[:, :width], total, 0.0).astype(BF16)
    delta = jnp.sum(grad_out.astype(F32) * attn[:, :width], axis=0, keepdims=True)
    a, b, c = split3(-lse[:, :width])
    d, e, f = split3(-delta)
    stats = rows_of(16, width, [(0, a), (1, b), (2, c), (3, d), (4, e), (5, f), (6, 1.0)])
    pack = jnp.concatenate([grad_out, stats.astype(BF16), tap_grad, swish], axis=0)
    pack_ref[...] = pack


def backward(place_ref, all_ref, packs_ref, own_ref, pair_ref, pack_own_ref, pack_pair_ref, mine_ref, other_ref):
    blocks = all_ref.shape[0]
    base = place_ref[4] * blocks
    pair_base = blocks - base
    pair_bias = jnp.concatenate([bias_of(place_ref, place_ref[0], base), bias_of(place_ref, place_ref[0], pair_base)], axis=1)
    head = 64
    width = 128
    scale = head ** -0.5
    both = jnp.concatenate([own_ref[...], pair_ref[...]], axis=1)
    packs = jnp.concatenate([pack_own_ref[0:80], pack_pair_ref[0:80]], axis=1)
    query = (both[0:head].astype(F32) * scale).astype(BF16)
    query = jnp.concatenate([query, packs[head : head + 16]], axis=0)
    ones = [(0, 1.0), (1, 1.0), (2, 1.0)]
    key_rows = rows_of(16, 2 * width, ones + [(6, pair_bias)]).astype(BF16)
    key = jnp.concatenate([both[head : 2 * head], key_rows], axis=0)
    value_rows = rows_of(16, 2 * width, [(3, 1.0), (4, 1.0), (5, 1.0)]).astype(BF16)
    value = jnp.concatenate([both[2 * head : 3 * head], value_rows], axis=0)
    d_query = jnp.zeros((head, 2 * width), F32)
    d_key = jnp.zeros((head, 2 * width), F32)
    d_value = jnp.zeros((head, 2 * width), F32)
    tap_sum = jnp.zeros((16, width), F32)
    for first in range(0, blocks, 2):
        keys, queries, grads, query_scores, key_scores, weights = [], [], [], [], [], []
        for b in (first, first + 1):
            key_b = all_ref[b, head : 2 * head]
            key_aug = jnp.concatenate([key_b, rows_of(16, width, ones + [(6, bias_of(place_ref, b, base))]).astype(BF16)], axis=0)
            value_aug = jnp.concatenate([all_ref[b, 2 * head : 3 * head], value_rows[:, :width]], axis=0)
            weight = jnp.exp(dot00(key_aug, query))
            query_scores.append((weight * dot00(value_aug, packs)).astype(BF16))
            keys.append(key_b)
            query_b = (all_ref[b, 0:head].astype(F32) * scale).astype(BF16)
            query_aug = jnp.concatenate([query_b, packs_ref[b, head : head + 16]], axis=0)
            weight = jnp.exp(dot00(query_aug, key))
            key_scores.append((weight * dot00(packs_ref[b, 0:80], value)).astype(BF16))
            weights.append(weight.astype(BF16))
            queries.append(query_b)
            grads.append(packs_ref[b, 0:head])
            tap_sum = tap_sum + packs_ref[b, 80:96].astype(F32)
        d_query = d_query + dot10(jnp.concatenate(keys, axis=1), jnp.concatenate(query_scores, axis=0))
        d_key = d_key + dot10(jnp.concatenate(queries, axis=1), jnp.concatenate(key_scores, axis=0))
        d_value = d_value + dot10(jnp.concatenate(grads, axis=1), jnp.concatenate(weights, axis=0))
    d_query = d_query * scale
    for ref, at in ((mine_ref, 0), (other_ref, width)):
        kind = ref.dtype
        ref[0:head] = d_query[:, at : at + width].astype(kind)
        ref[head : 2 * head] = d_key[:, at : at + width].astype(kind)
        ref[2 * head : 3 * head] = d_value[:, at : at + width].astype(kind)
        ref[3 * head : 3 * head + 16] = tap_sum.astype(kind)


def finish(norm, mine_ref, got_ref, query_ref, key_ref, value_ref, taps_ref):
    total = mine_ref[...] + got_ref[...].astype(F32)
    query_ref[...] = total[0:64].astype(BF16)
    key_ref[...] = total[64:128].astype(BF16)
    value_ref[...] = total[128:192].astype(BF16)
    tap = total[192:208] * norm
    taps_ref[0:16] = tap[:, 0:64]
    taps_ref[16:32] = tap[:, 64:128]


def mix_slab(packs_ref, slab_ref, out_ref):
    rows = out_ref.shape[0]
    total = jnp.zeros((2 * rows, 64), F32)
    for b in range(packs_ref.shape[0]):
        total = total + dot11(slab_ref[b], packs_ref[b, 96:160])
    out_ref[...] = jnp.concatenate([total[0:rows], total[rows:]], axis=1)


def mix_spread(both_ref, out_ref):
    total = (both_ref[0] + both_ref[1]).astype(BF16)
    for j in range(out_ref.shape[0]):
        out_ref[j] = total


def mix_place(norm, parts_ref, out_ref):
    rows = []
    for z in range(parts_ref.shape[0]):
        both = parts_ref[z].astype(F32)
        rows += [both[:, 0:64], both[:, 64:128]]
    full = jnp.concatenate(rows, axis=0) * norm
    for piece in range(out_ref.shape[1] // 128):
        columns = slice(128 * piece, 128 * piece + 128)
        out_ref[:, columns] = full[columns].T


def sum_blocks(parts_ref, out_ref):
    total = jnp.zeros(out_ref.shape, F32)
    for j in range(parts_ref.shape[0]):
        total = total + parts_ref[j].astype(F32)
    out_ref[...] = total.astype(BF16)


def body(query_rows, key_rows, value_rows, valid_frames, depth_kernel, mix_weight, out_grad):
    width, head = query_rows.shape
    depth = lax.axis_size("z")
    ctx = ("yh", "z")
    devices = 2 * depth
    lanes = lax.axis_size("tp")
    model = mix_weight.shape[1]
    rows8 = out_grad.shape[0]
    norm = (width * devices) ** -0.5
    valid = valid_frames[0]
    half = lax.axis_index("yh")
    spot = lax.axis_index("z")
    place = jnp.stack([spot, (half * depth + spot) * width, valid, jnp.int32(width * devices), half]).astype(jnp.int32)
    swap = [(0, 1), (1, 0)]
    taps = depth_kernel.T
    rim_pairs = []
    sides = RIM // rows8
    for i in range(devices - 1):
        for k in range(sides):
            rim_pairs.append((i * lanes + lanes - sides + k, (i + 1) * lanes + k))
            rim_pairs.append(((i + 1) * lanes + k, i * lanes + lanes - sides + k))

    rim_rows = lax.ppermute(out_grad, ("yh", "z", "tp"), rim_pairs)
    own = jnp.concatenate([query_rows.T, key_rows.T, value_rows.T], axis=0)
    both = lax.all_gather(own, "yh", axis=0)
    rim_rows, both = lax.optimization_barrier((rim_rows, both))
    front, pair = call(
        first_pack,
        (jax.ShapeDtypeStruct((3 * head + 32, width), BF16), jax.ShapeDtypeStruct((3 * head, width), BF16)),
        2 ** 20,
        scalars=1,
    )(place, both)
    with_rim = jnp.concatenate([out_grad, rim_rows], axis=0)
    shared = lax.all_to_all(jnp.broadcast_to(with_rim[None], (lanes,) + with_rim.shape), "tp", 0, 0, tiled=True)
    everyone = lax.all_gather(front, "z", axis=0)
    shared, everyone = lax.optimization_barrier((shared, everyone))

    part = jax.ShapeDtypeStruct((head + 8, 2 * width), F32)
    block = jax.ShapeDtypeStruct((head, width), BF16)
    mine, other = call(
        attend, (part, part), 2 ** 28, [pltpu.VMEM((depth, width, 3 * width), F32)], scalars=1
    )(place, everyone, own, pair)
    shared, other = lax.optimization_barrier((shared, other))
    got = lax.all_gather(other, "yh", axis=0)
    rim_shape = jax.ShapeDtypeStruct((RIM, model), BF16)
    grad_block, grad_low, grad_high, turned = call(
        lay_grads,
        (jax.ShapeDtypeStruct((width, model), BF16), rim_shape, rim_shape, jax.ShapeDtypeStruct((model, width), BF16)),
        2 ** 33,
    )(shared)
    slab = lax.all_to_all(turned.reshape(depth, model // depth, width), "z", 0, 0, tiled=True)
    pack_rows = 96 + head
    partial, pack = call(
        middle_part,
        (
            jax.ShapeDtypeStruct((width, model), BF16),
            jax.ShapeDtypeStruct((pack_rows, width), BF16),
        ),
        2 ** 27,
        scalars=1,
    )(place, mine, got, taps, mix_weight, grad_block, grad_low, grad_high)
    pack_pair = lax.ppermute(pack, "yh", swap)
    packs = lax.all_gather(pack, "z", axis=0)
    packs, pack_pair, slab, partial = lax.optimization_barrier((packs, pack_pair, slab, partial))

    slab_rows = model // depth // 2
    mix_mine = call(mix_slab, jax.ShapeDtypeStruct((slab_rows, width), F32), 2 ** 27)(packs, slab)
    mix_both = lax.all_gather(mix_mine, "yh", axis=0)
    spread = call(mix_spread, jax.ShapeDtypeStruct((depth, slab_rows, width), BF16), 2 ** 20)(mix_both)
    block_parts = lax.all_to_all(partial.reshape(lanes, rows8, model), "tp", 0, 0, tiled=True)
    spread, block_parts = lax.optimization_barrier((spread, block_parts))
    pieces = lax.all_to_all(spread, "z", 0, 0, tiled=True)
    result = jax.ShapeDtypeStruct((3 * head + 16, width), F32)
    sent = jax.ShapeDtypeStruct(result.shape, BF16)
    mine, other = call(backward, (result, sent), 2 ** 29, scalars=1)(
        place, everyone, packs, own, pair, pack, pack_pair
    )
    got = lax.ppermute(other, "yh", swap)
    d_query, d_key, d_value, tap_total = call(
        functools.partial(finish, norm), (block, block, block, jax.ShapeDtypeStruct((KSIZE, head), F32)), 2 ** 20
    )(mine, got)

    block_out = call(sum_blocks, jax.ShapeDtypeStruct((rows8, model), BF16), 2 ** 20)(block_parts)
    mix_grad = call(functools.partial(mix_place, norm), jax.ShapeDtypeStruct((head, model), F32), 2 ** 20)(pieces)
    return block_out, d_query.T, d_key.T, d_value.T, mix_grad, tap_total


def solution(mesh):
    count = mesh.shape["ctx"]
    fine = Mesh(mesh.devices.reshape(2, count // 2, mesh.shape["tp"]), ("yh", "z", "tp"))
    ctx = ("yh", "z")
    every = ("yh", "z", "tp")
    return jax.shard_map(
        body,
        mesh=fine,
        in_specs=(
            P(ctx, "tp"),
            P(ctx, "tp"),
            P(ctx, "tp"),
            P(),
            P(None, "tp"),
            P("tp", None),
            P(every, None),
        ),
        out_specs=(
            P(every, None),
            P(ctx, "tp"),
            P(ctx, "tp"),
            P(ctx, "tp"),
            P("tp", None),
            P(None, "tp"),
        ),
        check_vma=False,
    )
```

```python
import functools

import jax
import jax.numpy as jnp
from jax import lax
from jax.experimental import pallas as pl
from jax.experimental.pallas import tpu as pltpu
from jax.sharding import Mesh, PartitionSpec as P

F32 = jnp.float32
BF16 = jnp.bfloat16
KSIZE = 32
RIM = KSIZE // 2
LOW = -1e30
VMEM_BYTES = 48 * 1024 * 1024


def dot00(a, b):
    return lax.dot_general(a, b, (((0,), (0,)), ((), ())), preferred_element_type=F32)


def dot10(a, b):
    return lax.dot_general(a, b, (((1,), (0,)), ((), ())), preferred_element_type=F32)


def dot11(a, b):
    return lax.dot_general(a, b, (((1,), (1,)), ((), ())), preferred_element_type=F32)


def rows_of(count, lanes, entries):
    index = lax.broadcasted_iota(jnp.int32, (count, lanes), 0)
    out = jnp.zeros((count, lanes), F32)
    for where, value in entries:
        out = jnp.where(index == where, value, out)
    return out


def split3(x):
    high = x.astype(BF16).astype(F32)
    rest = x - high
    mid = rest.astype(BF16).astype(F32)
    return high, mid, rest - mid


def call(kernel, out_shapes, flops, scratch=(), scalars=0):
    specs = {}
    if scalars:
        count = kernel.__code__.co_argcount - len(scratch) - len(jax.tree.leaves(out_shapes))
        specs["in_specs"] = [pl.BlockSpec(memory_space=pltpu.SMEM)] + [pl.BlockSpec(memory_space=pltpu.VMEM)] * (count - 1)
    return pl.pallas_call(
        kernel,
        out_shape=out_shapes,
        **specs,
        scratch_shapes=list(scratch),
        compiler_params=pltpu.CompilerParams(vmem_limit_bytes=VMEM_BYTES),
        cost_estimate=pl.CostEstimate(flops=flops, bytes_accessed=2 ** 20, transcendentals=0),
    )


def side_of(low, high):
    lane = lax.broadcasted_iota(jnp.int32, low.shape, 1)
    return jnp.where(lane < low.shape[1] // 2, high, low)


def bias_of(place_ref, block, base):
    lane = lax.broadcasted_iota(jnp.int32, (1, 128), 1)
    return jnp.where((base + block) * 128 + lane < place_ref[2], 0.0, LOW)


def edges_of(packed):
    packed = packed.astype(F32)
    return jnp.concatenate([packed, pltpu.roll(packed, 64, 1)], axis=0)


def first_pack(place_ref, both_ref, pack_ref, pair_ref):
    own = both_ref[place_ref[4]]
    pair = both_ref[1 - place_ref[4]]
    query = pair[0:64].astype(F32)
    lane = lax.broadcasted_iota(jnp.int32, query.shape, 1)
    edge = jnp.where(lane < 32, query, pltpu.roll(query, 64, 1))
    edge = jnp.where(lane[0:32] < 64, edge[0:32], pltpu.roll(edge[32:64], 64, 1))
    pair_ref[...] = pair
    pack_ref[0:192] = own
    pack_ref[192:224] = edge.astype(BF16)


def lay_grads(shared_ref, grad_ref, low_ref, high_ref):
    lanes = shared_ref.shape[0]
    for i in range(lanes // 2):
        even = shared_ref[2 * i].astype(F32)
        odd = shared_ref[2 * i + 1].astype(F32)
        grad_ref[16 * i : 16 * i + 16] = jnp.concatenate([even[0:8], odd[0:8]], axis=0).astype(BF16)
        if i == 0:
            low_ref[...] = jnp.concatenate([even[8:16], odd[8:16]], axis=0).astype(BF16)
        if i == lanes // 2 - 1:
            high_ref[...] = jnp.concatenate([even[8:16], odd[8:16]], axis=0).astype(BF16)


def attend(place_ref, all_ref, own_ref, pair_ref, mine_ref, other_ref, score_ref):
    blocks = all_ref.shape[0]
    head = 64
    width = 128
    lanes = 3 * width
    scale = head ** -0.5
    spot = place_ref[0]
    first = spot == 0
    spot_rows = place_ref[4] * blocks
    last = spot == blocks - 1
    before = lax.rem(spot + blocks - 1, blocks)
    after = lax.rem(spot + 1, blocks)
    low_here = all_ref[before, 0:head].astype(F32)
    high_here = all_ref[after, 0:head].astype(F32)
    low_there = pltpu.roll(edges_of(all_ref[before, 3 * head : 3 * head + 32]), width // 2, 1)
    high_there = edges_of(all_ref[after, 3 * head : 3 * head + 32])
    side_own = side_of(jnp.where(first, low_there, low_here), jnp.where(last, high_there, high_here))
    side_pair = side_of(jnp.where(first, low_here, low_there), jnp.where(last, high_here, high_there))
    lane = lax.broadcasted_iota(jnp.int32, (head, width), 1)
    middle = (lane >= 32) & (lane < 96)
    edges = jnp.where(middle, pltpu.roll(side_pair, width // 2, 1), side_own)
    query = jnp.concatenate([own_ref[0:head].astype(F32), pair_ref[0:head].astype(F32), edges], axis=1) * scale
    query = jnp.concatenate([query, rows_of(16, lanes, [(6, 1.0)])], axis=0).astype(BF16)
    peak = jnp.full((1, lanes), LOW, F32)
    for b in range(blocks):
        key = jnp.concatenate(
            [all_ref[b, head : 2 * head], rows_of(16, width, [(6, bias_of(place_ref, b, spot_rows))]).astype(BF16)], axis=0
        )
        score = dot00(key, query)
        score_ref[b] = score
        peak = jnp.maximum(peak, jnp.max(score, axis=0, keepdims=True))
    total = jnp.zeros((1, lanes), F32)
    out = jnp.zeros((head, lanes), F32)
    for b in range(0, blocks, 2):
        pair_weight = []
        for k in (b, b + 1):
            weight = jnp.exp(score_ref[k] - peak)
            total = total + jnp.sum(weight, axis=0, keepdims=True)
            pair_weight.append(weight.astype(BF16))
        values = jnp.concatenate([all_ref[b, 2 * head : 3 * head], all_ref[b + 1, 2 * head : 3 * head]], axis=1)
        out = out + dot10(values, jnp.concatenate(pair_weight, axis=0))
    out = out / total
    lse = peak + jnp.log(total)
    both = jnp.concatenate([out, jnp.broadcast_to(lse, (8, lanes))], axis=0)
    edges = both[:, 2 * width :]
    mine_ref[:, 0:width] = both[:, 0:width]
    mine_ref[:, width:] = edges
    other_ref[:, 0:width] = both[:, width : 2 * width]
    other_ref[:, width:] = pltpu.roll(edges, width // 2, 1)


def shifted(ring, offset):
    if offset == 0:
        return ring
    return pltpu.roll(ring, (-offset) % ring.shape[1], 1)


def middle_part(place_ref, mine_ref, got_ref, taps_ref, weight_ref, grad_ref, low_ref, high_ref, partial_ref, pack_ref, copies_ref):
    width = 128
    ring = 2 * width
    start = place_ref[1]
    valid = place_ref[2]
    frames = place_ref[3]
    mine = mine_ref[64:65]
    side_at = 1 - place_ref[4]
    got = got_ref[side_at, 64:65]
    top = jnp.maximum(mine, got)
    lse = top + jnp.log(jnp.exp(mine - top) + jnp.exp(got - top))
    attn = mine_ref[0:64] * jnp.exp(mine - lse) + got_ref[side_at, 0:64] * jnp.exp(got - lse)
    attn = attn.astype(BF16).astype(F32)
    lane = lax.broadcasted_iota(jnp.int32, (1, ring), 1)
    frame = start + jnp.where(lane < ring - width // 2, lane, lane - ring)
    inside = (frame >= 0) & (frame < frames) & ((lane < width + 32) | (lane >= ring - 32))
    live = inside & (frame < valid)
    masked = jnp.where(live, attn, 0.0)
    taps = taps_ref[...]
    depth = jnp.zeros((64, ring), F32)
    for t in range(KSIZE):
        depth = depth + taps[:, t : t + 1] * shifted(masked, t - RIM)
    gate = jax.nn.sigmoid(depth)
    swish = (depth[:, :width] * gate[:, :width]).astype(BF16)
    grad = grad_ref[...]
    mix = dot10(swish, grad)
    mix = jnp.concatenate([mix[:, at : at + width] for at in range(0, mix.shape[1], width)], axis=0).astype(BF16)
    weight = weight_ref[...]
    partial_ref[...] = dot00(swish, weight).astype(BF16)
    gap = jnp.zeros((width - 2 * RIM, grad.shape[1]), BF16)
    side = jnp.concatenate([high_ref[...], gap, low_ref[...]], axis=0)
    back = jnp.concatenate([dot11(weight, grad), dot11(weight, side)], axis=1)
    dgrad = back * gate * (1.0 + depth * (1.0 - gate))
    dgrad = jnp.where(inside, dgrad, 0.0).astype(BF16).astype(F32)
    row = lax.broadcasted_iota(jnp.int32, (64, width), 1)
    sums = jnp.zeros((64, width), F32)
    total = jnp.zeros((64, width), F32)
    for t in range(KSIZE):
        column = jnp.sum(shifted(masked, t - RIM)[:, :width] * dgrad[:, :width], axis=1, keepdims=True)
        sums = jnp.where(row == t, column, sums)
        total = total + taps[:, t : t + 1] * shifted(dgrad, RIM - t)[:, :width]
    turned = sums.T
    tap_grad = jnp.concatenate([turned[0:16, 0:64], turned[16:32, 0:64]], axis=1).astype(BF16)
    grad_out = jnp.where(live[:, :width], total, 0.0).astype(BF16)
    delta = jnp.sum(grad_out.astype(F32) * attn[:, :width], axis=0, keepdims=True)
    a, b, c = split3(-lse[:, :width])
    d, e, f = split3(-delta)
    stats = rows_of(16, width, [(0, a), (1, b), (2, c), (3, d), (4, e), (5, f), (6, 1.0)])
    pack = jnp.concatenate([grad_out, stats.astype(BF16), tap_grad], axis=0)
    pack_ref[...] = pack
    share = copies_ref.shape[1] - 96
    for j in range(copies_ref.shape[0]):
        copies_ref[j, 0:96] = pack
        copies_ref[j, 96:] = mix[j * share : (j + 1) * share]


def backward(place_ref, all_ref, packs_ref, own_ref, pair_ref, pack_own_ref, pack_pair_ref, mine_ref, other_ref):
    blocks = all_ref.shape[0]
    base = place_ref[4] * blocks
    pair_base = blocks - base
    pair_bias = jnp.concatenate([bias_of(place_ref, place_ref[0], base), bias_of(place_ref, place_ref[0], pair_base)], axis=1)
    head = 64
    width = 128
    scale = head ** -0.5
    both = jnp.concatenate([own_ref[...], pair_ref[...]], axis=1)
    packs = jnp.concatenate([pack_own_ref[0:80], pack_pair_ref[0:80]], axis=1)
    query = (both[0:head].astype(F32) * scale).astype(BF16)
    query = jnp.concatenate([query, packs[head : head + 16]], axis=0)
    ones = [(0, 1.0), (1, 1.0), (2, 1.0)]
    key_rows = rows_of(16, 2 * width, ones + [(6, pair_bias)]).astype(BF16)
    key = jnp.concatenate([both[head : 2 * head], key_rows], axis=0)
    value_rows = rows_of(16, 2 * width, [(3, 1.0), (4, 1.0), (5, 1.0)]).astype(BF16)
    value = jnp.concatenate([both[2 * head : 3 * head], value_rows], axis=0)
    d_query = jnp.zeros((head, 2 * width), F32)
    d_key = jnp.zeros((head, 2 * width), F32)
    d_value = jnp.zeros((head, 2 * width), F32)
    tap_sum = jnp.zeros((16, width), F32)
    for first in range(0, blocks, 2):
        keys, queries, grads, query_scores, key_scores, weights = [], [], [], [], [], []
        for b in (first, first + 1):
            key_b = all_ref[b, head : 2 * head]
            key_aug = jnp.concatenate([key_b, rows_of(16, width, ones + [(6, bias_of(place_ref, b, base))]).astype(BF16)], axis=0)
            value_aug = jnp.concatenate([all_ref[b, 2 * head : 3 * head], value_rows[:, :width]], axis=0)
            weight = jnp.exp(dot00(key_aug, query))
            query_scores.append((weight * dot00(value_aug, packs)).astype(BF16))
            keys.append(key_b)
            query_b = (all_ref[b, 0:head].astype(F32) * scale).astype(BF16)
            query_aug = jnp.concatenate([query_b, packs_ref[b, head : head + 16]], axis=0)
            weight = jnp.exp(dot00(query_aug, key))
            key_scores.append((weight * dot00(packs_ref[b, 0:80], value)).astype(BF16))
            weights.append(weight.astype(BF16))
            queries.append(query_b)
            grads.append(packs_ref[b, 0:head])
            tap_sum = tap_sum + packs_ref[b, 80:96].astype(F32)
        d_query = d_query + dot10(jnp.concatenate(keys, axis=1), jnp.concatenate(query_scores, axis=0))
        d_key = d_key + dot10(jnp.concatenate(queries, axis=1), jnp.concatenate(key_scores, axis=0))
        d_value = d_value + dot10(jnp.concatenate(grads, axis=1), jnp.concatenate(weights, axis=0))
    d_query = d_query * scale
    for ref, at in ((mine_ref, 0), (other_ref, width)):
        kind = ref.dtype
        ref[0:head] = d_query[:, at : at + width].astype(kind)
        ref[head : 2 * head] = d_key[:, at : at + width].astype(kind)
        ref[2 * head : 3 * head] = d_value[:, at : at + width].astype(kind)
        ref[3 * head : 3 * head + 16] = tap_sum.astype(kind)


def finish(norm, mine_ref, got_ref, query_ref, key_ref, value_ref, taps_ref):
    total = mine_ref[...] + got_ref[...].astype(F32)
    query_ref[...] = total[0:64].astype(BF16)
    key_ref[...] = total[64:128].astype(BF16)
    value_ref[...] = total[128:192].astype(BF16)
    tap = total[192:208] * norm
    taps_ref[0:16] = tap[:, 0:64]
    taps_ref[16:32] = tap[:, 64:128]


def mix_sum(packs_ref, out_ref):
    total = jnp.zeros(out_ref.shape, F32)
    for j in range(packs_ref.shape[0]):
        total = total + packs_ref[j, 96:].astype(F32)
    out_ref[...] = total


def mix_spread(both_ref, out_ref):
    total = (both_ref[0] + both_ref[1]).astype(BF16)
    for j in range(out_ref.shape[0]):
        out_ref[j] = total


def mix_place(norm, parts_ref, out_ref):
    for piece in range(parts_ref.shape[0]):
        out_ref[:, piece * 128 : (piece + 1) * 128] = parts_ref[piece].astype(F32) * norm


def sum_blocks(parts_ref, out_ref):
    total = jnp.zeros(out_ref.shape, F32)
    for j in range(parts_ref.shape[0]):
        total = total + parts_ref[j].astype(F32)
    out_ref[...] = total.astype(BF16)


def body(query_rows, key_rows, value_rows, valid_frames, depth_kernel, mix_weight, out_grad):
    width, head = query_rows.shape
    depth = lax.axis_size("z")
    ctx = ("yh", "z")
    devices = 2 * depth
    lanes = lax.axis_size("tp")
    model = mix_weight.shape[1]
    rows8 = out_grad.shape[0]
    norm = (width * devices) ** -0.5
    valid = valid_frames[0]
    half = lax.axis_index("yh")
    spot = lax.axis_index("z")
    place = jnp.stack([spot, (half * depth + spot) * width, valid, jnp.int32(width * devices), half]).astype(jnp.int32)
    swap = [(0, 1), (1, 0)]
    taps = depth_kernel.T
    rim_pairs = []
    sides = RIM // rows8
    for i in range(devices - 1):
        for k in range(sides):
            rim_pairs.append((i * lanes + lanes - sides + k, (i + 1) * lanes + k))
            rim_pairs.append(((i + 1) * lanes + k, i * lanes + lanes - sides + k))

    rim_rows = lax.ppermute(out_grad, ("yh", "z", "tp"), rim_pairs)
    own = jnp.concatenate([query_rows.T, key_rows.T, value_rows.T], axis=0)
    both = lax.all_gather(own, "yh", axis=0)
    rim_rows, both = lax.optimization_barrier((rim_rows, both))
    front, pair = call(
        first_pack,
        (jax.ShapeDtypeStruct((3 * head + 32, width), BF16), jax.ShapeDtypeStruct((3 * head, width), BF16)),
        2 ** 20,
        scalars=1,
    )(place, both)
    with_rim = jnp.concatenate([out_grad, rim_rows], axis=0)
    shared = lax.all_to_all(jnp.broadcast_to(with_rim[None], (lanes,) + with_rim.shape), "tp", 0, 0, tiled=True)
    everyone = lax.all_gather(front, "z", axis=0)
    shared, everyone = lax.optimization_barrier((shared, everyone))

    part = jax.ShapeDtypeStruct((head + 8, 2 * width), F32)
    block = jax.ShapeDtypeStruct((head, width), BF16)
    mine, other = call(
        attend, (part, part), 2 ** 28, [pltpu.VMEM((depth, width, 3 * width), F32)], scalars=1
    )(place, everyone, own, pair)
    shared, other = lax.optimization_barrier((shared, other))
    got = lax.all_gather(other, "yh", axis=0)
    rim_shape = jax.ShapeDtypeStruct((RIM, model), BF16)
    grad_block, grad_low, grad_high = call(
        lay_grads, (jax.ShapeDtypeStruct((width, model), BF16), rim_shape, rim_shape), 2 ** 22
    )(shared)
    share = head * model // width // depth
    partial, pack, copies = call(
        middle_part,
        (
            jax.ShapeDtypeStruct((width, model), BF16),
            jax.ShapeDtypeStruct((96, width), BF16),
            jax.ShapeDtypeStruct((depth, 96 + share, width), BF16),
        ),
        2 ** 27,
        scalars=1,
    )(place, mine, got, taps, mix_weight, grad_block, grad_low, grad_high)
    packs = lax.all_to_all(copies, "z", 0, 0, tiled=True)
    pack_pair = lax.ppermute(pack, "yh", swap)
    packs, pack_pair, partial = lax.optimization_barrier((packs, pack_pair, partial))

    mix_mine = call(mix_sum, jax.ShapeDtypeStruct((share, width), F32), 2 ** 22)(packs)
    mix_both = lax.all_gather(mix_mine, "yh", axis=0)
    spread = call(mix_spread, jax.ShapeDtypeStruct((depth, share, width), BF16), 2 ** 20)(mix_both)
    block_parts = lax.all_to_all(partial.reshape(lanes, rows8, model), "tp", 0, 0, tiled=True)
    spread, block_parts = lax.optimization_barrier((spread, block_parts))
    pieces = lax.all_to_all(spread, "z", 0, 0, tiled=True).reshape(model // width, head, width)
    result = jax.ShapeDtypeStruct((3 * head + 16, width), F32)
    sent = jax.ShapeDtypeStruct(result.shape, BF16)
    mine, other = call(backward, (result, sent), 2 ** 29, scalars=1)(
        place, everyone, packs, own, pair, pack, pack_pair
    )
    got = lax.ppermute(other, "yh", swap)
    d_query, d_key, d_value, tap_total = call(
        functools.partial(finish, norm), (block, block, block, jax.ShapeDtypeStruct((KSIZE, head), F32)), 2 ** 20
    )(mine, got)

    block_out = call(sum_blocks, jax.ShapeDtypeStruct((rows8, model), BF16), 2 ** 20)(block_parts)
    mix_grad = call(functools.partial(mix_place, norm), jax.ShapeDtypeStruct((head, model), F32), 2 ** 20)(pieces)
    return block_out, d_query.T, d_key.T, d_value.T, mix_grad, tap_total


def solution(mesh):
    count = mesh.shape["ctx"]
    fine = Mesh(mesh.devices.reshape(2, count // 2, mesh.shape["tp"]), ("yh", "z", "tp"))
    ctx = ("yh", "z")
    every = ("yh", "z", "tp")
    return jax.shard_map(
        body,
        mesh=fine,
        in_specs=(
            P(ctx, "tp"),
            P(ctx, "tp"),
            P(ctx, "tp"),
            P(),
            P(None, "tp"),
            P("tp", None),
            P(every, None),
        ),
        out_specs=(
            P(every, None),
            P(ctx, "tp"),
            P(ctx, "tp"),
            P(ctx, "tp"),
            P("tp", None),
            P(None, "tp"),
        ),
        check_vma=False,
    )
```

```python
import functools

import jax
import jax.numpy as jnp
from jax import lax
from jax.experimental import pallas as pl
from jax.experimental.pallas import tpu as pltpu
from jax.sharding import Mesh, PartitionSpec as P

F32 = jnp.float32
BF16 = jnp.bfloat16
KSIZE = 32
RIM = KSIZE // 2
LOW = -1e30
VMEM_BYTES = 48 * 1024 * 1024


def dot00(a, b):
    return lax.dot_general(a, b, (((0,), (0,)), ((), ())), preferred_element_type=F32)


def dot10(a, b):
    return lax.dot_general(a, b, (((1,), (0,)), ((), ())), preferred_element_type=F32)


def dot11(a, b):
    return lax.dot_general(a, b, (((1,), (1,)), ((), ())), preferred_element_type=F32)


def rows_of(count, lanes, entries):
    index = lax.broadcasted_iota(jnp.int32, (count, lanes), 0)
    out = jnp.zeros((count, lanes), F32)
    for where, value in entries:
        out = jnp.where(index == where, value, out)
    return out


def split3(x):
    high = x.astype(BF16).astype(F32)
    rest = x - high
    mid = rest.astype(BF16).astype(F32)
    return high, mid, rest - mid


def call(kernel, out_shapes, flops, scratch=(), scalars=0, remote=0):
    specs = {}
    if scalars:
        count = kernel.__code__.co_argcount - len(scratch) - len(jax.tree.leaves(out_shapes))
        spaces = [pltpu.SMEM] + [pl.ANY] * remote + [pltpu.VMEM] * (count - 1 - remote)
        specs["in_specs"] = [pl.BlockSpec(memory_space=space) for space in spaces]
    return pl.pallas_call(
        kernel,
        out_shape=out_shapes,
        **specs,
        scratch_shapes=list(scratch),
        compiler_params=pltpu.CompilerParams(vmem_limit_bytes=VMEM_BYTES),
        cost_estimate=pl.CostEstimate(flops=flops, bytes_accessed=2 ** 20, transcendentals=0),
    )


def side_of(low, high):
    lane = lax.broadcasted_iota(jnp.int32, low.shape, 1)
    return jnp.where(lane < low.shape[1] // 2, high, low)


def bias_of(place_ref, block, base):
    lane = lax.broadcasted_iota(jnp.int32, (1, 128), 1)
    return jnp.where((base + block) * 128 + lane < place_ref[2], 0.0, LOW)


def edges_of(packed):
    packed = packed.astype(F32)
    return jnp.concatenate([packed, pltpu.roll(packed, 64, 1)], axis=0)


def first_pack(place_ref, both_ref, pack_ref, pair_ref):
    own = both_ref[place_ref[4]]
    pair = both_ref[1 - place_ref[4]]
    query = pair[0:64].astype(F32)
    lane = lax.broadcasted_iota(jnp.int32, query.shape, 1)
    edge = jnp.where(lane < 32, query, pltpu.roll(query, 64, 1))
    edge = jnp.where(lane[0:32] < 64, edge[0:32], pltpu.roll(edge[32:64], 64, 1))
    pair_ref[...] = pair
    pack_ref[0:192] = own
    pack_ref[192:224] = edge.astype(BF16)


def lay_grads(shared_ref):
    rows = []
    for i in range(shared_ref.shape[0] // 2):
        even = shared_ref[2 * i].astype(F32)
        odd = shared_ref[2 * i + 1].astype(F32)
        rows.append(jnp.concatenate([even[0:8], odd[0:8]], axis=0).astype(BF16))
        rim = jnp.concatenate([even[8:16], odd[8:16]], axis=0).astype(BF16)
        if i == 0:
            low = rim
    gap = jnp.zeros((128 - 2 * RIM, shared_ref.shape[2]), BF16)
    return jnp.concatenate(rows, axis=0), jnp.concatenate([rim, gap, low], axis=0)


def attend(place_ref, all_ref, own_ref, pair_ref, mine_ref, other_ref, score_ref):
    blocks = all_ref.shape[0]
    head = 64
    width = 128
    lanes = 3 * width
    scale = head ** -0.5
    spot = place_ref[0]
    first = spot == 0
    spot_rows = place_ref[4] * blocks
    last = spot == blocks - 1
    before = lax.rem(spot + blocks - 1, blocks)
    after = lax.rem(spot + 1, blocks)
    low_here = all_ref[before, 0:head].astype(F32)
    high_here = all_ref[after, 0:head].astype(F32)
    low_there = pltpu.roll(edges_of(all_ref[before, 3 * head : 3 * head + 32]), width // 2, 1)
    high_there = edges_of(all_ref[after, 3 * head : 3 * head + 32])
    side_own = side_of(jnp.where(first, low_there, low_here), jnp.where(last, high_there, high_here))
    side_pair = side_of(jnp.where(first, low_here, low_there), jnp.where(last, high_here, high_there))
    lane = lax.broadcasted_iota(jnp.int32, (head, width), 1)
    middle = (lane >= 32) & (lane < 96)
    edges = jnp.where(middle, pltpu.roll(side_pair, width // 2, 1), side_own)
    query = jnp.concatenate([own_ref[0:head].astype(F32), pair_ref[0:head].astype(F32), edges], axis=1) * scale
    query = jnp.concatenate([query, rows_of(16, lanes, [(6, 1.0)])], axis=0).astype(BF16)
    peak = jnp.full((1, lanes), LOW, F32)
    for b in range(blocks):
        key = jnp.concatenate(
            [all_ref[b, head : 2 * head], rows_of(16, width, [(6, bias_of(place_ref, b, spot_rows))]).astype(BF16)], axis=0
        )
        score = dot00(key, query)
        score_ref[b] = score
        peak = jnp.maximum(peak, jnp.max(score, axis=0, keepdims=True))
    total = jnp.zeros((1, lanes), F32)
    out = jnp.zeros((head, lanes), F32)
    for b in range(0, blocks, 2):
        pair_weight = []
        for k in (b, b + 1):
            weight = jnp.exp(score_ref[k] - peak)
            total = total + jnp.sum(weight, axis=0, keepdims=True)
            pair_weight.append(weight.astype(BF16))
        values = jnp.concatenate([all_ref[b, 2 * head : 3 * head], all_ref[b + 1, 2 * head : 3 * head]], axis=1)
        out = out + dot10(values, jnp.concatenate(pair_weight, axis=0))
    out = out / total
    lse = peak + jnp.log(total)
    both = jnp.concatenate([out, jnp.broadcast_to(lse, (8, lanes))], axis=0)
    edges = both[:, 2 * width :]
    mine_ref[:, 0:width] = both[:, 0:width]
    mine_ref[:, width:] = edges
    other_ref[:, 0:width] = both[:, width : 2 * width]
    other_ref[:, width:] = pltpu.roll(edges, width // 2, 1)


def shifted(ring, offset):
    if offset == 0:
        return ring
    return pltpu.roll(ring, (-offset) % ring.shape[1], 1)


def middle_part(place_ref, weight_hbm, mine_ref, got_ref, taps_ref, shared_ref, keep_ref, send_ref, pack_ref, copies_ref, weight_ref, sem):
    fetch = pltpu.make_async_copy(weight_hbm, weight_ref, sem)
    fetch.start()
    width = 128
    ring = 2 * width
    start = place_ref[1]
    valid = place_ref[2]
    frames = place_ref[3]
    mine = mine_ref[64:65]
    side_at = 1 - place_ref[4]
    got = got_ref[side_at, 64:65]
    top = jnp.maximum(mine, got)
    lse = top + jnp.log(jnp.exp(mine - top) + jnp.exp(got - top))
    attn = mine_ref[0:64] * jnp.exp(mine - lse) + got_ref[side_at, 0:64] * jnp.exp(got - lse)
    attn = attn.astype(BF16).astype(F32)
    lane = lax.broadcasted_iota(jnp.int32, (1, ring), 1)
    frame = start + jnp.where(lane < ring - width // 2, lane, lane - ring)
    inside = (frame >= 0) & (frame < frames) & ((lane < width + 32) | (lane >= ring - 32))
    live = inside & (frame < valid)
    masked = jnp.where(live, attn, 0.0)
    taps = taps_ref[...]
    depth = jnp.zeros((64, ring), F32)
    for t in range(KSIZE):
        depth = depth + taps[:, t : t + 1] * shifted(masked, t - RIM)
    gate = jax.nn.sigmoid(depth)
    swish = (depth[:, :width] * gate[:, :width]).astype(BF16)
    grad, side = lay_grads(shared_ref)
    mix = dot10(swish, grad)
    mix = jnp.concatenate([mix[:, at : at + width] for at in range(0, mix.shape[1], width)], axis=0).astype(BF16)
    fetch.wait()
    weight = weight_ref[...]
    partial = dot00(swish, weight)
    core = place_ref[5] == 0
    even = jnp.concatenate([partial[at : at + 8] for at in range(0, width, 16)], axis=0)
    odd = jnp.concatenate([partial[at + 8 : at + 16] for at in range(0, width, 16)], axis=0)
    keep_ref[...] = jnp.where(core, even, odd).astype(BF16)
    send_ref[...] = jnp.where(core, odd, even).astype(BF16)
    back = jnp.concatenate([dot11(weight, grad), dot11(weight, side)], axis=1)
    dgrad = back * gate * (1.0 + depth * (1.0 - gate))
    dgrad = jnp.where(inside, dgrad, 0.0).astype(BF16).astype(F32)
    row = lax.broadcasted_iota(jnp.int32, (64, width), 1)
    sums = jnp.zeros((64, width), F32)
    total = jnp.zeros((64, width), F32)
    for t in range(KSIZE):
        column = jnp.sum(shifted(masked, t - RIM)[:, :width] * dgrad[:, :width], axis=1, keepdims=True)
        sums = jnp.where(row == t, column, sums)
        total = total + taps[:, t : t + 1] * shifted(dgrad, RIM - t)[:, :width]
    turned = sums.T
    tap_grad = jnp.concatenate([turned[0:16, 0:64], turned[16:32, 0:64]], axis=1)
    grad_out = jnp.where(live[:, :width], total, 0.0).astype(BF16)
    delta = jnp.sum(grad_out.astype(F32) * attn[:, :width], axis=0, keepdims=True)
    a, b, c = split3(-lse[:, :width])
    d, e, f = split3(-delta)
    stats = rows_of(16, width, [(0, a), (1, b), (2, c), (3, d), (4, e), (5, f), (6, 1.0)])
    pack_ref[...] = jnp.concatenate([grad_out, stats.astype(BF16)], axis=0)
    row = lax.broadcasted_iota(jnp.int32, stats.shape, 0)
    share = copies_ref.shape[1] - 80
    for j in range(copies_ref.shape[0]):
        copies_ref[j, 0:64] = grad_out
        copies_ref[j, 64:80] = jnp.where(row == 7, tap_grad[j : j + 1], stats).astype(BF16)
        copies_ref[j, 80:] = mix[j * share : (j + 1) * share]


def backward(place_ref, all_ref, packs_ref, own_ref, pair_ref, pack_own_ref, pack_pair_ref, mine_ref, other_ref):
    blocks = all_ref.shape[0]
    base = place_ref[4] * blocks
    pair_base = blocks - base
    pair_bias = jnp.concatenate([bias_of(place_ref, place_ref[0], base), bias_of(place_ref, place_ref[0], pair_base)], axis=1)
    head = 64
    width = 128
    scale = head ** -0.5
    both = jnp.concatenate([own_ref[...], pair_ref[...]], axis=1)
    packs = jnp.concatenate([pack_own_ref[0:80], pack_pair_ref[0:80]], axis=1)
    query = (both[0:head].astype(F32) * scale).astype(BF16)
    query = jnp.concatenate([query, packs[head : head + 16]], axis=0)
    ones = [(0, 1.0), (1, 1.0), (2, 1.0)]
    key_rows = rows_of(16, 2 * width, ones + [(6, pair_bias)]).astype(BF16)
    key = jnp.concatenate([both[head : 2 * head], key_rows], axis=0)
    value_rows = rows_of(16, 2 * width, [(3, 1.0), (4, 1.0), (5, 1.0)]).astype(BF16)
    value = jnp.concatenate([both[2 * head : 3 * head], value_rows], axis=0)
    d_query = jnp.zeros((head, 2 * width), F32)
    d_key = jnp.zeros((head, 2 * width), F32)
    d_value = jnp.zeros((head, 2 * width), F32)
    for first in range(0, blocks, 2):
        keys, queries, grads, query_scores, key_scores, weights = [], [], [], [], [], []
        for b in (first, first + 1):
            key_b = all_ref[b, head : 2 * head]
            key_aug = jnp.concatenate([key_b, rows_of(16, width, ones + [(6, bias_of(place_ref, b, base))]).astype(BF16)], axis=0)
            value_aug = jnp.concatenate([all_ref[b, 2 * head : 3 * head], value_rows[:, :width]], axis=0)
            weight = jnp.exp(dot00(key_aug, query))
            query_scores.append((weight * dot00(value_aug, packs)).astype(BF16))
            keys.append(key_b)
            query_b = (all_ref[b, 0:head].astype(F32) * scale).astype(BF16)
            query_aug = jnp.concatenate([query_b, packs_ref[b, head : head + 16]], axis=0)
            weight = jnp.exp(dot00(query_aug, key))
            key_scores.append((weight * dot00(packs_ref[b, 0:80], value)).astype(BF16))
            weights.append(weight.astype(BF16))
            queries.append(query_b)
            grads.append(packs_ref[b, 0:head])
        d_query = d_query + dot10(jnp.concatenate(keys, axis=1), jnp.concatenate(query_scores, axis=0))
        d_key = d_key + dot10(jnp.concatenate(queries, axis=1), jnp.concatenate(key_scores, axis=0))
        d_value = d_value + dot10(jnp.concatenate(grads, axis=1), jnp.concatenate(weights, axis=0))
    d_query = d_query * scale
    for ref, at in ((mine_ref, 0), (other_ref, width)):
        kind = ref.dtype
        ref[0:head] = d_query[:, at : at + width].astype(kind)
        ref[head : 2 * head] = d_key[:, at : at + width].astype(kind)
        ref[2 * head : 3 * head] = d_value[:, at : at + width].astype(kind)


def finish(mine_ref, got_ref, query_ref, key_ref, value_ref):
    total = mine_ref[...] + got_ref[...].astype(F32)
    query_ref[...] = total[0:64].astype(BF16)
    key_ref[...] = total[64:128].astype(BF16)
    value_ref[...] = total[128:192].astype(BF16)


def add_pair(mine_ref, got_ref, out_ref):
    out_ref[...] = (mine_ref[...].astype(F32) + got_ref[...].astype(F32)).astype(BF16)


def mix_sum(packs_ref, out_ref):
    share = packs_ref.shape[1] - 80
    total = jnp.zeros((share, 128), F32)
    stats = jnp.zeros((16, 128), F32)
    for j in range(packs_ref.shape[0]):
        total = total + packs_ref[j, 80:].astype(F32)
        stats = stats + packs_ref[j, 64:80].astype(F32)
    out_ref[0:share] = total
    out_ref[share:] = rows_of(out_ref.shape[0] - share, 128, [(0, stats[7:8])])


def mix_spread(both_ref, out_ref):
    total = (both_ref[0] + both_ref[1]).astype(BF16)
    for j in range(out_ref.shape[0]):
        out_ref[j] = total


def mix_place(norm, share, parts_ref, out_ref, taps_ref):
    pieces = [parts_ref[z].astype(F32) * norm for z in range(parts_ref.shape[0])]
    full = jnp.concatenate([piece[0:share] for piece in pieces], axis=0)
    for at in range(out_ref.shape[1] // 128):
        out_ref[:, at * 128 : (at + 1) * 128] = full[at * 64 : (at + 1) * 64]
    tap = rows_of(len(pieces), 128, [(z, piece[share : share + 1]) for z, piece in enumerate(pieces)])
    taps_ref[0:16] = tap[:, 0:64]
    taps_ref[16:32] = tap[:, 64:128]


def sum_blocks(parts_ref, out_ref):
    total = jnp.zeros(out_ref.shape, F32)
    for j in range(parts_ref.shape[0]):
        total = total + parts_ref[j].astype(F32)
    out_ref[...] = total.astype(BF16)


def body(query_rows, key_rows, value_rows, valid_frames, depth_kernel, mix_weight, out_grad):
    width, head = query_rows.shape
    depth = lax.axis_size("z")
    ctx = ("yh", "z")
    tp = ("chip", "core")
    devices = 2 * depth
    lanes = lax.axis_size(tp)
    model = mix_weight.shape[1]
    rows8 = out_grad.shape[0]
    norm = (width * devices) ** -0.5
    valid = valid_frames[0]
    half = lax.axis_index("yh")
    spot = lax.axis_index("z")
    place = jnp.stack([spot, (half * depth + spot) * width, valid, jnp.int32(width * devices), half, lax.axis_index("core")]).astype(jnp.int32)
    swap = [(0, 1), (1, 0)]
    taps = depth_kernel.T
    rim_pairs = []
    sides = RIM // rows8
    for i in range(devices - 1):
        for k in range(sides):
            rim_pairs.append((i * lanes + lanes - sides + k, (i + 1) * lanes + k))
            rim_pairs.append(((i + 1) * lanes + k, i * lanes + lanes - sides + k))

    rim_rows = lax.ppermute(out_grad, ctx + tp, rim_pairs)
    own = jnp.concatenate([query_rows.T, key_rows.T, value_rows.T], axis=0)
    both = lax.all_gather(own, "yh", axis=0)
    rim_rows, both = lax.optimization_barrier((rim_rows, both))
    front, pair = call(
        first_pack,
        (jax.ShapeDtypeStruct((3 * head + 32, width), BF16), jax.ShapeDtypeStruct((3 * head, width), BF16)),
        2 ** 20,
        scalars=1,
    )(place, both)
    with_rim = jnp.concatenate([out_grad, rim_rows], axis=0)
    shared = lax.all_to_all(jnp.broadcast_to(with_rim[None], (lanes,) + with_rim.shape), tp, 0, 0, tiled=True)
    everyone = lax.all_gather(front, "z", axis=0)
    shared, everyone = lax.optimization_barrier((shared, everyone))

    part = jax.ShapeDtypeStruct((head + 8, 2 * width), F32)
    block = jax.ShapeDtypeStruct((head, width), BF16)
    mine, other = call(
        attend, (part, part), 2 ** 28, [pltpu.VMEM((depth, width, 3 * width), F32)], scalars=1
    )(place, everyone, own, pair)
    shared, other = lax.optimization_barrier((shared, other))
    got = lax.all_gather(other, "yh", axis=0)
    share = head * model // width // depth
    half_rows = jax.ShapeDtypeStruct((width // 2, model), BF16)
    keep, send, pack, copies = call(
        middle_part,
        (
            half_rows,
            half_rows,
            jax.ShapeDtypeStruct((80, width), BF16),
            jax.ShapeDtypeStruct((depth, 80 + share, width), BF16),
        ),
        2 ** 27,
        [pltpu.VMEM(mix_weight.shape, BF16), pltpu.SemaphoreType.DMA],
        scalars=1,
        remote=1,
    )(place, mix_weight, mine, got, taps, shared)
    packs = lax.all_to_all(copies, "z", 0, 0, tiled=True)
    keep_got = lax.ppermute(send, "core", swap)
    partial = call(add_pair, half_rows, 2 ** 20)(keep, keep_got)
    pack_pair = lax.ppermute(pack, "yh", swap)
    packs, pack_pair, partial = lax.optimization_barrier((packs, pack_pair, partial))

    mix_mine = call(mix_sum, jax.ShapeDtypeStruct((share + 16, width), F32), 2 ** 22)(packs)
    mix_both = lax.all_gather(mix_mine, "yh", axis=0)
    spread = call(mix_spread, jax.ShapeDtypeStruct((depth, share + 16, width), BF16), 2 ** 20)(mix_both)
    block_parts = lax.all_to_all(partial.reshape(lanes // 2, rows8, model), "chip", 0, 0, tiled=True)
    spread, block_parts = lax.optimization_barrier((spread, block_parts))
    pieces = lax.all_to_all(spread, "z", 0, 0, tiled=True)
    result = jax.ShapeDtypeStruct((3 * head, width), F32)
    sent = jax.ShapeDtypeStruct(result.shape, BF16)
    mine, other = call(backward, (result, sent), 2 ** 29, scalars=1)(
        place, everyone, packs, own, pair, pack, pack_pair
    )
    got = lax.ppermute(other, "yh", swap)
    d_query, d_key, d_value = call(finish, (block, block, block), 2 ** 20)(mine, got)

    block_out = call(sum_blocks, jax.ShapeDtypeStruct((rows8, model), BF16), 2 ** 20)(block_parts)
    mix_grad, tap_total = call(
        functools.partial(mix_place, norm, share),
        (jax.ShapeDtypeStruct((head, model), F32), jax.ShapeDtypeStruct((KSIZE, head), F32)),
        2 ** 20,
    )(pieces)
    return block_out, d_query.T, d_key.T, d_value.T, mix_grad, tap_total


def solution(mesh):
    count = mesh.shape["ctx"]
    fine = Mesh(mesh.devices.reshape(2, count // 2, mesh.shape["tp"] // 2, 2), ("yh", "z", "chip", "core"))
    ctx = ("yh", "z")
    tp = ("chip", "core")
    every = ctx + tp
    return jax.shard_map(
        body,
        mesh=fine,
        in_specs=(
            P(ctx, tp),
            P(ctx, tp),
            P(ctx, tp),
            P(),
            P(None, tp),
            P(tp, None),
            P(every, None),
        ),
        out_specs=(
            P(every, None),
            P(ctx, tp),
            P(ctx, tp),
            P(ctx, tp),
            P(tp, None),
            P(None, tp),
        ),
        check_vma=False,
    )
```

```python
import functools

import jax
import jax.numpy as jnp
from jax import lax
from jax.experimental import pallas as pl
from jax.experimental.pallas import tpu as pltpu
from jax.sharding import Mesh, PartitionSpec as P

F32 = jnp.float32
BF16 = jnp.bfloat16
KSIZE = 32
RIM = KSIZE // 2
LOW = -1e30
VMEM_BYTES = 48 * 1024 * 1024


def dot00(a, b):
    return lax.dot_general(a, b, (((0,), (0,)), ((), ())), preferred_element_type=F32)


def dot10(a, b):
    return lax.dot_general(a, b, (((1,), (0,)), ((), ())), preferred_element_type=F32)


def dot11(a, b):
    return lax.dot_general(a, b, (((1,), (1,)), ((), ())), preferred_element_type=F32)


def rows_of(count, lanes, entries):
    index = lax.broadcasted_iota(jnp.int32, (count, lanes), 0)
    out = jnp.zeros((count, lanes), F32)
    for where, value in entries:
        out = jnp.where(index == where, value, out)
    return out


def split3(x):
    high = x.astype(BF16).astype(F32)
    rest = x - high
    mid = rest.astype(BF16).astype(F32)
    return high, mid, rest - mid


def call(kernel, out_shapes, flops, scratch=(), scalars=0, remote=0):
    specs = {}
    if scalars:
        count = kernel.__code__.co_argcount - len(scratch) - len(jax.tree.leaves(out_shapes))
        spaces = [pltpu.SMEM] + [pl.ANY] * remote + [pltpu.VMEM] * (count - 1 - remote)
        specs["in_specs"] = [pl.BlockSpec(memory_space=space) for space in spaces]
    return pl.pallas_call(
        kernel,
        out_shape=out_shapes,
        **specs,
        scratch_shapes=list(scratch),
        compiler_params=pltpu.CompilerParams(vmem_limit_bytes=VMEM_BYTES),
        cost_estimate=pl.CostEstimate(flops=flops, bytes_accessed=2 ** 20, transcendentals=0),
    )


def side_of(low, high):
    lane = lax.broadcasted_iota(jnp.int32, low.shape, 1)
    return jnp.where(lane < low.shape[1] // 2, high, low)


def bias_of(place_ref, block, base):
    lane = lax.broadcasted_iota(jnp.int32, (1, 128), 1)
    return jnp.where((base + block) * 128 + lane < place_ref[2], 0.0, LOW)


def edges_of(packed):
    packed = packed.astype(F32)
    return jnp.concatenate([packed, pltpu.roll(packed, 64, 1)], axis=0)


def first_pack(place_ref, both_ref, pack_ref, pair_ref):
    own = both_ref[place_ref[4]]
    pair = both_ref[1 - place_ref[4]]
    query = pair[0:64].astype(F32)
    lane = lax.broadcasted_iota(jnp.int32, query.shape, 1)
    edge = jnp.where(lane < 32, query, pltpu.roll(query, 64, 1))
    edge = jnp.where(lane[0:32] < 64, edge[0:32], pltpu.roll(edge[32:64], 64, 1))
    pair_ref[...] = pair
    pack_ref[0:192] = own
    pack_ref[192:224] = edge.astype(BF16)


def lay_grads(shared_ref):
    rows = []
    for i in range(shared_ref.shape[0] // 2):
        even = shared_ref[2 * i].astype(F32)
        odd = shared_ref[2 * i + 1].astype(F32)
        rows.append(jnp.concatenate([even[0:8], odd[0:8]], axis=0).astype(BF16))
        rim = jnp.concatenate([even[8:16], odd[8:16]], axis=0).astype(BF16)
        if i == 0:
            low = rim
    gap = jnp.zeros((128 - 2 * RIM, shared_ref.shape[2]), BF16)
    return jnp.concatenate(rows, axis=0), jnp.concatenate([rim, gap, low], axis=0)


def attend(place_ref, all_ref, own_ref, pair_ref, mine_ref, other_ref, score_ref):
    blocks = all_ref.shape[0]
    head = 64
    width = 128
    lanes = 3 * width
    scale = head ** -0.5
    spot = place_ref[0]
    first = spot == 0
    spot_rows = place_ref[4] * blocks
    last = spot == blocks - 1
    before = lax.rem(spot + blocks - 1, blocks)
    after = lax.rem(spot + 1, blocks)
    low_here = all_ref[before, 0:head].astype(F32)
    high_here = all_ref[after, 0:head].astype(F32)
    low_there = pltpu.roll(edges_of(all_ref[before, 3 * head : 3 * head + 32]), width // 2, 1)
    high_there = edges_of(all_ref[after, 3 * head : 3 * head + 32])
    side_own = side_of(jnp.where(first, low_there, low_here), jnp.where(last, high_there, high_here))
    side_pair = side_of(jnp.where(first, low_here, low_there), jnp.where(last, high_here, high_there))
    lane = lax.broadcasted_iota(jnp.int32, (head, width), 1)
    middle = (lane >= 32) & (lane < 96)
    edges = jnp.where(middle, pltpu.roll(side_pair, width // 2, 1), side_own)
    query = jnp.concatenate([own_ref[0:head].astype(F32), pair_ref[0:head].astype(F32), edges], axis=1) * scale
    query = jnp.concatenate([query, rows_of(16, lanes, [(6, 1.0)])], axis=0).astype(BF16)
    peak = jnp.full((1, lanes), LOW, F32)
    for b in range(blocks):
        key = jnp.concatenate(
            [all_ref[b, head : 2 * head], rows_of(16, width, [(6, bias_of(place_ref, b, spot_rows))]).astype(BF16)], axis=0
        )
        score = dot00(key, query)
        score_ref[b] = score
        peak = jnp.maximum(peak, jnp.max(score, axis=0, keepdims=True))
    total = jnp.zeros((1, lanes), F32)
    out = jnp.zeros((head, lanes), F32)
    for b in range(0, blocks, 2):
        pair_weight = []
        for k in (b, b + 1):
            weight = jnp.exp(score_ref[k] - peak)
            total = total + jnp.sum(weight, axis=0, keepdims=True)
            pair_weight.append(weight.astype(BF16))
        values = jnp.concatenate([all_ref[b, 2 * head : 3 * head], all_ref[b + 1, 2 * head : 3 * head]], axis=1)
        out = out + dot10(values, jnp.concatenate(pair_weight, axis=0))
    out = out / total
    lse = peak + jnp.log(total)
    both = jnp.concatenate([out, jnp.broadcast_to(lse, (8, lanes))], axis=0)
    edges = both[:, 2 * width :]
    mine_ref[:, 0:width] = both[:, 0:width]
    mine_ref[:, width:] = edges
    other_ref[:, 0:width] = both[:, width : 2 * width]
    other_ref[:, width:] = pltpu.roll(edges, width // 2, 1)


def shifted(ring, offset):
    if offset == 0:
        return ring
    return pltpu.roll(ring, (-offset) % ring.shape[1], 1)


def middle_part(place_ref, weight_hbm, mine_ref, got_ref, taps_ref, shared_ref, keep_ref, send_ref, pack_ref, copies_ref, weight_ref, sem):
    fetch = pltpu.make_async_copy(weight_hbm, weight_ref, sem)
    fetch.start()
    width = 128
    ring = 2 * width
    start = place_ref[1]
    valid = place_ref[2]
    frames = place_ref[3]
    mine = mine_ref[64:65]
    side_at = 1 - place_ref[4]
    got = got_ref[side_at, 64:65]
    top = jnp.maximum(mine, got)
    lse = top + jnp.log(jnp.exp(mine - top) + jnp.exp(got - top))
    attn = mine_ref[0:64] * jnp.exp(mine - lse) + got_ref[side_at, 0:64] * jnp.exp(got - lse)
    attn = attn.astype(BF16).astype(F32)
    lane = lax.broadcasted_iota(jnp.int32, (1, ring), 1)
    frame = start + jnp.where(lane < ring - width // 2, lane, lane - ring)
    inside = (frame >= 0) & (frame < frames) & ((lane < width + 32) | (lane >= ring - 32))
    live = inside & (frame < valid)
    masked = jnp.where(live, attn, 0.0)
    taps = taps_ref[...]
    depth = jnp.zeros((64, ring), F32)
    for t in range(KSIZE):
        depth = depth + taps[:, t : t + 1] * shifted(masked, t - RIM)
    gate = jax.nn.sigmoid(depth)
    swish = (depth[:, :width] * gate[:, :width]).astype(BF16)
    grad, side = lay_grads(shared_ref)
    mix = dot10(swish, grad)
    mix = jnp.concatenate([mix[:, at : at + width] for at in range(0, mix.shape[1], width)], axis=0).astype(BF16)
    fetch.wait()
    weight = weight_ref[...]
    partial = dot00(swish, weight)
    core = place_ref[5] == 0
    even = jnp.concatenate([partial[at : at + 8] for at in range(0, width, 16)], axis=0)
    odd = jnp.concatenate([partial[at + 8 : at + 16] for at in range(0, width, 16)], axis=0)
    keep_ref[...] = jnp.where(core, even, odd).astype(BF16)
    send_ref[...] = jnp.where(core, odd, even).astype(BF16)
    back = jnp.concatenate([dot11(weight, grad), dot11(weight, side)], axis=1)
    dgrad = back * gate * (1.0 + depth * (1.0 - gate))
    dgrad = jnp.where(inside, dgrad, 0.0).astype(BF16).astype(F32)
    row = lax.broadcasted_iota(jnp.int32, (64, width), 1)
    sums = jnp.zeros((64, width), F32)
    total = jnp.zeros((64, width), F32)
    for t in range(KSIZE):
        column = jnp.sum(shifted(masked, t - RIM)[:, :width] * dgrad[:, :width], axis=1, keepdims=True)
        sums = jnp.where(row == t, column, sums)
        total = total + taps[:, t : t + 1] * shifted(dgrad, RIM - t)[:, :width]
    turned = sums.T
    tap_grad = jnp.concatenate([turned[0:16, 0:64], turned[16:32, 0:64]], axis=1)
    grad_out = jnp.where(live[:, :width], total, 0.0).astype(BF16)
    delta = jnp.sum(grad_out.astype(F32) * attn[:, :width], axis=0, keepdims=True)
    a, b, c = split3(-lse[:, :width])
    d, e, f = split3(-delta)
    stats = rows_of(16, width, [(0, a), (1, b), (2, c), (3, d), (4, e), (5, f), (6, 1.0)])
    pack_ref[...] = jnp.concatenate([grad_out, stats.astype(BF16)], axis=0)
    row = lax.broadcasted_iota(jnp.int32, stats.shape, 0)
    share = copies_ref.shape[1] - 72
    for j in range(copies_ref.shape[0]):
        copies_ref[j, 0:64] = grad_out
        rest = jnp.where(row == 7, tap_grad[j : j + 1], stats)[0:8]
        rest = jnp.concatenate([rest, mix[j * share : (j + 1) * share].astype(F32)], axis=0)
        copies_ref[j, 64:] = rest.astype(BF16)


ONES = [(0, 1.0), (1, 1.0), (2, 1.0)]
DELTAS = [(3, 1.0), (4, 1.0), (5, 1.0)]


def query_back(place_ref, all_ref, own_ref, pair_ref, pack_own_ref, pack_pair_ref, out_ref):
    blocks = all_ref.shape[0]
    base = place_ref[4] * blocks
    head = 64
    width = 128
    scale = head ** -0.5
    query = jnp.concatenate([own_ref[0:head], pair_ref[0:head]], axis=1)
    packs = jnp.concatenate([pack_own_ref[...], pack_pair_ref[...]], axis=1)
    query = (query.astype(F32) * scale).astype(BF16)
    query = jnp.concatenate([query, packs[head : head + 16]], axis=0)
    value_rows = rows_of(16, width, DELTAS).astype(BF16)
    total = jnp.zeros((head, 2 * width), F32)
    for first in range(0, blocks, 2):
        keys, scores = [], []
        for b in (first, first + 1):
            key_b = all_ref[b, head : 2 * head]
            key_rows = rows_of(16, width, ONES + [(6, bias_of(place_ref, b, base))]).astype(BF16)
            value_aug = jnp.concatenate([all_ref[b, 2 * head : 3 * head], value_rows], axis=0)
            weight = jnp.exp(dot00(jnp.concatenate([key_b, key_rows], axis=0), query))
            scores.append((weight * dot00(value_aug, packs)).astype(BF16))
            keys.append(key_b)
        total = total + dot10(jnp.concatenate(keys, axis=1), jnp.concatenate(scores, axis=0))
    out_ref[...] = total * scale


def backward(place_ref, all_ref, packs_ref, own_ref, pair_ref, d_query_ref, mine_ref, other_ref):
    blocks = all_ref.shape[0]
    base = place_ref[4] * blocks
    pair_base = blocks - base
    pair_bias = jnp.concatenate([bias_of(place_ref, place_ref[0], base), bias_of(place_ref, place_ref[0], pair_base)], axis=1)
    head = 64
    width = 128
    scale = head ** -0.5
    both = jnp.concatenate([own_ref[head:], pair_ref[head:]], axis=1)
    more = packs_ref.shape[1] - head
    key_rows = rows_of(more, 2 * width, ONES + [(6, pair_bias)]).astype(BF16)
    key = jnp.concatenate([both[0:head], key_rows], axis=0)
    value = jnp.concatenate([both[head:], rows_of(more, 2 * width, DELTAS).astype(BF16)], axis=0)
    d_key = jnp.zeros((head, 2 * width), F32)
    d_value = jnp.zeros((head, 2 * width), F32)
    for first in range(0, blocks, 2):
        queries, grads, scores, weights = [], [], [], []
        for b in (first, first + 1):
            query_b = (all_ref[b, 0:head].astype(F32) * scale).astype(BF16)
            query_aug = jnp.concatenate([query_b, packs_ref[b, head:]], axis=0)
            weight = jnp.exp(dot00(query_aug, key))
            scores.append((weight * dot00(packs_ref[b], value)).astype(BF16))
            weights.append(weight.astype(BF16))
            queries.append(query_b)
            grads.append(packs_ref[b, 0:head])
        d_key = d_key + dot10(jnp.concatenate(queries, axis=1), jnp.concatenate(scores, axis=0))
        d_value = d_value + dot10(jnp.concatenate(grads, axis=1), jnp.concatenate(weights, axis=0))
    for ref, at in ((mine_ref, 0), (other_ref, width)):
        kind = ref.dtype
        ref[0:head] = d_query_ref[:, at : at + width].astype(kind)
        ref[head : 2 * head] = d_key[:, at : at + width].astype(kind)
        ref[2 * head : 3 * head] = d_value[:, at : at + width].astype(kind)


def finish(place_ref, mine_ref, got_ref, query_ref, key_ref, value_ref):
    total = mine_ref[...] + got_ref[1 - place_ref[4]].astype(F32)
    query_ref[...] = total[0:64].astype(BF16)
    key_ref[...] = total[64:128].astype(BF16)
    value_ref[...] = total[128:192].astype(BF16)


def add_pair(mine_ref, got_ref, out_ref):
    out_ref[...] = (mine_ref[...].astype(F32) + got_ref[...].astype(F32)).astype(BF16)


def mix_sum(packs_ref, out_ref):
    share = packs_ref.shape[1] - 72
    total = jnp.zeros((share + 8, 128), F32)
    for j in range(packs_ref.shape[0]):
        total = total + packs_ref[j, 64:].astype(F32)
    out_ref[0:share] = total[8:]
    out_ref[share:] = rows_of(out_ref.shape[0] - share, 128, [(0, total[7:8])])


def mix_spread(both_ref, out_ref):
    total = (both_ref[0] + both_ref[1]).astype(BF16)
    for j in range(out_ref.shape[0]):
        out_ref[j] = total


def mix_place(norm, share, parts_ref, out_ref, taps_ref):
    pieces = [parts_ref[z].astype(F32) * norm for z in range(parts_ref.shape[0])]
    full = jnp.concatenate([piece[0:share] for piece in pieces], axis=0)
    for at in range(out_ref.shape[1] // 128):
        out_ref[:, at * 128 : (at + 1) * 128] = full[at * 64 : (at + 1) * 64]
    tap = rows_of(len(pieces), 128, [(z, piece[share : share + 1]) for z, piece in enumerate(pieces)])
    taps_ref[0:16] = tap[:, 0:64]
    taps_ref[16:32] = tap[:, 64:128]


def sum_blocks(parts_ref, out_ref):
    total = jnp.zeros(out_ref.shape, F32)
    for j in range(parts_ref.shape[0]):
        total = total + parts_ref[j].astype(F32)
    out_ref[...] = total.astype(BF16)


def body(query_rows, key_rows, value_rows, valid_frames, depth_kernel, mix_weight, out_grad):
    width, head = query_rows.shape
    depth = lax.axis_size("z")
    ctx = ("yh", "z")
    tp = ("chip", "core")
    devices = 2 * depth
    lanes = lax.axis_size(tp)
    model = mix_weight.shape[1]
    rows8 = out_grad.shape[0]
    norm = (width * devices) ** -0.5
    valid = valid_frames[0]
    half = lax.axis_index("yh")
    spot = lax.axis_index("z")
    place = jnp.stack([spot, (half * depth + spot) * width, valid, jnp.int32(width * devices), half, lax.axis_index("core")]).astype(jnp.int32)
    swap = [(0, 1), (1, 0)]
    taps = depth_kernel.T
    rim_pairs = []
    sides = RIM // rows8
    for i in range(devices - 1):
        for k in range(sides):
            rim_pairs.append((i * lanes + lanes - sides + k, (i + 1) * lanes + k))
            rim_pairs.append(((i + 1) * lanes + k, i * lanes + lanes - sides + k))

    rim_rows = lax.ppermute(out_grad, ctx + tp, rim_pairs)
    own = jnp.concatenate([query_rows.T, key_rows.T, value_rows.T], axis=0)
    both = lax.all_gather(own, "yh", axis=0)
    rim_rows, both = lax.optimization_barrier((rim_rows, both))
    front, pair = call(
        first_pack,
        (jax.ShapeDtypeStruct((3 * head + 32, width), BF16), jax.ShapeDtypeStruct((3 * head, width), BF16)),
        2 ** 20,
        scalars=1,
    )(place, both)
    with_rim = jnp.concatenate([out_grad, rim_rows], axis=0)
    shared = lax.all_to_all(jnp.broadcast_to(with_rim[None], (lanes,) + with_rim.shape), tp, 0, 0, tiled=True)
    everyone = lax.all_gather(front, "z", axis=0)
    shared, everyone = lax.optimization_barrier((shared, everyone))

    part = jax.ShapeDtypeStruct((head + 8, 2 * width), F32)
    block = jax.ShapeDtypeStruct((head, width), BF16)
    mine, other = call(
        attend, (part, part), 2 ** 28, [pltpu.VMEM((depth, width, 3 * width), F32)], scalars=1
    )(place, everyone, own, pair)
    shared, other = lax.optimization_barrier((shared, other))
    got = lax.all_gather(other, "yh", axis=0)
    share = head * model // width // depth
    half_rows = jax.ShapeDtypeStruct((width // 2, model), BF16)
    keep, send, pack, copies = call(
        middle_part,
        (
            half_rows,
            half_rows,
            jax.ShapeDtypeStruct((80, width), BF16),
            jax.ShapeDtypeStruct((depth, 72 + share, width), BF16),
        ),
        2 ** 27,
        [pltpu.VMEM(mix_weight.shape, BF16), pltpu.SemaphoreType.DMA],
        scalars=1,
        remote=1,
    )(place, mix_weight, mine, got, taps, shared)
    packs = lax.all_to_all(copies, "z", 0, 0, tiled=True)
    keep_got = lax.ppermute(send, "core", swap)
    partial = call(add_pair, half_rows, 2 ** 20)(keep, keep_got)
    pack_pair = lax.ppermute(pack, "yh", swap)
    d_query = call(query_back, jax.ShapeDtypeStruct((head, 2 * width), F32), 2 ** 28, scalars=1)(
        place, everyone, own, pair, pack, pack_pair
    )
    packs, d_query, partial = lax.optimization_barrier((packs, d_query, partial))

    mix_mine = call(mix_sum, jax.ShapeDtypeStruct((share + 8, width), F32), 2 ** 22)(packs)
    mix_both = lax.all_gather(mix_mine, "yh", axis=0)
    spread = call(mix_spread, jax.ShapeDtypeStruct((depth, share + 8, width), BF16), 2 ** 20)(mix_both)
    block_parts = lax.all_to_all(partial.reshape(lanes // 2, rows8, model), "chip", 0, 0, tiled=True)
    spread, block_parts = lax.optimization_barrier((spread, block_parts))
    pieces = lax.all_to_all(spread, "z", 0, 0, tiled=True)
    result = jax.ShapeDtypeStruct((3 * head, width), F32)
    sent = jax.ShapeDtypeStruct(result.shape, BF16)
    mine, other = call(backward, (result, sent), 2 ** 29, scalars=1)(
        place, everyone, packs, own, pair, d_query
    )
    got = lax.all_gather(other, "yh", axis=0)
    d_query, d_key, d_value = call(finish, (block, block, block), 2 ** 20, scalars=1)(place, mine, got)

    block_out = call(sum_blocks, jax.ShapeDtypeStruct((rows8, model), BF16), 2 ** 20)(block_parts)
    mix_grad, tap_total = call(
        functools.partial(mix_place, norm, share),
        (jax.ShapeDtypeStruct((head, model), F32), jax.ShapeDtypeStruct((KSIZE, head), F32)),
        2 ** 20,
    )(pieces)
    return block_out, d_query.T, d_key.T, d_value.T, mix_grad, tap_total


def solution(mesh):
    count = mesh.shape["ctx"]
    fine = Mesh(mesh.devices.reshape(2, count // 2, mesh.shape["tp"] // 2, 2), ("yh", "z", "chip", "core"))
    ctx = ("yh", "z")
    tp = ("chip", "core")
    every = ctx + tp
    return jax.shard_map(
        body,
        mesh=fine,
        in_specs=(
            P(ctx, tp),
            P(ctx, tp),
            P(ctx, tp),
            P(),
            P(None, tp),
            P(tp, None),
            P(every, None),
        ),
        out_specs=(
            P(every, None),
            P(ctx, tp),
            P(ctx, tp),
            P(ctx, tp),
            P(tp, None),
            P(None, tp),
        ),
        check_vma=False,
    )
```

```python
import functools

import jax
import jax.numpy as jnp
from jax import lax
from jax.experimental import pallas as pl
from jax.experimental.pallas import tpu as pltpu
from jax.sharding import Mesh, PartitionSpec as P

F32 = jnp.float32
BF16 = jnp.bfloat16
KSIZE = 32
RIM = KSIZE // 2
LOW = -1e30
VMEM_BYTES = 48 * 1024 * 1024


def dot00(a, b):
    return lax.dot_general(a, b, (((0,), (0,)), ((), ())), preferred_element_type=F32)


def dot10(a, b):
    return lax.dot_general(a, b, (((1,), (0,)), ((), ())), preferred_element_type=F32)


def dot11(a, b):
    return lax.dot_general(a, b, (((1,), (1,)), ((), ())), preferred_element_type=F32)


def rows_of(count, lanes, entries):
    index = lax.broadcasted_iota(jnp.int32, (count, lanes), 0)
    out = jnp.zeros((count, lanes), F32)
    for where, value in entries:
        out = jnp.where(index == where, value, out)
    return out


def split3(x):
    high = x.astype(BF16).astype(F32)
    rest = x - high
    mid = rest.astype(BF16).astype(F32)
    return high, mid, rest - mid


def call(kernel, out_shapes, flops, scratch=(), scalars=0, remote=0):
    specs = {}
    if scalars:
        count = kernel.__code__.co_argcount - len(scratch) - len(jax.tree.leaves(out_shapes))
        spaces = [pltpu.SMEM] + [pl.ANY] * remote + [pltpu.VMEM] * (count - 1 - remote)
        specs["in_specs"] = [pl.BlockSpec(memory_space=space) for space in spaces]
    return pl.pallas_call(
        kernel,
        out_shape=out_shapes,
        **specs,
        scratch_shapes=list(scratch),
        compiler_params=pltpu.CompilerParams(vmem_limit_bytes=VMEM_BYTES),
        cost_estimate=pl.CostEstimate(flops=flops, bytes_accessed=2 ** 20, transcendentals=0),
    )


def side_of(low, high):
    lane = lax.broadcasted_iota(jnp.int32, low.shape, 1)
    return jnp.where(lane < low.shape[1] // 2, high, low)


def bias_of(place_ref, block, base):
    lane = lax.broadcasted_iota(jnp.int32, (1, 128), 1)
    return jnp.where((base + block) * 128 + lane < place_ref[2], 0.0, LOW)


def edges_of(packed):
    packed = packed.astype(F32)
    return jnp.concatenate([packed, pltpu.roll(packed, 64, 1)], axis=0)


def first_pack(place_ref, both_ref, pack_ref, pair_ref):
    own = both_ref[place_ref[4]]
    pair = both_ref[1 - place_ref[4]]
    query = pair[0:64].astype(F32)
    lane = lax.broadcasted_iota(jnp.int32, query.shape, 1)
    edge = jnp.where(lane < 32, query, pltpu.roll(query, 64, 1))
    edge = jnp.where(lane[0:32] < 64, edge[0:32], pltpu.roll(edge[32:64], 64, 1))
    pair_ref[...] = pair
    pack_ref[0:192] = own
    pack_ref[192:224] = edge.astype(BF16)


def lay_grads(shared_ref):
    rows = []
    for i in range(shared_ref.shape[0] // 2):
        even = shared_ref[2 * i].astype(F32)
        odd = shared_ref[2 * i + 1].astype(F32)
        rows.append(jnp.concatenate([even[0:8], odd[0:8]], axis=0).astype(BF16))
        rim = jnp.concatenate([even[8:16], odd[8:16]], axis=0).astype(BF16)
        if i == 0:
            low = rim
    return jnp.concatenate([low] + rows + [rim], axis=0)


def attend(place_ref, all_ref, own_ref, pair_ref, mine_ref, other_ref, score_ref):
    blocks = all_ref.shape[0]
    head = 64
    width = 128
    lanes = 3 * width
    scale = head ** -0.5
    spot = place_ref[0]
    first = spot == 0
    spot_rows = place_ref[4] * blocks
    last = spot == blocks - 1
    before = lax.rem(spot + blocks - 1, blocks)
    after = lax.rem(spot + 1, blocks)
    low_here = all_ref[before, 0:head].astype(F32)
    high_here = all_ref[after, 0:head].astype(F32)
    low_there = pltpu.roll(edges_of(all_ref[before, 3 * head : 3 * head + 32]), width // 2, 1)
    high_there = edges_of(all_ref[after, 3 * head : 3 * head + 32])
    side_own = side_of(jnp.where(first, low_there, low_here), jnp.where(last, high_there, high_here))
    side_pair = side_of(jnp.where(first, low_here, low_there), jnp.where(last, high_here, high_there))
    lane = lax.broadcasted_iota(jnp.int32, (head, width), 1)
    middle = (lane >= 32) & (lane < 96)
    edges = jnp.where(middle, pltpu.roll(side_pair, width // 2, 1), side_own)
    query = jnp.concatenate([own_ref[0:head].astype(F32), pair_ref[0:head].astype(F32), edges], axis=1) * scale
    query = jnp.concatenate([query, rows_of(16, lanes, [(6, 1.0)])], axis=0).astype(BF16)
    peak = jnp.full((1, lanes), LOW, F32)
    for b in range(blocks):
        key = jnp.concatenate(
            [all_ref[b, head : 2 * head], rows_of(16, width, [(6, bias_of(place_ref, b, spot_rows))]).astype(BF16)], axis=0
        )
        score = dot00(key, query)
        score_ref[b] = score
        peak = jnp.maximum(peak, jnp.max(score, axis=0, keepdims=True))
    total = jnp.zeros((1, lanes), F32)
    out = jnp.zeros((head, lanes), F32)
    for b in range(0, blocks, 2):
        pair_weight = []
        for k in (b, b + 1):
            weight = jnp.exp(score_ref[k] - peak)
            total = total + jnp.sum(weight, axis=0, keepdims=True)
            pair_weight.append(weight.astype(BF16))
        values = jnp.concatenate([all_ref[b, 2 * head : 3 * head], all_ref[b + 1, 2 * head : 3 * head]], axis=1)
        out = out + dot10(values, jnp.concatenate(pair_weight, axis=0))
    out = out / total
    lse = peak + jnp.log(total)
    both = jnp.concatenate([out, jnp.broadcast_to(lse, (8, lanes))], axis=0)
    edges = both[:, 2 * width :]
    mine_ref[:, 0:width] = both[:, 0:width]
    mine_ref[:, width:] = edges
    other_ref[:, 0:width] = both[:, width : 2 * width]
    other_ref[:, width:] = pltpu.roll(edges, width // 2, 1)


def middle_part(place_ref, weight_hbm, mine_ref, got_ref, taps_ref, shared_ref, keep_ref, send_ref, pack_ref, copies_ref, weight_ref, sem, wide_ref, back_ref):
    fetch = pltpu.make_async_copy(weight_hbm, weight_ref, sem)
    fetch.start()
    width = 128
    head = 64
    ring = 2 * width
    half = KSIZE // 2
    reach = width + 2 * RIM
    start = place_ref[1]
    valid = place_ref[2]
    frames = place_ref[3]
    mine = mine_ref[64:65]
    side_at = 1 - place_ref[4]
    got = got_ref[side_at, 64:65]
    top = jnp.maximum(mine, got)
    lse = top + jnp.log(jnp.exp(mine - top) + jnp.exp(got - top))
    attn = mine_ref[0:64] * jnp.exp(mine - lse) + got_ref[side_at, 0:64] * jnp.exp(got - lse)
    attn = attn.astype(BF16).astype(F32)
    lane = lax.broadcasted_iota(jnp.int32, (1, ring), 1)
    frame = start + jnp.where(lane < ring - width // 2, lane, lane - ring)
    masked = jnp.where((frame >= 0) & (frame < frames) & (frame < valid), attn, 0.0)
    own_rows = masked[:, 0:width].T
    side_rows = masked[:, width:ring].T
    rows = jnp.concatenate([side_rows[96:128], own_rows, side_rows[0:32]], axis=0)
    wide_ref[...] = jnp.concatenate([rows[0 : reach + half], rows[half : reach + KSIZE]], axis=1)
    taps = jnp.concatenate([taps_ref[0:half], taps_ref[half:KSIZE]], axis=1)
    depth = jnp.zeros((reach, width), F32)
    for t in range(half):
        depth = depth + taps[t : t + 1] * wide_ref[t : t + reach]
    depth = depth[:, 0:head] + depth[:, head:width]
    gate = jax.nn.sigmoid(depth)
    swish = (depth * gate)[RIM : RIM + width].astype(BF16)
    grad = lay_grads(shared_ref)
    mix = dot00(swish, grad[RIM : RIM + width])
    mix = jnp.concatenate([mix[:, at : at + width] for at in range(0, mix.shape[1], width)], axis=0)
    fetch.wait()
    weight = weight_ref[...]
    partial = dot10(swish, weight)
    core = place_ref[5] == 0
    even = jnp.concatenate([partial[at : at + 8] for at in range(0, width, 16)], axis=0)
    odd = jnp.concatenate([partial[at + 8 : at + 16] for at in range(0, width, 16)], axis=0)
    keep_ref[...] = jnp.where(core, even, odd).astype(BF16)
    send_ref[...] = jnp.where(core, odd, even).astype(BF16)
    dgrad = dot11(grad, weight) * gate * (1.0 + depth * (1.0 - gate))
    row = start - RIM + lax.broadcasted_iota(jnp.int32, (reach, head), 0)
    dgrad = jnp.where((row >= 0) & (row < frames), dgrad, 0.0).astype(BF16).astype(F32)
    back_ref[...] = jnp.concatenate([dgrad[half:reach], dgrad[0 : reach - half]], axis=1)
    inner = dgrad[RIM : RIM + width]
    inner = jnp.concatenate([inner, inner], axis=1)
    total = jnp.zeros((width, width), F32)
    tap_rows = []
    for t in range(half):
        total = total + taps[t : t + 1] * back_ref[half - t : half - t + width]
        tap_rows.append((t, jnp.sum(wide_ref[RIM + t : RIM + t + width] * inner, axis=0, keepdims=True)))
    tap_grad = rows_of(half, width, tap_rows)
    total = total[:, 0:head] + total[:, head:width]
    row = start + lax.broadcasted_iota(jnp.int32, (width, head), 0)
    grad_out = jnp.where(row < valid, total, 0.0).T.astype(BF16)
    delta = jnp.sum(grad_out.astype(F32) * attn[:, :width], axis=0, keepdims=True)
    a, b, c = split3(-lse[:, :width])
    d, e, f = split3(-delta)
    stats = rows_of(16, width, [(0, a), (1, b), (2, c), (3, d), (4, e), (5, f), (6, 1.0)])
    pack_ref[...] = jnp.concatenate([grad_out, stats.astype(BF16)], axis=0)
    row = lax.broadcasted_iota(jnp.int32, (8, width), 0)
    share = copies_ref.shape[1] - 72
    for j in range(copies_ref.shape[0]):
        copies_ref[j, 0:64] = grad_out
        rest = jnp.where(row == 7, tap_grad[j : j + 1], stats[0:8])
        rest = jnp.concatenate([rest, mix[j * share : (j + 1) * share]], axis=0)
        copies_ref[j, 64:] = rest.astype(BF16)


ONES = [(0, 1.0), (1, 1.0), (2, 1.0)]
DELTAS = [(3, 1.0), (4, 1.0), (5, 1.0)]


def query_back(place_ref, all_ref, own_ref, pair_ref, pack_own_ref, pack_pair_ref, out_ref):
    blocks = all_ref.shape[0]
    base = place_ref[4] * blocks
    head = 64
    width = 128
    scale = head ** -0.5
    query = jnp.concatenate([own_ref[0:head], pair_ref[0:head]], axis=1)
    packs = jnp.concatenate([pack_own_ref[...], pack_pair_ref[...]], axis=1)
    query = (query.astype(F32) * scale).astype(BF16)
    query = jnp.concatenate([query, packs[head : head + 16]], axis=0)
    value_rows = rows_of(16, width, DELTAS).astype(BF16)
    total = jnp.zeros((head, 2 * width), F32)
    for first in range(0, blocks, 2):
        keys, scores = [], []
        for b in (first, first + 1):
            key_b = all_ref[b, head : 2 * head]
            key_rows = rows_of(16, width, ONES + [(6, bias_of(place_ref, b, base))]).astype(BF16)
            value_aug = jnp.concatenate([all_ref[b, 2 * head : 3 * head], value_rows], axis=0)
            weight = jnp.exp(dot00(jnp.concatenate([key_b, key_rows], axis=0), query))
            scores.append((weight * dot00(value_aug, packs)).astype(BF16))
            keys.append(key_b)
        total = total + dot10(jnp.concatenate(keys, axis=1), jnp.concatenate(scores, axis=0))
    out_ref[...] = total * scale


def backward(place_ref, all_ref, packs_ref, own_ref, pair_ref, d_query_ref, mine_ref, other_ref):
    blocks = all_ref.shape[0]
    base = place_ref[4] * blocks
    pair_base = blocks - base
    pair_bias = jnp.concatenate([bias_of(place_ref, place_ref[0], base), bias_of(place_ref, place_ref[0], pair_base)], axis=1)
    head = 64
    width = 128
    scale = head ** -0.5
    both = jnp.concatenate([own_ref[head:], pair_ref[head:]], axis=1)
    more = packs_ref.shape[1] - head
    key_rows = rows_of(more, 2 * width, ONES + [(6, pair_bias)]).astype(BF16)
    key = jnp.concatenate([both[0:head], key_rows], axis=0)
    value = jnp.concatenate([both[head:], rows_of(more, 2 * width, DELTAS).astype(BF16)], axis=0)
    d_key = jnp.zeros((head, 2 * width), F32)
    d_value = jnp.zeros((head, 2 * width), F32)
    for first in range(0, blocks, 2):
        queries, grads, scores, weights = [], [], [], []
        for b in (first, first + 1):
            query_b = (all_ref[b, 0:head].astype(F32) * scale).astype(BF16)
            query_aug = jnp.concatenate([query_b, packs_ref[b, head:]], axis=0)
            weight = jnp.exp(dot00(query_aug, key))
            scores.append((weight * dot00(packs_ref[b], value)).astype(BF16))
            weights.append(weight.astype(BF16))
            queries.append(query_b)
            grads.append(packs_ref[b, 0:head])
        d_key = d_key + dot10(jnp.concatenate(queries, axis=1), jnp.concatenate(scores, axis=0))
        d_value = d_value + dot10(jnp.concatenate(grads, axis=1), jnp.concatenate(weights, axis=0))
    for ref, at in ((mine_ref, 0), (other_ref, width)):
        kind = ref.dtype
        ref[0:head] = d_query_ref[:, at : at + width].astype(kind)
        ref[head : 2 * head] = d_key[:, at : at + width].astype(kind)
        ref[2 * head : 3 * head] = d_value[:, at : at + width].astype(kind)


def finish(place_ref, mine_ref, got_ref, query_ref, key_ref, value_ref):
    total = mine_ref[...] + got_ref[1 - place_ref[4]].astype(F32)
    query_ref[...] = total[0:64].astype(BF16)
    key_ref[...] = total[64:128].astype(BF16)
    value_ref[...] = total[128:192].astype(BF16)


def add_pair(mine_ref, got_ref, out_ref):
    out_ref[...] = (mine_ref[...].astype(F32) + got_ref[...].astype(F32)).astype(BF16)


def mix_sum(packs_ref, out_ref):
    share = packs_ref.shape[1] - 72
    total = jnp.zeros((share + 8, 128), F32)
    for j in range(packs_ref.shape[0]):
        total = total + packs_ref[j, 64:].astype(F32)
    out_ref[0:share] = total[8:]
    out_ref[share:] = rows_of(out_ref.shape[0] - share, 128, [(0, total[7:8])])


def mix_spread(both_ref, out_ref):
    total = (both_ref[0] + both_ref[1]).astype(BF16)
    for j in range(out_ref.shape[0]):
        out_ref[j] = total


def mix_place(norm, share, parts_ref, out_ref, taps_ref):
    pieces = [parts_ref[z].astype(F32) * norm for z in range(parts_ref.shape[0])]
    full = jnp.concatenate([piece[0:share] for piece in pieces], axis=0)
    for at in range(out_ref.shape[1] // 128):
        out_ref[:, at * 128 : (at + 1) * 128] = full[at * 64 : (at + 1) * 64]
    tap = rows_of(len(pieces), 128, [(z, piece[share : share + 1]) for z, piece in enumerate(pieces)])
    taps_ref[0:16] = tap[:, 0:64]
    taps_ref[16:32] = tap[:, 64:128]


def sum_blocks(parts_ref, out_ref):
    total = jnp.zeros(out_ref.shape, F32)
    for j in range(parts_ref.shape[0]):
        total = total + parts_ref[j].astype(F32)
    out_ref[...] = total.astype(BF16)


def body(query_rows, key_rows, value_rows, valid_frames, depth_kernel, mix_weight, out_grad):
    width, head = query_rows.shape
    depth = lax.axis_size("z")
    ctx = ("yh", "z")
    tp = ("chip", "core")
    devices = 2 * depth
    lanes = lax.axis_size(tp)
    model = mix_weight.shape[1]
    rows8 = out_grad.shape[0]
    norm = (width * devices) ** -0.5
    valid = valid_frames[0]
    half = lax.axis_index("yh")
    spot = lax.axis_index("z")
    place = jnp.stack([spot, (half * depth + spot) * width, valid, jnp.int32(width * devices), half, lax.axis_index("core")]).astype(jnp.int32)
    swap = [(0, 1), (1, 0)]
    rim_pairs = []
    sides = RIM // rows8
    for i in range(devices - 1):
        for k in range(sides):
            rim_pairs.append((i * lanes + lanes - sides + k, (i + 1) * lanes + k))
            rim_pairs.append(((i + 1) * lanes + k, i * lanes + lanes - sides + k))

    rim_rows = lax.ppermute(out_grad, ctx + tp, rim_pairs)
    own = jnp.concatenate([query_rows.T, key_rows.T, value_rows.T], axis=0)
    both = lax.all_gather(own, "yh", axis=0)
    rim_rows, both = lax.optimization_barrier((rim_rows, both))
    front, pair = call(
        first_pack,
        (jax.ShapeDtypeStruct((3 * head + 32, width), BF16), jax.ShapeDtypeStruct((3 * head, width), BF16)),
        2 ** 20,
        scalars=1,
    )(place, both)
    with_rim = jnp.concatenate([out_grad, rim_rows], axis=0)
    shared = lax.all_to_all(jnp.broadcast_to(with_rim[None], (lanes,) + with_rim.shape), tp, 0, 0, tiled=True)
    everyone = lax.all_gather(front, "z", axis=0)
    shared, everyone = lax.optimization_barrier((shared, everyone))

    part = jax.ShapeDtypeStruct((head + 8, 2 * width), F32)
    block = jax.ShapeDtypeStruct((head, width), BF16)
    mine, other = call(
        attend, (part, part), 2 ** 28, [pltpu.VMEM((depth, width, 3 * width), F32)], scalars=1
    )(place, everyone, own, pair)
    shared, other = lax.optimization_barrier((shared, other))
    got = lax.all_gather(other, "yh", axis=0)
    share = head * model // width // depth
    half_rows = jax.ShapeDtypeStruct((width // 2, model), BF16)
    keep, send, pack, copies = call(
        middle_part,
        (
            half_rows,
            half_rows,
            jax.ShapeDtypeStruct((80, width), BF16),
            jax.ShapeDtypeStruct((depth, 72 + share, width), BF16),
        ),
        2 ** 27,
        [
            pltpu.VMEM(mix_weight.shape, BF16),
            pltpu.SemaphoreType.DMA,
            pltpu.VMEM((width + 2 * RIM + KSIZE // 2, width), F32),
            pltpu.VMEM((width + 2 * RIM - KSIZE // 2, width), F32),
        ],
        scalars=1,
        remote=1,
    )(place, mix_weight, mine, got, depth_kernel, shared)
    packs = lax.all_to_all(copies, "z", 0, 0, tiled=True)
    keep_got = lax.ppermute(send, "core", swap)
    partial = call(add_pair, half_rows, 2 ** 20)(keep, keep_got)
    pack_pair = lax.ppermute(pack, "yh", swap)
    d_query = call(query_back, jax.ShapeDtypeStruct((head, 2 * width), F32), 2 ** 28, scalars=1)(
        place, everyone, own, pair, pack, pack_pair
    )
    packs, d_query, partial = lax.optimization_barrier((packs, d_query, partial))

    mix_mine = call(mix_sum, jax.ShapeDtypeStruct((share + 8, width), F32), 2 ** 22)(packs)
    mix_both = lax.all_gather(mix_mine, "yh", axis=0)
    spread = call(mix_spread, jax.ShapeDtypeStruct((depth, share + 8, width), BF16), 2 ** 20)(mix_both)
    block_parts = lax.all_to_all(partial.reshape(lanes // 2, rows8, model), "chip", 0, 0, tiled=True)
    spread, block_parts = lax.optimization_barrier((spread, block_parts))
    pieces = lax.all_to_all(spread, "z", 0, 0, tiled=True)
    result = jax.ShapeDtypeStruct((3 * head, width), F32)
    sent = jax.ShapeDtypeStruct(result.shape, BF16)
    mine, other = call(backward, (result, sent), 2 ** 29, scalars=1)(
        place, everyone, packs, own, pair, d_query
    )
    got = lax.all_gather(other, "yh", axis=0)
    d_query, d_key, d_value = call(finish, (block, block, block), 2 ** 20, scalars=1)(place, mine, got)

    block_out = call(sum_blocks, jax.ShapeDtypeStruct((rows8, model), BF16), 2 ** 20)(block_parts)
    mix_grad, tap_total = call(
        functools.partial(mix_place, norm, share),
        (jax.ShapeDtypeStruct((head, model), F32), jax.ShapeDtypeStruct((KSIZE, head), F32)),
        2 ** 20,
    )(pieces)
    return block_out, d_query.T, d_key.T, d_value.T, mix_grad, tap_total


def solution(mesh):
    count = mesh.shape["ctx"]
    fine = Mesh(mesh.devices.reshape(2, count // 2, mesh.shape["tp"] // 2, 2), ("yh", "z", "chip", "core"))
    ctx = ("yh", "z")
    tp = ("chip", "core")
    every = ctx + tp
    return jax.shard_map(
        body,
        mesh=fine,
        in_specs=(
            P(ctx, tp),
            P(ctx, tp),
            P(ctx, tp),
            P(),
            P(None, tp),
            P(tp, None),
            P(every, None),
        ),
        out_specs=(
            P(every, None),
            P(ctx, tp),
            P(ctx, tp),
            P(ctx, tp),
            P(tp, None),
            P(None, tp),
        ),
        check_vma=False,
    )
```

```python
import functools

import jax
import jax.numpy as jnp
from jax import lax
from jax.experimental import pallas as pl
from jax.experimental.pallas import tpu as pltpu
from jax.sharding import Mesh, PartitionSpec as P

F32 = jnp.float32
BF16 = jnp.bfloat16
KSIZE = 32
RIM = KSIZE // 2
LOW = -1e30
VMEM_BYTES = 48 * 1024 * 1024


def dot00(a, b):
    return lax.dot_general(a, b, (((0,), (0,)), ((), ())), preferred_element_type=F32)


def dot10(a, b):
    return lax.dot_general(a, b, (((1,), (0,)), ((), ())), preferred_element_type=F32)


def dot11(a, b):
    return lax.dot_general(a, b, (((1,), (1,)), ((), ())), preferred_element_type=F32)


def rows_of(count, lanes, entries):
    index = lax.broadcasted_iota(jnp.int32, (count, lanes), 0)
    out = jnp.zeros((count, lanes), F32)
    for where, value in entries:
        out = jnp.where(index == where, value, out)
    return out


def split3(x):
    high = x.astype(BF16).astype(F32)
    rest = x - high
    mid = rest.astype(BF16).astype(F32)
    return high, mid, rest - mid


def call(kernel, out_shapes, flops, scratch=(), scalars=0, remote=0):
    specs = {}
    if scalars:
        count = kernel.__code__.co_argcount - len(scratch) - len(jax.tree.leaves(out_shapes))
        spaces = [pltpu.SMEM] + [pl.ANY] * remote + [pltpu.VMEM] * (count - 1 - remote)
        specs["in_specs"] = [pl.BlockSpec(memory_space=space) for space in spaces]
    return pl.pallas_call(
        kernel,
        out_shape=out_shapes,
        **specs,
        scratch_shapes=list(scratch),
        compiler_params=pltpu.CompilerParams(vmem_limit_bytes=VMEM_BYTES),
        cost_estimate=pl.CostEstimate(flops=flops, bytes_accessed=2 ** 20, transcendentals=0),
    )


def side_of(low, high):
    lane = lax.broadcasted_iota(jnp.int32, low.shape, 1)
    return jnp.where(lane < low.shape[1] // 2, high, low)


def bias_of(place_ref, block, base):
    lane = lax.broadcasted_iota(jnp.int32, (1, 128), 1)
    return jnp.where((base + block) * 128 + lane < place_ref[2], 0.0, LOW)


def edges_of(packed):
    packed = packed.astype(F32)
    return jnp.concatenate([packed, pltpu.roll(packed, 64, 1)], axis=0)


def copy_rows(own_ref, rim_ref, out_ref):
    both = jnp.concatenate([own_ref[...].astype(F32), rim_ref[...].astype(F32)], axis=0).astype(BF16)
    for j in range(out_ref.shape[0]):
        out_ref[j] = both


def first_pack(place_ref, both_ref, pack_ref, pair_ref):
    own = both_ref[place_ref[4]]
    pair = both_ref[1 - place_ref[4]]
    query = pair[0:64].astype(F32)
    lane = lax.broadcasted_iota(jnp.int32, query.shape, 1)
    edge = jnp.where(lane < 32, query, pltpu.roll(query, 64, 1))
    edge = jnp.where(lane[0:32] < 64, edge[0:32], pltpu.roll(edge[32:64], 64, 1))
    pair_ref[...] = pair
    pack_ref[0:192] = own
    pack_ref[192:224] = edge.astype(BF16)


def lay_grads(shared_ref):
    rows = []
    for i in range(shared_ref.shape[0] // 2):
        even = shared_ref[2 * i].astype(F32)
        odd = shared_ref[2 * i + 1].astype(F32)
        rows.append(jnp.concatenate([even[0:8], odd[0:8]], axis=0).astype(BF16))
        rim = jnp.concatenate([even[8:16], odd[8:16]], axis=0).astype(BF16)
        if i == 0:
            low = rim
    return jnp.concatenate([low] + rows + [rim], axis=0)


def attend(place_ref, all_ref, own_ref, pair_ref, mine_ref, other_ref, score_ref):
    blocks = all_ref.shape[0]
    head = 64
    width = 128
    lanes = 3 * width
    scale = head ** -0.5
    spot = place_ref[0]
    first = spot == 0
    spot_rows = place_ref[4] * blocks
    last = spot == blocks - 1
    before = lax.rem(spot + blocks - 1, blocks)
    after = lax.rem(spot + 1, blocks)
    low_here = all_ref[before, 0:head].astype(F32)
    high_here = all_ref[after, 0:head].astype(F32)
    low_there = pltpu.roll(edges_of(all_ref[before, 3 * head : 3 * head + 32]), width // 2, 1)
    high_there = edges_of(all_ref[after, 3 * head : 3 * head + 32])
    side_own = side_of(jnp.where(first, low_there, low_here), jnp.where(last, high_there, high_here))
    side_pair = side_of(jnp.where(first, low_here, low_there), jnp.where(last, high_here, high_there))
    lane = lax.broadcasted_iota(jnp.int32, (head, width), 1)
    middle = (lane >= 32) & (lane < 96)
    edges = jnp.where(middle, pltpu.roll(side_pair, width // 2, 1), side_own)
    query = jnp.concatenate([own_ref[0:head].astype(F32), pair_ref[0:head].astype(F32), edges], axis=1) * scale
    query = jnp.concatenate([query, rows_of(16, lanes, [(6, 1.0)])], axis=0).astype(BF16)
    peak = jnp.full((1, lanes), LOW, F32)
    for b in range(blocks):
        key = jnp.concatenate(
            [all_ref[b, head : 2 * head], rows_of(16, width, [(6, bias_of(place_ref, b, spot_rows))]).astype(BF16)], axis=0
        )
        score = dot00(key, query)
        score_ref[b] = score
        peak = jnp.maximum(peak, jnp.max(score, axis=0, keepdims=True))
    total = jnp.zeros((1, lanes), F32)
    out = jnp.zeros((head, lanes), F32)
    for b in range(0, blocks, 2):
        pair_weight = []
        for k in (b, b + 1):
            weight = jnp.exp(score_ref[k] - peak)
            total = total + jnp.sum(weight, axis=0, keepdims=True)
            pair_weight.append(weight.astype(BF16))
        values = jnp.concatenate([all_ref[b, 2 * head : 3 * head], all_ref[b + 1, 2 * head : 3 * head]], axis=1)
        out = out + dot10(values, jnp.concatenate(pair_weight, axis=0))
    out = out / total
    lse = peak + jnp.log(total)
    both = jnp.concatenate([out, jnp.broadcast_to(lse, (8, lanes))], axis=0)
    edges = both[:, 2 * width :]
    mine_ref[:, 0:width] = both[:, 0:width]
    mine_ref[:, width:] = edges
    other = jnp.concatenate([both[:, width : 2 * width], pltpu.roll(edges, width // 2, 1)], axis=1)
    log_rows = rows_of(16, 2 * width, list(enumerate(split3(other[head : head + 1]))))
    other_ref[...] = jnp.concatenate([other[0:head], log_rows], axis=0).astype(BF16)


def middle_part(place_ref, weight_hbm, mine_ref, got_ref, taps_ref, shared_ref, keep_ref, send_ref, pack_ref, copies_ref, weight_ref, sem, wide_ref, back_ref):
    fetch = pltpu.make_async_copy(weight_hbm, weight_ref, sem)
    fetch.start()
    width = 128
    head = 64
    ring = 2 * width
    half = KSIZE // 2
    reach = width + 2 * RIM
    start = place_ref[1]
    valid = place_ref[2]
    frames = place_ref[3]
    mine = mine_ref[64:65]
    side_at = 1 - place_ref[4]
    sent = got_ref[side_at].astype(F32)
    got = sent[64:65] + sent[65:66] + sent[66:67]
    top = jnp.maximum(mine, got)
    lse = top + jnp.log(jnp.exp(mine - top) + jnp.exp(got - top))
    attn = mine_ref[0:64] * jnp.exp(mine - lse) + sent[0:64] * jnp.exp(got - lse)
    attn = attn.astype(BF16).astype(F32)
    lane = lax.broadcasted_iota(jnp.int32, (1, ring), 1)
    frame = start + jnp.where(lane < ring - width // 2, lane, lane - ring)
    masked = jnp.where((frame >= 0) & (frame < frames) & (frame < valid), attn, 0.0)
    own_rows = masked[:, 0:width].T
    side_rows = masked[:, width:ring].T
    rows = jnp.concatenate([side_rows[96:128], own_rows, side_rows[0:32]], axis=0)
    wide_ref[...] = jnp.concatenate([rows[0 : reach + half], rows[half : reach + KSIZE]], axis=1)
    taps = jnp.concatenate([taps_ref[0:half], taps_ref[half:KSIZE]], axis=1)
    depth = jnp.zeros((reach, width), F32)
    for t in range(half):
        depth = depth + taps[t : t + 1] * wide_ref[t : t + reach]
    depth = depth[:, 0:head] + depth[:, head:width]
    gate = jax.nn.sigmoid(depth)
    swish = (depth * gate)[RIM : RIM + width].astype(BF16)
    grad = lay_grads(shared_ref)
    mix = dot00(swish, grad[RIM : RIM + width])
    mix = jnp.concatenate([mix[:, at : at + width] for at in range(0, mix.shape[1], width)], axis=0)
    fetch.wait()
    weight = weight_ref[...]
    partial = dot10(swish, weight)
    core = place_ref[5] == 0
    even = jnp.concatenate([partial[at : at + 8] for at in range(0, width, 16)], axis=0)
    odd = jnp.concatenate([partial[at + 8 : at + 16] for at in range(0, width, 16)], axis=0)
    keep_ref[...] = jnp.where(core, even, odd).astype(BF16)
    send_ref[...] = jnp.where(core, odd, even).astype(BF16)
    dgrad = dot11(grad, weight) * gate * (1.0 + depth * (1.0 - gate))
    row = start - RIM + lax.broadcasted_iota(jnp.int32, (reach, head), 0)
    dgrad = jnp.where((row >= 0) & (row < frames), dgrad, 0.0).astype(BF16).astype(F32)
    back_ref[...] = jnp.concatenate([dgrad[half:reach], dgrad[0 : reach - half]], axis=1)
    inner = dgrad[RIM : RIM + width]
    inner = jnp.concatenate([inner, inner], axis=1)
    total = jnp.zeros((width, width), F32)
    tap_rows = []
    for t in range(half):
        total = total + taps[t : t + 1] * back_ref[half - t : half - t + width]
        tap_rows.append((t, jnp.sum(wide_ref[RIM + t : RIM + t + width] * inner, axis=0, keepdims=True)))
    tap_grad = rows_of(half, width, tap_rows)
    total = total[:, 0:head] + total[:, head:width]
    row = start + lax.broadcasted_iota(jnp.int32, (width, head), 0)
    grad_out = jnp.where(row < valid, total, 0.0).T.astype(BF16)
    delta = jnp.sum(grad_out.astype(F32) * attn[:, :width], axis=0, keepdims=True)
    a, b, c = split3(-lse[:, :width])
    d, e, f = split3(-delta)
    stats = rows_of(16, width, [(0, a), (1, b), (2, c), (3, d), (4, e), (5, f), (6, 1.0)])
    pack_ref[...] = jnp.concatenate([grad_out, stats.astype(BF16)], axis=0)
    row = lax.broadcasted_iota(jnp.int32, (8, width), 0)
    share = copies_ref.shape[1] - 72
    for j in range(copies_ref.shape[0]):
        copies_ref[j, 0:64] = grad_out
        rest = jnp.where(row == 7, tap_grad[j : j + 1], stats[0:8])
        rest = jnp.concatenate([rest, mix[j * share : (j + 1) * share]], axis=0)
        copies_ref[j, 64:] = rest.astype(BF16)


ONES = [(0, 1.0), (1, 1.0), (2, 1.0)]
DELTAS = [(3, 1.0), (4, 1.0), (5, 1.0)]


def query_back(place_ref, all_ref, own_ref, pair_ref, pack_own_ref, pack_pair_ref, out_ref):
    blocks = all_ref.shape[0]
    base = place_ref[4] * blocks
    head = 64
    width = 128
    scale = head ** -0.5
    query = jnp.concatenate([own_ref[0:head], pair_ref[0:head]], axis=1)
    packs = jnp.concatenate([pack_own_ref[...], pack_pair_ref[...]], axis=1)
    query = (query.astype(F32) * scale).astype(BF16)
    query = jnp.concatenate([query, packs[head : head + 16]], axis=0)
    value_rows = rows_of(16, width, DELTAS).astype(BF16)
    total = jnp.zeros((head, 2 * width), F32)
    for first in range(0, blocks, 2):
        keys, scores = [], []
        for b in (first, first + 1):
            key_b = all_ref[b, head : 2 * head]
            key_rows = rows_of(16, width, ONES + [(6, bias_of(place_ref, b, base))]).astype(BF16)
            value_aug = jnp.concatenate([all_ref[b, 2 * head : 3 * head], value_rows], axis=0)
            weight = jnp.exp(dot00(jnp.concatenate([key_b, key_rows], axis=0), query))
            scores.append((weight * dot00(value_aug, packs)).astype(BF16))
            keys.append(key_b)
        total = total + dot10(jnp.concatenate(keys, axis=1), jnp.concatenate(scores, axis=0))
    out_ref[...] = total * scale


def backward(place_ref, all_ref, packs_ref, own_ref, pair_ref, d_query_ref, mine_ref, other_ref):
    blocks = all_ref.shape[0]
    base = place_ref[4] * blocks
    pair_base = blocks - base
    pair_bias = jnp.concatenate([bias_of(place_ref, place_ref[0], base), bias_of(place_ref, place_ref[0], pair_base)], axis=1)
    head = 64
    width = 128
    scale = head ** -0.5
    both = jnp.concatenate([own_ref[head:], pair_ref[head:]], axis=1)
    more = packs_ref.shape[1] - head
    key_rows = rows_of(more, 2 * width, ONES + [(6, pair_bias)]).astype(BF16)
    key = jnp.concatenate([both[0:head], key_rows], axis=0)
    value = jnp.concatenate([both[head:], rows_of(more, 2 * width, DELTAS).astype(BF16)], axis=0)
    d_key = jnp.zeros((head, 2 * width), F32)
    d_value = jnp.zeros((head, 2 * width), F32)
    for first in range(0, blocks, 2):
        queries, grads, scores, weights = [], [], [], []
        for b in (first, first + 1):
            query_b = (all_ref[b, 0:head].astype(F32) * scale).astype(BF16)
            query_aug = jnp.concatenate([query_b, packs_ref[b, head:]], axis=0)
            weight = jnp.exp(dot00(query_aug, key))
            scores.append((weight * dot00(packs_ref[b], value)).astype(BF16))
            weights.append(weight.astype(BF16))
            queries.append(query_b)
            grads.append(packs_ref[b, 0:head])
        d_key = d_key + dot10(jnp.concatenate(queries, axis=1), jnp.concatenate(scores, axis=0))
        d_value = d_value + dot10(jnp.concatenate(grads, axis=1), jnp.concatenate(weights, axis=0))
    for ref, at in ((mine_ref, 0), (other_ref, width)):
        kind = ref.dtype
        ref[0:head] = d_query_ref[:, at : at + width].astype(kind)
        ref[head : 2 * head] = d_key[:, at : at + width].astype(kind)
        ref[2 * head : 3 * head] = d_value[:, at : at + width].astype(kind)


def finish(place_ref, mine_ref, got_ref, query_ref, key_ref, value_ref):
    total = mine_ref[...] + got_ref[1 - place_ref[4]].astype(F32)
    query_ref[...] = total[0:64].astype(BF16)
    key_ref[...] = total[64:128].astype(BF16)
    value_ref[...] = total[128:192].astype(BF16)


def add_pair(mine_ref, got_ref, out_ref):
    out_ref[...] = (mine_ref[...].astype(F32) + got_ref[...].astype(F32)).astype(BF16)


def mix_sum(packs_ref, out_ref):
    share = packs_ref.shape[1] - 72
    total = jnp.zeros((share + 8, 128), F32)
    for j in range(packs_ref.shape[0]):
        total = total + packs_ref[j, 64:].astype(F32)
    out_ref[0:share] = total[8:]
    out_ref[share:] = rows_of(out_ref.shape[0] - share, 128, [(0, total[7:8])])


def mix_spread(both_ref, out_ref):
    total = (both_ref[0] + both_ref[1]).astype(BF16)
    for j in range(out_ref.shape[0]):
        out_ref[j] = total


def mix_place(norm, share, parts_ref, out_ref, taps_ref):
    pieces = [parts_ref[z].astype(F32) * norm for z in range(parts_ref.shape[0])]
    full = jnp.concatenate([piece[0:share] for piece in pieces], axis=0)
    for at in range(out_ref.shape[1] // 128):
        out_ref[:, at * 128 : (at + 1) * 128] = full[at * 64 : (at + 1) * 64]
    tap = rows_of(len(pieces), 128, [(z, piece[share : share + 1]) for z, piece in enumerate(pieces)])
    taps_ref[0:16] = tap[:, 0:64]
    taps_ref[16:32] = tap[:, 64:128]


def sum_blocks(parts_ref, out_ref):
    total = jnp.zeros(out_ref.shape, F32)
    for j in range(parts_ref.shape[0]):
        total = total + parts_ref[j].astype(F32)
    out_ref[...] = total.astype(BF16)


def body(query_rows, key_rows, value_rows, valid_frames, depth_kernel, mix_weight, out_grad):
    width, head = query_rows.shape
    depth = lax.axis_size("z")
    ctx = ("yh", "z")
    tp = ("chip", "core")
    devices = 2 * depth
    lanes = lax.axis_size(tp)
    model = mix_weight.shape[1]
    rows8 = out_grad.shape[0]
    norm = (width * devices) ** -0.5
    valid = valid_frames[0]
    half = lax.axis_index("yh")
    spot = lax.axis_index("z")
    place = jnp.stack([spot, (half * depth + spot) * width, valid, jnp.int32(width * devices), half, lax.axis_index("core")]).astype(jnp.int32)
    swap = [(0, 1), (1, 0)]
    rim_pairs = []
    sides = RIM // rows8
    for i in range(devices - 1):
        for k in range(sides):
            rim_pairs.append((i * lanes + lanes - sides + k, (i + 1) * lanes + k))
            rim_pairs.append(((i + 1) * lanes + k, i * lanes + lanes - sides + k))

    rim_rows = lax.ppermute(out_grad, ctx + tp, rim_pairs)
    own = jnp.concatenate([query_rows.T, key_rows.T, value_rows.T], axis=0)
    both = lax.all_gather(own, "yh", axis=0)
    rim_rows, both = lax.optimization_barrier((rim_rows, both))
    front, pair = call(
        first_pack,
        (jax.ShapeDtypeStruct((3 * head + 32, width), BF16), jax.ShapeDtypeStruct((3 * head, width), BF16)),
        2 ** 20,
        scalars=1,
    )(place, both)
    grads = call(copy_rows, jax.ShapeDtypeStruct((lanes, 2 * rows8, model), BF16), 2 ** 20)(out_grad, rim_rows)
    shared = lax.all_to_all(grads, tp, 0, 0, tiled=True)
    everyone = lax.all_gather(front, "z", axis=0)
    shared, everyone = lax.optimization_barrier((shared, everyone))

    part = jax.ShapeDtypeStruct((head + 8, 2 * width), F32)
    block = jax.ShapeDtypeStruct((head, width), BF16)
    mine, other = call(
        attend, (part, jax.ShapeDtypeStruct((head + 16, 2 * width), BF16)), 2 ** 28, [pltpu.VMEM((depth, width, 3 * width), F32)], scalars=1
    )(place, everyone, own, pair)
    shared, other = lax.optimization_barrier((shared, other))
    got = lax.all_gather(other, "yh", axis=0)
    share = head * model // width // depth
    half_rows = jax.ShapeDtypeStruct((width // 2, model), BF16)
    keep, send, pack, copies = call(
        middle_part,
        (
            half_rows,
            half_rows,
            jax.ShapeDtypeStruct((80, width), BF16),
            jax.ShapeDtypeStruct((depth, 72 + share, width), BF16),
        ),
        2 ** 27,
        [
            pltpu.VMEM(mix_weight.shape, BF16),
            pltpu.SemaphoreType.DMA,
            pltpu.VMEM((width + 2 * RIM + KSIZE // 2, width), F32),
            pltpu.VMEM((width + 2 * RIM - KSIZE // 2, width), F32),
        ],
        scalars=1,
        remote=1,
    )(place, mix_weight, mine, got, depth_kernel, shared)
    packs = lax.all_to_all(copies, "z", 0, 0, tiled=True)
    keep_got = lax.ppermute(send, "core", swap)
    partial = call(add_pair, half_rows, 2 ** 20)(keep, keep_got)
    pack_pair = lax.ppermute(pack, "yh", swap)
    d_query = call(query_back, jax.ShapeDtypeStruct((head, 2 * width), F32), 2 ** 28, scalars=1)(
        place, everyone, own, pair, pack, pack_pair
    )
    packs, d_query, partial = lax.optimization_barrier((packs, d_query, partial))

    mix_mine = call(mix_sum, jax.ShapeDtypeStruct((share + 8, width), F32), 2 ** 22)(packs)
    mix_both = lax.all_gather(mix_mine, "yh", axis=0)
    spread = call(mix_spread, jax.ShapeDtypeStruct((depth, share + 8, width), BF16), 2 ** 20)(mix_both)
    block_parts = lax.all_to_all(partial.reshape(lanes // 2, rows8, model), "chip", 0, 0, tiled=True)
    spread, block_parts = lax.optimization_barrier((spread, block_parts))
    pieces = lax.all_to_all(spread, "z", 0, 0, tiled=True)
    result = jax.ShapeDtypeStruct((3 * head, width), F32)
    sent = jax.ShapeDtypeStruct(result.shape, BF16)
    mine, other = call(backward, (result, sent), 2 ** 29, scalars=1)(
        place, everyone, packs, own, pair, d_query
    )
    got = lax.all_gather(other, "yh", axis=0)
    d_query, d_key, d_value = call(finish, (block, block, block), 2 ** 20, scalars=1)(place, mine, got)

    block_out = call(sum_blocks, jax.ShapeDtypeStruct((rows8, model), BF16), 2 ** 20)(block_parts)
    mix_grad, tap_total = call(
        functools.partial(mix_place, norm, share),
        (jax.ShapeDtypeStruct((head, model), F32), jax.ShapeDtypeStruct((KSIZE, head), F32)),
        2 ** 20,
    )(pieces)
    return block_out, d_query.T, d_key.T, d_value.T, mix_grad, tap_total


def solution(mesh):
    count = mesh.shape["ctx"]
    fine = Mesh(mesh.devices.reshape(2, count // 2, mesh.shape["tp"] // 2, 2), ("yh", "z", "chip", "core"))
    ctx = ("yh", "z")
    tp = ("chip", "core")
    every = ctx + tp
    return jax.shard_map(
        body,
        mesh=fine,
        in_specs=(
            P(ctx, tp),
            P(ctx, tp),
            P(ctx, tp),
            P(),
            P(None, tp),
            P(tp, None),
            P(every, None),
        ),
        out_specs=(
            P(every, None),
            P(ctx, tp),
            P(ctx, tp),
            P(ctx, tp),
            P(tp, None),
            P(None, tp),
        ),
        check_vma=False,
    )
```

```python
import functools

import jax
import jax.numpy as jnp
from jax import lax
from jax.experimental import pallas as pl
from jax.experimental.pallas import tpu as pltpu
from jax.sharding import Mesh, PartitionSpec as P

F32 = jnp.float32
BF16 = jnp.bfloat16
KSIZE = 32
RIM = KSIZE // 2
LOW = -1e30
VMEM_BYTES = 48 * 1024 * 1024


def dot00(a, b):
    return lax.dot_general(a, b, (((0,), (0,)), ((), ())), preferred_element_type=F32)


def dot10(a, b):
    return lax.dot_general(a, b, (((1,), (0,)), ((), ())), preferred_element_type=F32)


def dot11(a, b):
    return lax.dot_general(a, b, (((1,), (1,)), ((), ())), preferred_element_type=F32)


def rows_of(count, lanes, entries):
    index = lax.broadcasted_iota(jnp.int32, (count, lanes), 0)
    out = jnp.zeros((count, lanes), F32)
    for where, value in entries:
        out = jnp.where(index == where, value, out)
    return out


def split3(x):
    high = x.astype(BF16).astype(F32)
    rest = x - high
    mid = rest.astype(BF16).astype(F32)
    return high, mid, rest - mid


def call(kernel, out_shapes, flops, scratch=(), scalars=0, remote=0):
    specs = {}
    if scalars:
        count = kernel.__code__.co_argcount - len(scratch) - len(jax.tree.leaves(out_shapes))
        spaces = [pltpu.SMEM] + [pl.ANY] * remote + [pltpu.VMEM] * (count - 1 - remote)
        specs["in_specs"] = [pl.BlockSpec(memory_space=space) for space in spaces]
    return pl.pallas_call(
        kernel,
        out_shape=out_shapes,
        **specs,
        scratch_shapes=list(scratch),
        compiler_params=pltpu.CompilerParams(vmem_limit_bytes=VMEM_BYTES),
        cost_estimate=pl.CostEstimate(flops=flops, bytes_accessed=2 ** 20, transcendentals=0),
    )


def side_of(low, high):
    lane = lax.broadcasted_iota(jnp.int32, low.shape, 1)
    return jnp.where(lane < low.shape[1] // 2, high, low)


def bias_of(place_ref, block, base):
    lane = lax.broadcasted_iota(jnp.int32, (1, 128), 1)
    return jnp.where((base + block) * 128 + lane < place_ref[2], 0.0, LOW)


def edges_of(packed):
    packed = packed.astype(F32)
    return jnp.concatenate([packed, pltpu.roll(packed, 64, 1)], axis=0)


def copy_rows(own_ref, rim_ref, out_ref):
    both = jnp.concatenate([own_ref[...].astype(F32), rim_ref[...].astype(F32)], axis=0).astype(BF16)
    for j in range(out_ref.shape[0]):
        out_ref[j] = both


def first_pack(place_ref, both_ref, pack_ref, pair_ref):
    own = both_ref[place_ref[4]]
    pair = both_ref[1 - place_ref[4]]
    query = pair[0:64].astype(F32)
    lane = lax.broadcasted_iota(jnp.int32, query.shape, 1)
    edge = jnp.where(lane < 32, query, pltpu.roll(query, 64, 1))
    edge = jnp.where(lane[0:32] < 64, edge[0:32], pltpu.roll(edge[32:64], 64, 1))
    pair_ref[...] = pair
    pack_ref[0:192] = own
    pack_ref[192:224] = edge.astype(BF16)


def lay_grads(shared_ref):
    rows = []
    for i in range(shared_ref.shape[0] // 2):
        even = shared_ref[2 * i].astype(F32)
        odd = shared_ref[2 * i + 1].astype(F32)
        rows.append(jnp.concatenate([even[0:8], odd[0:8]], axis=0).astype(BF16))
        rim = jnp.concatenate([even[8:16], odd[8:16]], axis=0).astype(BF16)
        if i == 0:
            low = rim
    return jnp.concatenate([low] + rows + [rim], axis=0)


def attend(place_ref, all_ref, own_ref, pair_ref, mine_ref, other_ref, score_ref):
    blocks = all_ref.shape[0]
    head = 64
    width = 128
    lanes = 3 * width
    scale = head ** -0.5
    spot = place_ref[0]
    first = spot == 0
    spot_rows = place_ref[4] * blocks
    last = spot == blocks - 1
    before = lax.rem(spot + blocks - 1, blocks)
    after = lax.rem(spot + 1, blocks)
    low_here = all_ref[before, 0:head].astype(F32)
    high_here = all_ref[after, 0:head].astype(F32)
    low_there = pltpu.roll(edges_of(all_ref[before, 3 * head : 3 * head + 32]), width // 2, 1)
    high_there = edges_of(all_ref[after, 3 * head : 3 * head + 32])
    side_own = side_of(jnp.where(first, low_there, low_here), jnp.where(last, high_there, high_here))
    side_pair = side_of(jnp.where(first, low_here, low_there), jnp.where(last, high_here, high_there))
    lane = lax.broadcasted_iota(jnp.int32, (head, width), 1)
    middle = (lane >= 32) & (lane < 96)
    edges = jnp.where(middle, pltpu.roll(side_pair, width // 2, 1), side_own)
    query = jnp.concatenate([own_ref[0:head].astype(F32), pair_ref[0:head].astype(F32), edges], axis=1) * scale
    query = jnp.concatenate([query, rows_of(16, lanes, [(6, 1.0)])], axis=0).astype(BF16)
    peak = jnp.full((1, lanes), LOW, F32)
    for b in range(blocks):
        key = jnp.concatenate(
            [all_ref[b, head : 2 * head], rows_of(16, width, [(6, bias_of(place_ref, b, spot_rows))]).astype(BF16)], axis=0
        )
        score = dot00(key, query)
        score_ref[b] = score
        peak = jnp.maximum(peak, jnp.max(score, axis=0, keepdims=True))
    total = jnp.zeros((1, lanes), F32)
    out = jnp.zeros((head, lanes), F32)
    for b in range(0, blocks, 2):
        pair_weight = []
        for k in (b, b + 1):
            weight = jnp.exp(score_ref[k] - peak)
            total = total + jnp.sum(weight, axis=0, keepdims=True)
            pair_weight.append(weight.astype(BF16))
        values = jnp.concatenate([all_ref[b, 2 * head : 3 * head], all_ref[b + 1, 2 * head : 3 * head]], axis=1)
        out = out + dot10(values, jnp.concatenate(pair_weight, axis=0))
    out = out / total
    lse = peak + jnp.log(total)
    both = jnp.concatenate([out, jnp.broadcast_to(lse, (8, lanes))], axis=0)
    edges = both[:, 2 * width :]
    mine_ref[:, 0:width] = both[:, 0:width]
    mine_ref[:, width:] = edges
    other = jnp.concatenate([both[:, width : 2 * width], pltpu.roll(edges, width // 2, 1)], axis=1)
    log_rows = rows_of(16, 2 * width, list(enumerate(split3(other[head : head + 1]))))
    other_ref[...] = jnp.concatenate([other[0:head], log_rows], axis=0).astype(BF16)


def middle_part(place_ref, weight_hbm, mine_ref, got_ref, taps_ref, shared_ref, keep_ref, send_ref, pack_ref, copies_ref, weight_ref, sem, wide_ref, back_ref):
    fetch = pltpu.make_async_copy(weight_hbm, weight_ref, sem)
    fetch.start()
    width = 128
    head = 64
    ring = 2 * width
    half = KSIZE // 2
    reach = width + 2 * RIM
    start = place_ref[1]
    valid = place_ref[2]
    frames = place_ref[3]
    mine = mine_ref[64:65]
    side_at = 1 - place_ref[4]
    sent = got_ref[side_at].astype(F32)
    got = sent[64:65] + sent[65:66] + sent[66:67]
    top = jnp.maximum(mine, got)
    lse = top + jnp.log(jnp.exp(mine - top) + jnp.exp(got - top))
    attn = mine_ref[0:64] * jnp.exp(mine - lse) + sent[0:64] * jnp.exp(got - lse)
    attn = attn.astype(BF16).astype(F32)
    lane = lax.broadcasted_iota(jnp.int32, (1, ring), 1)
    frame = start + jnp.where(lane < ring - width // 2, lane, lane - ring)
    masked = jnp.where((frame >= 0) & (frame < frames) & (frame < valid), attn, 0.0)
    own_rows = masked[:, 0:width].T
    side_rows = masked[:, width:ring].T
    rows = jnp.concatenate([side_rows[96:128], own_rows, side_rows[0:32]], axis=0)
    wide_ref[...] = jnp.concatenate([rows[0 : reach + half], rows[half : reach + KSIZE]], axis=1)
    taps = jnp.concatenate([taps_ref[0:half], taps_ref[half:KSIZE]], axis=1)
    depth = jnp.zeros((reach, width), F32)
    for t in range(half):
        depth = depth + taps[t : t + 1] * wide_ref[t : t + reach]
    depth = depth[:, 0:head] + depth[:, head:width]
    gate = jax.nn.sigmoid(depth)
    swish = (depth * gate)[RIM : RIM + width].astype(BF16)
    grad = lay_grads(shared_ref)
    mix = dot00(swish, grad[RIM : RIM + width])
    mix = jnp.concatenate([mix[:, at : at + width] for at in range(0, mix.shape[1], width)], axis=0)
    fetch.wait()
    weight = weight_ref[...]
    partial = dot10(swish, weight)
    core = place_ref[5] == 0
    even = jnp.concatenate([partial[at : at + 8] for at in range(0, width, 16)], axis=0)
    odd = jnp.concatenate([partial[at + 8 : at + 16] for at in range(0, width, 16)], axis=0)
    keep_ref[...] = jnp.where(core, even, odd).astype(BF16)
    send_ref[...] = jnp.where(core, odd, even).astype(BF16)
    dgrad = dot11(grad, weight) * gate * (1.0 + depth * (1.0 - gate))
    row = start - RIM + lax.broadcasted_iota(jnp.int32, (reach, head), 0)
    dgrad = jnp.where((row >= 0) & (row < frames), dgrad, 0.0).astype(BF16).astype(F32)
    back_ref[...] = jnp.concatenate([dgrad[half:reach], dgrad[0 : reach - half]], axis=1)
    inner = dgrad[RIM : RIM + width]
    inner = jnp.concatenate([inner, inner], axis=1)
    total = jnp.zeros((width, width), F32)
    tap_rows = []
    for t in range(half):
        total = total + taps[t : t + 1] * back_ref[half - t : half - t + width]
        tap_rows.append((t, jnp.sum(wide_ref[RIM + t : RIM + t + width] * inner, axis=0, keepdims=True)))
    tap_grad = rows_of(half, width, tap_rows)
    total = total[:, 0:head] + total[:, head:width]
    row = start + lax.broadcasted_iota(jnp.int32, (width, head), 0)
    grad_out = jnp.where(row < valid, total, 0.0).T.astype(BF16)
    delta = jnp.sum(grad_out.astype(F32) * attn[:, :width], axis=0, keepdims=True)
    a, b, c = split3(-lse[:, :width])
    d, e, f = split3(-delta)
    stats = rows_of(16, width, [(0, a), (1, b), (2, c), (3, d), (4, e), (5, f), (6, 1.0)])
    pack_ref[...] = jnp.concatenate([grad_out, stats.astype(BF16)], axis=0)
    row = lax.broadcasted_iota(jnp.int32, (8, width), 0)
    share = copies_ref.shape[1] - 72
    for j in range(copies_ref.shape[0]):
        copies_ref[j, 0:64] = grad_out
        rest = jnp.where(row == 7, tap_grad[j : j + 1], stats[0:8])
        rest = jnp.concatenate([rest, mix[j * share : (j + 1) * share]], axis=0)
        copies_ref[j, 64:] = rest.astype(BF16)


ONES = [(0, 1.0), (1, 1.0), (2, 1.0)]
DELTAS = [(3, 1.0), (4, 1.0), (5, 1.0)]


def query_back(place_ref, all_ref, own_ref, pair_ref, pack_own_ref, pack_pair_ref, out_ref):
    blocks = all_ref.shape[0]
    base = place_ref[4] * blocks
    head = 64
    width = 128
    scale = head ** -0.5
    query = jnp.concatenate([own_ref[0:head], pair_ref[0:head]], axis=1)
    packs = jnp.concatenate([pack_own_ref[...], pack_pair_ref[...]], axis=1)
    query = (query.astype(F32) * scale).astype(BF16)
    query = jnp.concatenate([query, packs[head : head + 16]], axis=0)
    value_rows = rows_of(16, width, DELTAS).astype(BF16)
    total = jnp.zeros((head, 2 * width), F32)
    for first in range(0, blocks, 2):
        keys, scores = [], []
        for b in (first, first + 1):
            key_b = all_ref[b, head : 2 * head]
            key_rows = rows_of(16, width, ONES + [(6, bias_of(place_ref, b, base))]).astype(BF16)
            value_aug = jnp.concatenate([all_ref[b, 2 * head : 3 * head], value_rows], axis=0)
            weight = jnp.exp(dot00(jnp.concatenate([key_b, key_rows], axis=0), query))
            scores.append((weight * dot00(value_aug, packs)).astype(BF16))
            keys.append(key_b)
        total = total + dot10(jnp.concatenate(keys, axis=1), jnp.concatenate(scores, axis=0))
    out_ref[...] = total * scale


def backward(place_ref, all_ref, packs_ref, own_ref, pair_ref, d_query_ref, mine_ref, other_ref):
    blocks = all_ref.shape[0]
    base = place_ref[4] * blocks
    pair_base = blocks - base
    pair_bias = jnp.concatenate([bias_of(place_ref, place_ref[0], base), bias_of(place_ref, place_ref[0], pair_base)], axis=1)
    head = 64
    width = 128
    scale = head ** -0.5
    both = jnp.concatenate([own_ref[head:], pair_ref[head:]], axis=1)
    more = packs_ref.shape[1] - head
    key_rows = rows_of(more, 2 * width, ONES + [(6, pair_bias)]).astype(BF16)
    key = jnp.concatenate([both[0:head], key_rows], axis=0)
    value = jnp.concatenate([both[head:], rows_of(more, 2 * width, DELTAS).astype(BF16)], axis=0)
    d_key = jnp.zeros((head, 2 * width), F32)
    d_value = jnp.zeros((head, 2 * width), F32)
    for first in range(0, blocks, 2):
        queries, grads, scores, weights = [], [], [], []
        for b in (first, first + 1):
            query_b = (all_ref[b, 0:head].astype(F32) * scale).astype(BF16)
            query_aug = jnp.concatenate([query_b, packs_ref[b, head:]], axis=0)
            weight = jnp.exp(dot00(query_aug, key))
            scores.append((weight * dot00(packs_ref[b], value)).astype(BF16))
            weights.append(weight.astype(BF16))
            queries.append(query_b)
            grads.append(packs_ref[b, 0:head])
        d_key = d_key + dot10(jnp.concatenate(queries, axis=1), jnp.concatenate(scores, axis=0))
        d_value = d_value + dot10(jnp.concatenate(grads, axis=1), jnp.concatenate(weights, axis=0))
    for ref, at in ((mine_ref, 0), (other_ref, width)):
        kind = ref.dtype
        ref[0:head] = d_query_ref[:, at : at + width].astype(kind)
        ref[head : 2 * head] = d_key[:, at : at + width].astype(kind)
        ref[2 * head : 3 * head] = d_value[:, at : at + width].astype(kind)


def finish(place_ref, mine_ref, got_ref, parts_ref, query_ref, key_ref, value_ref, block_ref):
    rows = jnp.zeros(block_ref.shape, F32)
    for j in range(parts_ref.shape[0]):
        rows = rows + parts_ref[j].astype(F32)
    block_ref[...] = rows.astype(BF16)
    total = mine_ref[...] + got_ref[1 - place_ref[4]].astype(F32)
    query_ref[...] = total[0:64].astype(BF16)
    key_ref[...] = total[64:128].astype(BF16)
    value_ref[...] = total[128:192].astype(BF16)


def add_pair(mine_ref, got_ref, out_ref):
    out_ref[...] = (mine_ref[...].astype(F32) + got_ref[...].astype(F32)).astype(BF16)


def mix_sum(packs_ref, out_ref):
    share = packs_ref.shape[1] - 72
    total = jnp.zeros((share + 8, 128), F32)
    for j in range(packs_ref.shape[0]):
        total = total + packs_ref[j, 64:].astype(F32)
    out_ref[0:share] = total[8:]
    out_ref[share:] = rows_of(out_ref.shape[0] - share, 128, [(0, total[7:8])])


def mix_spread(both_ref, out_ref):
    total = (both_ref[0] + both_ref[1]).astype(BF16)
    for j in range(out_ref.shape[0]):
        out_ref[j] = total


def mix_place(norm, share, parts_ref, out_ref, taps_ref):
    pieces = [parts_ref[z].astype(F32) * norm for z in range(parts_ref.shape[0])]
    full = jnp.concatenate([piece[0:share] for piece in pieces], axis=0)
    for at in range(out_ref.shape[1] // 128):
        out_ref[:, at * 128 : (at + 1) * 128] = full[at * 64 : (at + 1) * 64]
    tap = rows_of(len(pieces), 128, [(z, piece[share : share + 1]) for z, piece in enumerate(pieces)])
    taps_ref[0:16] = tap[:, 0:64]
    taps_ref[16:32] = tap[:, 64:128]


def body(query_rows, key_rows, value_rows, valid_frames, depth_kernel, mix_weight, out_grad):
    width, head = query_rows.shape
    depth = lax.axis_size("z")
    ctx = ("yh", "z")
    tp = ("chip", "core")
    devices = 2 * depth
    lanes = lax.axis_size(tp)
    model = mix_weight.shape[1]
    rows8 = out_grad.shape[0]
    norm = (width * devices) ** -0.5
    valid = valid_frames[0]
    half = lax.axis_index("yh")
    spot = lax.axis_index("z")
    place = jnp.stack([spot, (half * depth + spot) * width, valid, jnp.int32(width * devices), half, lax.axis_index("core")]).astype(jnp.int32)
    swap = [(0, 1), (1, 0)]
    rim_pairs = []
    sides = RIM // rows8
    for i in range(devices - 1):
        for k in range(sides):
            rim_pairs.append((i * lanes + lanes - sides + k, (i + 1) * lanes + k))
            rim_pairs.append(((i + 1) * lanes + k, i * lanes + lanes - sides + k))

    rim_rows = lax.ppermute(out_grad, ctx + tp, rim_pairs)
    own = jnp.concatenate([query_rows.T, key_rows.T, value_rows.T], axis=0)
    both = lax.all_gather(own, "yh", axis=0)
    rim_rows, both = lax.optimization_barrier((rim_rows, both))
    front, pair = call(
        first_pack,
        (jax.ShapeDtypeStruct((3 * head + 32, width), BF16), jax.ShapeDtypeStruct((3 * head, width), BF16)),
        2 ** 20,
        scalars=1,
    )(place, both)
    grads = call(copy_rows, jax.ShapeDtypeStruct((lanes, 2 * rows8, model), BF16), 2 ** 20)(out_grad, rim_rows)
    shared = lax.all_to_all(grads, tp, 0, 0, tiled=True)
    everyone = lax.all_gather(front, "z", axis=0)
    shared, everyone = lax.optimization_barrier((shared, everyone))

    part = jax.ShapeDtypeStruct((head + 8, 2 * width), F32)
    block = jax.ShapeDtypeStruct((head, width), BF16)
    mine, other = call(
        attend, (part, jax.ShapeDtypeStruct((head + 16, 2 * width), BF16)), 2 ** 28, [pltpu.VMEM((depth, width, 3 * width), F32)], scalars=1
    )(place, everyone, own, pair)
    shared, other = lax.optimization_barrier((shared, other))
    got = lax.all_gather(other, "yh", axis=0)
    share = head * model // width // depth
    half_rows = jax.ShapeDtypeStruct((width // 2, model), BF16)
    keep, send, pack, copies = call(
        middle_part,
        (
            half_rows,
            half_rows,
            jax.ShapeDtypeStruct((80, width), BF16),
            jax.ShapeDtypeStruct((depth, 72 + share, width), BF16),
        ),
        2 ** 27,
        [
            pltpu.VMEM(mix_weight.shape, BF16),
            pltpu.SemaphoreType.DMA,
            pltpu.VMEM((width + 2 * RIM + KSIZE // 2, width), F32),
            pltpu.VMEM((width + 2 * RIM - KSIZE // 2, width), F32),
        ],
        scalars=1,
        remote=1,
    )(place, mix_weight, mine, got, depth_kernel, shared)
    packs = lax.all_to_all(copies, "z", 0, 0, tiled=True)
    keep_got = lax.ppermute(send, "core", swap)
    partial = call(add_pair, half_rows, 2 ** 20)(keep, keep_got)
    pack_pair = lax.ppermute(pack, "yh", swap)
    d_query = call(query_back, jax.ShapeDtypeStruct((head, 2 * width), F32), 2 ** 28, scalars=1)(
        place, everyone, own, pair, pack, pack_pair
    )
    packs, d_query, partial = lax.optimization_barrier((packs, d_query, partial))

    mix_mine = call(mix_sum, jax.ShapeDtypeStruct((share + 8, width), F32), 2 ** 22)(packs)
    mix_both = lax.all_gather(mix_mine, "yh", axis=0)
    spread = call(mix_spread, jax.ShapeDtypeStruct((depth, share + 8, width), BF16), 2 ** 20)(mix_both)
    block_parts = lax.all_to_all(partial.reshape(lanes // 2, rows8, model), "chip", 0, 0, tiled=True)
    spread, block_parts = lax.optimization_barrier((spread, block_parts))
    pieces = lax.all_to_all(spread, "z", 0, 0, tiled=True)
    result = jax.ShapeDtypeStruct((3 * head, width), F32)
    sent = jax.ShapeDtypeStruct(result.shape, BF16)
    mine, other = call(backward, (result, sent), 2 ** 29, scalars=1)(
        place, everyone, packs, own, pair, d_query
    )
    got = lax.all_gather(other, "yh", axis=0)
    d_query, d_key, d_value, block_out = call(
        finish, (block, block, block, jax.ShapeDtypeStruct((rows8, model), BF16)), 2 ** 20, scalars=1
    )(place, mine, got, block_parts)

    mix_grad, tap_total = call(
        functools.partial(mix_place, norm, share),
        (jax.ShapeDtypeStruct((head, model), F32), jax.ShapeDtypeStruct((KSIZE, head), F32)),
        2 ** 20,
    )(pieces)
    return block_out, d_query.T, d_key.T, d_value.T, mix_grad, tap_total


def solution(mesh):
    count = mesh.shape["ctx"]
    fine = Mesh(mesh.devices.reshape(2, count // 2, mesh.shape["tp"] // 2, 2), ("yh", "z", "chip", "core"))
    ctx = ("yh", "z")
    tp = ("chip", "core")
    every = ctx + tp
    return jax.shard_map(
        body,
        mesh=fine,
        in_specs=(
            P(ctx, tp),
            P(ctx, tp),
            P(ctx, tp),
            P(),
            P(None, tp),
            P(tp, None),
            P(every, None),
        ),
        out_specs=(
            P(every, None),
            P(ctx, tp),
            P(ctx, tp),
            P(ctx, tp),
            P(tp, None),
            P(None, tp),
        ),
        check_vma=False,
    )
```

```python
import functools

import jax
import jax.numpy as jnp
from jax import lax
from jax.experimental import pallas as pl
from jax.experimental.pallas import tpu as pltpu
from jax.sharding import Mesh, PartitionSpec as P

F32 = jnp.float32
BF16 = jnp.bfloat16
KSIZE = 32
RIM = KSIZE // 2
LOW = -1e30
VMEM_BYTES = 48 * 1024 * 1024


def dot00(a, b):
    return lax.dot_general(a, b, (((0,), (0,)), ((), ())), preferred_element_type=F32)


def dot10(a, b):
    return lax.dot_general(a, b, (((1,), (0,)), ((), ())), preferred_element_type=F32)


def dot11(a, b):
    return lax.dot_general(a, b, (((1,), (1,)), ((), ())), preferred_element_type=F32)


def rows_of(count, lanes, entries):
    index = lax.broadcasted_iota(jnp.int32, (count, lanes), 0)
    out = jnp.zeros((count, lanes), F32)
    for where, value in entries:
        out = jnp.where(index == where, value, out)
    return out


def split3(x):
    high = x.astype(BF16).astype(F32)
    rest = x - high
    mid = rest.astype(BF16).astype(F32)
    return high, mid, rest - mid


def call(kernel, out_shapes, flops, scratch=(), scalars=0, remote=0):
    specs = {}
    if scalars:
        count = kernel.__code__.co_argcount - len(scratch) - len(jax.tree.leaves(out_shapes))
        spaces = [pltpu.SMEM] + [pl.ANY] * remote + [pltpu.VMEM] * (count - 1 - remote)
        specs["in_specs"] = [pl.BlockSpec(memory_space=space) for space in spaces]
    return pl.pallas_call(
        kernel,
        out_shape=out_shapes,
        **specs,
        scratch_shapes=list(scratch),
        compiler_params=pltpu.CompilerParams(vmem_limit_bytes=VMEM_BYTES),
        cost_estimate=pl.CostEstimate(flops=flops, bytes_accessed=2 ** 20, transcendentals=0),
    )


def side_of(low, high):
    lane = lax.broadcasted_iota(jnp.int32, low.shape, 1)
    return jnp.where(lane < low.shape[1] // 2, high, low)


def bias_of(place_ref, block, base):
    lane = lax.broadcasted_iota(jnp.int32, (1, 128), 1)
    return jnp.where((base + block) * 128 + lane < place_ref[2], 0.0, LOW)


def edges_of(packed):
    packed = packed.astype(F32)
    return jnp.concatenate([packed, pltpu.roll(packed, 64, 1)], axis=0)


def copy_rows(own_ref, rim_ref, out_ref):
    both = jnp.concatenate([own_ref[...].astype(F32), rim_ref[...].astype(F32)], axis=0).astype(BF16)
    for j in range(out_ref.shape[0]):
        out_ref[j] = both


def first_pack(place_ref, both_ref, pack_ref, pair_ref):
    own = both_ref[place_ref[4]]
    pair = both_ref[1 - place_ref[4]]
    query = pair[0:64].astype(F32)
    lane = lax.broadcasted_iota(jnp.int32, query.shape, 1)
    edge = jnp.where(lane < 32, query, pltpu.roll(query, 64, 1))
    edge = jnp.where(lane[0:32] < 64, edge[0:32], pltpu.roll(edge[32:64], 64, 1))
    pair_ref[...] = pair
    pack_ref[0:192] = own
    pack_ref[192:224] = edge.astype(BF16)


def lay_grads(shared_ref):
    rows = []
    for i in range(shared_ref.shape[0] // 2):
        even = shared_ref[2 * i].astype(F32)
        odd = shared_ref[2 * i + 1].astype(F32)
        rows.append(jnp.concatenate([even[0:8], odd[0:8]], axis=0).astype(BF16))
        rim = jnp.concatenate([even[8:16], odd[8:16]], axis=0).astype(BF16)
        if i == 0:
            low = rim
    return jnp.concatenate([low] + rows + [rim], axis=0)


def attend(place_ref, all_ref, own_ref, pair_ref, mine_ref, other_ref, score_ref):
    blocks = all_ref.shape[0]
    head = 64
    width = 128
    lanes = 3 * width
    scale = head ** -0.5
    spot = place_ref[0]
    first = spot == 0
    spot_rows = place_ref[4] * blocks
    last = spot == blocks - 1
    before = lax.rem(spot + blocks - 1, blocks)
    after = lax.rem(spot + 1, blocks)
    low_here = all_ref[before, 0:head].astype(F32)
    high_here = all_ref[after, 0:head].astype(F32)
    low_there = pltpu.roll(edges_of(all_ref[before, 3 * head : 3 * head + 32]), width // 2, 1)
    high_there = edges_of(all_ref[after, 3 * head : 3 * head + 32])
    side_own = side_of(jnp.where(first, low_there, low_here), jnp.where(last, high_there, high_here))
    side_pair = side_of(jnp.where(first, low_here, low_there), jnp.where(last, high_here, high_there))
    lane = lax.broadcasted_iota(jnp.int32, (head, width), 1)
    middle = (lane >= 32) & (lane < 96)
    edges = jnp.where(middle, pltpu.roll(side_pair, width // 2, 1), side_own)
    query = jnp.concatenate([own_ref[0:head].astype(F32), pair_ref[0:head].astype(F32), edges], axis=1) * scale
    query = jnp.concatenate([query, rows_of(16, lanes, [(6, 1.0)])], axis=0).astype(BF16)
    peak = jnp.full((8, lanes), LOW, F32)
    for b in range(blocks):
        key = jnp.concatenate(
            [all_ref[b, head : 2 * head], rows_of(16, width, [(6, bias_of(place_ref, b, spot_rows))]).astype(BF16)], axis=0
        )
        score = dot00(key, query)
        score_ref[b] = score
        for at in range(0, width, 8):
            peak = jnp.maximum(peak, score[at : at + 8])
    peak = jnp.max(peak, axis=0, keepdims=True)
    total = jnp.zeros((8, lanes), F32)
    out = jnp.zeros((head, lanes), F32)
    for b in range(0, blocks, 2):
        pair_weight = []
        for k in (b, b + 1):
            weight = jnp.exp(score_ref[k] - peak)
            for at in range(0, width, 8):
                total = total + weight[at : at + 8]
            pair_weight.append(weight.astype(BF16))
        values = jnp.concatenate([all_ref[b, 2 * head : 3 * head], all_ref[b + 1, 2 * head : 3 * head]], axis=1)
        out = out + dot10(values, jnp.concatenate(pair_weight, axis=0))
    total = jnp.sum(total, axis=0, keepdims=True)
    out = out / total
    lse = peak + jnp.log(total)
    both = jnp.concatenate([out, jnp.broadcast_to(lse, (8, lanes))], axis=0)
    edges = both[:, 2 * width :]
    mine_ref[:, 0:width] = both[:, 0:width]
    mine_ref[:, width:] = edges
    other = jnp.concatenate([both[:, width : 2 * width], pltpu.roll(edges, width // 2, 1)], axis=1)
    log_rows = rows_of(16, 2 * width, list(enumerate(split3(other[head : head + 1]))))
    other_ref[...] = jnp.concatenate([other[0:head], log_rows], axis=0).astype(BF16)


def middle_part(place_ref, weight_hbm, mine_ref, got_ref, taps_ref, shared_ref, keep_ref, send_ref, pack_ref, copies_ref, weight_ref, sem, wide_ref, back_ref):
    fetch = pltpu.make_async_copy(weight_hbm, weight_ref, sem)
    fetch.start()
    width = 128
    head = 64
    ring = 2 * width
    half = KSIZE // 2
    reach = width + 2 * RIM
    start = place_ref[1]
    valid = place_ref[2]
    frames = place_ref[3]
    mine = mine_ref[64:65]
    side_at = 1 - place_ref[4]
    sent = got_ref[side_at].astype(F32)
    got = sent[64:65] + sent[65:66] + sent[66:67]
    top = jnp.maximum(mine, got)
    lse = top + jnp.log(jnp.exp(mine - top) + jnp.exp(got - top))
    attn = mine_ref[0:64] * jnp.exp(mine - lse) + sent[0:64] * jnp.exp(got - lse)
    attn = attn.astype(BF16).astype(F32)
    lane = lax.broadcasted_iota(jnp.int32, (1, ring), 1)
    frame = start + jnp.where(lane < ring - width // 2, lane, lane - ring)
    masked = jnp.where((frame >= 0) & (frame < frames) & (frame < valid), attn, 0.0)
    own_rows = masked[:, 0:width].T
    side_rows = masked[:, width:ring].T
    rows = jnp.concatenate([side_rows[96:128], own_rows, side_rows[0:32]], axis=0)
    wide_ref[...] = jnp.concatenate([rows[0 : reach + half], rows[half : reach + KSIZE]], axis=1)
    taps = jnp.concatenate([taps_ref[0:half], taps_ref[half:KSIZE]], axis=1)
    depth = jnp.zeros((reach, width), F32)
    for t in range(half):
        depth = depth + taps[t : t + 1] * wide_ref[t : t + reach]
    depth = depth[:, 0:head] + depth[:, head:width]
    gate = jax.nn.sigmoid(depth)
    swish = (depth * gate)[RIM : RIM + width].astype(BF16)
    grad = lay_grads(shared_ref)
    mix = dot00(swish, grad[RIM : RIM + width])
    mix = jnp.concatenate([mix[:, at : at + width] for at in range(0, mix.shape[1], width)], axis=0)
    fetch.wait()
    weight = weight_ref[...]
    partial = dot10(swish, weight)
    core = place_ref[5] == 0
    even = jnp.concatenate([partial[at : at + 8] for at in range(0, width, 16)], axis=0)
    odd = jnp.concatenate([partial[at + 8 : at + 16] for at in range(0, width, 16)], axis=0)
    keep_ref[...] = jnp.where(core, even, odd).astype(BF16)
    send_ref[...] = jnp.where(core, odd, even).astype(BF16)
    dgrad = dot11(grad, weight) * gate * (1.0 + depth * (1.0 - gate))
    row = start - RIM + lax.broadcasted_iota(jnp.int32, (reach, head), 0)
    dgrad = jnp.where((row >= 0) & (row < frames), dgrad, 0.0).astype(BF16).astype(F32)
    back_ref[...] = jnp.concatenate([dgrad[half:reach], dgrad[0 : reach - half]], axis=1)
    inner = dgrad[RIM : RIM + width]
    inner = jnp.concatenate([inner, inner], axis=1)
    total = jnp.zeros((width, width), F32)
    tap_rows = []
    for t in range(half):
        total = total + taps[t : t + 1] * back_ref[half - t : half - t + width]
        tap_rows.append((t, jnp.sum(wide_ref[RIM + t : RIM + t + width] * inner, axis=0, keepdims=True)))
    tap_grad = rows_of(half, width, tap_rows)
    total = total[:, 0:head] + total[:, head:width]
    row = start + lax.broadcasted_iota(jnp.int32, (width, head), 0)
    grad_out = jnp.where(row < valid, total, 0.0).T.astype(BF16)
    delta = jnp.sum(grad_out.astype(F32) * attn[:, :width], axis=0, keepdims=True)
    a, b, c = split3(-lse[:, :width])
    d, e, f = split3(-delta)
    stats = rows_of(16, width, [(0, a), (1, b), (2, c), (3, d), (4, e), (5, f), (6, 1.0)])
    pack_ref[...] = jnp.concatenate([grad_out, stats.astype(BF16)], axis=0)
    row = lax.broadcasted_iota(jnp.int32, (8, width), 0)
    share = copies_ref.shape[1] - 72
    for j in range(copies_ref.shape[0]):
        copies_ref[j, 0:64] = grad_out
        rest = jnp.where(row == 7, tap_grad[j : j + 1], stats[0:8])
        rest = jnp.concatenate([rest, mix[j * share : (j + 1) * share]], axis=0)
        copies_ref[j, 64:] = rest.astype(BF16)


ONES = [(0, 1.0), (1, 1.0), (2, 1.0)]
DELTAS = [(3, 1.0), (4, 1.0), (5, 1.0)]


def query_back(place_ref, all_ref, own_ref, pair_ref, pack_own_ref, pack_pair_ref, out_ref):
    blocks = all_ref.shape[0]
    base = place_ref[4] * blocks
    head = 64
    width = 128
    scale = head ** -0.5
    query = jnp.concatenate([own_ref[0:head], pair_ref[0:head]], axis=1)
    packs = jnp.concatenate([pack_own_ref[...], pack_pair_ref[...]], axis=1)
    query = (query.astype(F32) * scale).astype(BF16)
    query = jnp.concatenate([query, packs[head : head + 16]], axis=0)
    value_rows = rows_of(16, width, DELTAS).astype(BF16)
    total = jnp.zeros((head, 2 * width), F32)
    for first in range(0, blocks, 2):
        keys, scores = [], []
        for b in (first, first + 1):
            key_b = all_ref[b, head : 2 * head]
            key_rows = rows_of(16, width, ONES + [(6, bias_of(place_ref, b, base))]).astype(BF16)
            value_aug = jnp.concatenate([all_ref[b, 2 * head : 3 * head], value_rows], axis=0)
            weight = jnp.exp(dot00(jnp.concatenate([key_b, key_rows], axis=0), query))
            scores.append((weight * dot00(value_aug, packs)).astype(BF16))
            keys.append(key_b)
        total = total + dot10(jnp.concatenate(keys, axis=1), jnp.concatenate(scores, axis=0))
    out_ref[...] = total * scale


def backward(place_ref, all_ref, packs_ref, own_ref, pair_ref, d_query_ref, mine_ref, other_ref):
    blocks = all_ref.shape[0]
    base = place_ref[4] * blocks
    pair_base = blocks - base
    pair_bias = jnp.concatenate([bias_of(place_ref, place_ref[0], base), bias_of(place_ref, place_ref[0], pair_base)], axis=1)
    head = 64
    width = 128
    scale = head ** -0.5
    both = jnp.concatenate([own_ref[head:], pair_ref[head:]], axis=1)
    more = packs_ref.shape[1] - head
    key_rows = rows_of(more, 2 * width, ONES + [(6, pair_bias)]).astype(BF16)
    key = jnp.concatenate([both[0:head], key_rows], axis=0)
    value = jnp.concatenate([both[head:], rows_of(more, 2 * width, DELTAS).astype(BF16)], axis=0)
    d_key = jnp.zeros((head, 2 * width), F32)
    d_value = jnp.zeros((head, 2 * width), F32)
    for first in range(0, blocks, 2):
        queries, grads, scores, weights = [], [], [], []
        for b in (first, first + 1):
            query_b = (all_ref[b, 0:head].astype(F32) * scale).astype(BF16)
            query_aug = jnp.concatenate([query_b, packs_ref[b, head:]], axis=0)
            weight = jnp.exp(dot00(query_aug, key))
            scores.append((weight * dot00(packs_ref[b], value)).astype(BF16))
            weights.append(weight.astype(BF16))
            queries.append(query_b)
            grads.append(packs_ref[b, 0:head])
        d_key = d_key + dot10(jnp.concatenate(queries, axis=1), jnp.concatenate(scores, axis=0))
        d_value = d_value + dot10(jnp.concatenate(grads, axis=1), jnp.concatenate(weights, axis=0))
    for ref, at in ((mine_ref, 0), (other_ref, width)):
        kind = ref.dtype
        ref[0:head] = d_query_ref[:, at : at + width].astype(kind)
        ref[head : 2 * head] = d_key[:, at : at + width].astype(kind)
        ref[2 * head : 3 * head] = d_value[:, at : at + width].astype(kind)


def finish(place_ref, mine_ref, got_ref, query_ref, key_ref, value_ref):
    total = mine_ref[...] + got_ref[1 - place_ref[4]].astype(F32)
    query_ref[...] = total[0:64].astype(BF16)
    key_ref[...] = total[64:128].astype(BF16)
    value_ref[...] = total[128:192].astype(BF16)


def add_pair(mine_ref, got_ref, out_ref):
    out_ref[...] = (mine_ref[...].astype(F32) + got_ref[...].astype(F32)).astype(BF16)


def mix_sum(packs_ref, out_ref):
    share = packs_ref.shape[1] - 72
    total = jnp.zeros((share + 8, 128), F32)
    for j in range(packs_ref.shape[0]):
        total = total + packs_ref[j, 64:].astype(F32)
    out_ref[0:share] = total[8:]
    out_ref[share:] = rows_of(out_ref.shape[0] - share, 128, [(0, total[7:8])])


def mix_spread(both_ref, out_ref):
    total = (both_ref[0] + both_ref[1]).astype(BF16)
    for j in range(out_ref.shape[0]):
        out_ref[j] = total


def mix_place(norm, share, parts_ref, out_ref, taps_ref):
    pieces = [parts_ref[z].astype(F32) * norm for z in range(parts_ref.shape[0])]
    full = jnp.concatenate([piece[0:share] for piece in pieces], axis=0)
    for at in range(out_ref.shape[1] // 128):
        out_ref[:, at * 128 : (at + 1) * 128] = full[at * 64 : (at + 1) * 64]
    tap = rows_of(len(pieces), 128, [(z, piece[share : share + 1]) for z, piece in enumerate(pieces)])
    taps_ref[0:16] = tap[:, 0:64]
    taps_ref[16:32] = tap[:, 64:128]


def sum_blocks(parts_ref, out_ref):
    total = jnp.zeros(out_ref.shape, F32)
    for j in range(parts_ref.shape[0]):
        total = total + parts_ref[j].astype(F32)
    out_ref[...] = total.astype(BF16)


def body(query_rows, key_rows, value_rows, valid_frames, depth_kernel, mix_weight, out_grad):
    width, head = query_rows.shape
    depth = lax.axis_size("z")
    ctx = ("yh", "z")
    tp = ("chip", "core")
    devices = 2 * depth
    lanes = lax.axis_size(tp)
    model = mix_weight.shape[1]
    rows8 = out_grad.shape[0]
    norm = (width * devices) ** -0.5
    valid = valid_frames[0]
    half = lax.axis_index("yh")
    spot = lax.axis_index("z")
    place = jnp.stack([spot, (half * depth + spot) * width, valid, jnp.int32(width * devices), half, lax.axis_index("core")]).astype(jnp.int32)
    swap = [(0, 1), (1, 0)]
    rim_pairs = []
    sides = RIM // rows8
    for i in range(devices - 1):
        for k in range(sides):
            rim_pairs.append((i * lanes + lanes - sides + k, (i + 1) * lanes + k))
            rim_pairs.append(((i + 1) * lanes + k, i * lanes + lanes - sides + k))

    rim_rows = lax.ppermute(out_grad, ctx + tp, rim_pairs)
    own = jnp.concatenate([query_rows.T, key_rows.T, value_rows.T], axis=0)
    both = lax.all_gather(own, "yh", axis=0)
    rim_rows, both = lax.optimization_barrier((rim_rows, both))
    front, pair = call(
        first_pack,
        (jax.ShapeDtypeStruct((3 * head + 32, width), BF16), jax.ShapeDtypeStruct((3 * head, width), BF16)),
        2 ** 20,
        scalars=1,
    )(place, both)
    grads = call(copy_rows, jax.ShapeDtypeStruct((lanes, 2 * rows8, model), BF16), 2 ** 20)(out_grad, rim_rows)
    shared = lax.all_to_all(grads, tp, 0, 0, tiled=True)
    everyone = lax.all_gather(front, "z", axis=0)
    shared, everyone = lax.optimization_barrier((shared, everyone))

    part = jax.ShapeDtypeStruct((head + 8, 2 * width), F32)
    block = jax.ShapeDtypeStruct((head, width), BF16)
    mine, other = call(
        attend, (part, jax.ShapeDtypeStruct((head + 16, 2 * width), BF16)), 2 ** 28, [pltpu.VMEM((depth, width, 3 * width), F32)], scalars=1
    )(place, everyone, own, pair)
    shared, other = lax.optimization_barrier((shared, other))
    got = lax.all_gather(other, "yh", axis=0)
    share = head * model // width // depth
    half_rows = jax.ShapeDtypeStruct((width // 2, model), BF16)
    keep, send, pack, copies = call(
        middle_part,
        (
            half_rows,
            half_rows,
            jax.ShapeDtypeStruct((80, width), BF16),
            jax.ShapeDtypeStruct((depth, 72 + share, width), BF16),
        ),
        2 ** 27,
        [
            pltpu.VMEM(mix_weight.shape, BF16),
            pltpu.SemaphoreType.DMA,
            pltpu.VMEM((width + 2 * RIM + KSIZE // 2, width), F32),
            pltpu.VMEM((width + 2 * RIM - KSIZE // 2, width), F32),
        ],
        scalars=1,
        remote=1,
    )(place, mix_weight, mine, got, depth_kernel, shared)
    packs = lax.all_to_all(copies, "z", 0, 0, tiled=True)
    keep_got = lax.ppermute(send, "core", swap)
    partial = call(add_pair, half_rows, 2 ** 20)(keep, keep_got)
    pack_pair = lax.ppermute(pack, "yh", swap)
    d_query = call(query_back, jax.ShapeDtypeStruct((head, 2 * width), F32), 2 ** 28, scalars=1)(
        place, everyone, own, pair, pack, pack_pair
    )
    packs, d_query, partial = lax.optimization_barrier((packs, d_query, partial))

    mix_mine = call(mix_sum, jax.ShapeDtypeStruct((share + 8, width), F32), 2 ** 22)(packs)
    mix_both = lax.all_gather(mix_mine, "yh", axis=0)
    spread = call(mix_spread, jax.ShapeDtypeStruct((depth, share + 8, width), BF16), 2 ** 20)(mix_both)
    block_parts = lax.all_to_all(partial.reshape(lanes // 2, rows8, model), "chip", 0, 0, tiled=True)
    spread, block_parts = lax.optimization_barrier((spread, block_parts))
    pieces = lax.all_to_all(spread, "z", 0, 0, tiled=True)
    result = jax.ShapeDtypeStruct((3 * head, width), F32)
    sent = jax.ShapeDtypeStruct(result.shape, BF16)
    mine, other = call(backward, (result, sent), 2 ** 29, scalars=1)(
        place, everyone, packs, own, pair, d_query
    )
    got = lax.all_gather(other, "yh", axis=0)
    d_query, d_key, d_value = call(finish, (block, block, block), 2 ** 20, scalars=1)(place, mine, got)

    block_out = call(sum_blocks, jax.ShapeDtypeStruct((rows8, model), BF16), 2 ** 20)(block_parts)
    mix_grad, tap_total = call(
        functools.partial(mix_place, norm, share),
        (jax.ShapeDtypeStruct((head, model), F32), jax.ShapeDtypeStruct((KSIZE, head), F32)),
        2 ** 20,
    )(pieces)
    return block_out, d_query.T, d_key.T, d_value.T, mix_grad, tap_total


def solution(mesh):
    count = mesh.shape["ctx"]
    fine = Mesh(mesh.devices.reshape(2, count // 2, mesh.shape["tp"] // 2, 2), ("yh", "z", "chip", "core"))
    ctx = ("yh", "z")
    tp = ("chip", "core")
    every = ctx + tp
    return jax.shard_map(
        body,
        mesh=fine,
        in_specs=(
            P(ctx, tp),
            P(ctx, tp),
            P(ctx, tp),
            P(),
            P(None, tp),
            P(tp, None),
            P(every, None),
        ),
        out_specs=(
            P(every, None),
            P(ctx, tp),
            P(ctx, tp),
            P(ctx, tp),
            P(tp, None),
            P(None, tp),
        ),
        check_vma=False,
    )
```
